128 devices in a mesh: gx: 16 (over x, z), gy: 4 (over y), img: 2 (over core).
Axes of the slice: x: 4, y: 4, z: 4, core: 2. Of those that a mesh axis runs over, the one named last changes fastest.
Arguments:
- features: bfloat16 [1024, 49, 128], P(('img', 'gx', 'gy')), parts along dimension 0, may hold values from -6 to 6
- cotangent: bfloat16 [1024, 49, 128], P(('img', 'gx', 'gy')), parts along dimension 0, may hold values from -6 to 6
- w_zero: bfloat16 [896, 896], replicated, may hold values from -0.1875 to 0.1875
- w_one: bfloat16 [2, 768, 768], replicated, may hold values from -0.15625 to 0.15625
- w_two: bfloat16 [2, 640, 640], replicated, may hold values from -0.15625 to 0.15625
- radial_weight: float32 [512, 128], replicated, may hold values from -1 to 1
- inner_edges: int32 [128, 5, 96], P(('img', 'gx', 'gy')), parts along dimension 0, may hold values from 0 to 4095, as said below
- halo_edges: int32 [128, 8, 5, 8], P(('img', 'gx', 'gy')), parts along dimension 0, may hold values from 0 to 4095, as said below
- halo_counts: int32 [128, 8], P(('img', 'gx', 'gy')), parts along dimension 0, may hold values from 0 to 8, as said below
Outputs:
- aggregate: bfloat16 [1024, 49, 128], P(('img', 'gx', 'gy')), parts along dimension 0
- feature_grad: bfloat16 [1024, 49, 128], P(('img', 'gx', 'gy')), parts along dimension 0
The draws below stay inside these ranges and needn't reach their ends.
There are 2 independent parts, one for each index of `img`. The reference program is written for one: setup_inputs(seed, part) draws one part's arguments, and reference() takes and returns one part's arrays. A program takes and returns all parts, laid end to end along the dimension named above; an argument that names none is the same for every part. Nothing has to cross between parts.
Inputs may be any that keep to these rules, and one draw needn't show every extreme that they name: `inner_edges`: rows 0 and 1 are atoms of the domain, below 8; rows 2 and 3 are angle codes; row 4 is a length code below 1024. `halo_edges`: rows 0 and 1 are atoms below 8; rows 2 and 3 are angle codes; row 4 is a length code below 1024. Slots at or past the bucket's count hold arbitrary values of these ranges. `halo_counts`: zero exactly for buckets whose offset leads out of the grid of domains; 8 is reached in every draw.
All inputs are finite; a program needn't handle non-finite values.
Results may differ from the reference program's by a relative error of at most 0.0066.
Values may be sent and summed in bfloat16 or wider, within the bound.
A program may use at most 128 MiB of HBM per device.

```python
import math
import jax
import jax.numpy as jnp
import numpy as np
from jax import lax

C = 128
RADIAL = 512
A_DEV = 8
INNER = 96
CAP = 8
DOMAINS_X = 16
DOMAINS_Y = 4
DOMAINS = 64
ATOMS = 512


def edge_rows(key, leading):
    subkeys = jax.random.split(key, 5)
    limits = (A_DEV, A_DEV, 4096, 4096, 1024)
    columns = [jax.random.randint(subkeys[column], leading, 0, limits[column]) for column in range(5)]
    return jnp.stack(columns, axis=-2).astype(jnp.int32)


def draw_inner_edges(key, part):
    key = jax.random.fold_in(key, 11)
    drawn = edge_rows(key, (DOMAINS, INNER))
    return drawn.at[0, 2, 0].set(4095).astype(jnp.int32)


def draw_halo_edges(key, part):
    key = jax.random.fold_in(key, 13)
    drawn = edge_rows(key, (DOMAINS, 8, CAP))
    return drawn.at[0, 0, 2, 0].set(4095).astype(jnp.int32)


def draw_halo_counts(key, part):
    key = jax.random.fold_in(key, 17)
    domain = jnp.arange(DOMAINS, dtype=jnp.int32)
    place_x = domain // DOMAINS_Y
    place_y = domain % DOMAINS_Y
    shift_x = jnp.array([-1, -1, -1, 0, 0, 1, 1, 1], jnp.int32)
    shift_y = jnp.array([-1, 0, 1, -1, 1, -1, 0, 1], jnp.int32)
    target_x = place_x[:, None] + shift_x[None, :]
    target_y = place_y[:, None] + shift_y[None, :]
    inside = (target_x >= 0) & (target_x < DOMAINS_X) & (target_y >= 0) & (target_y < DOMAINS_Y)
    nearby = jnp.abs(place_x - DOMAINS_X // 2) <= 1
    lowest = jnp.where(nearby, 3 * CAP // 4, 1)
    drawn = jax.random.randint(key, (DOMAINS, 8), 0, 1 << 20)
    spread_top = CAP + 1 - lowest
    counts = lowest[:, None] + drawn % spread_top[:, None]
    counts = counts.at[:, 6].set(CAP)
    return jnp.where(inside, counts, 0).astype(jnp.int32)


def level_of(stream_key, shape, shards, smallest, top_value):
    loudness, own = 1.0, jax.random.fold_in(stream_key, 6)
    for dim, parts in shards:
        steps = jnp.exp(jax.random.uniform(jax.random.fold_in(own, dim), (parts,), jnp.float32, smallest / len(shards), top_value / len(shards)))
        loudness = loudness * jnp.repeat(steps, shape[dim] // parts).reshape([-1 if axis == dim else 1 for axis in range(len(shape))])
    return loudness


def noise(key, extent, scale, most, cuts=(), held_as=jnp.bfloat16):
    values = jax.random.normal(key, extent, jnp.float32) * scale
    if len(cuts) > 0:
        values = level_of(key, extent, cuts, -0.22, 0.18) * values
    return jnp.clip(values, min=-most, max=most).astype(held_as)


def setup_inputs(seed: int = 0, part: int = 0) -> dict:
    key_list = jax.random.split(jax.random.key(seed), 10)
    part_splits = jax.random.split(jax.random.fold_in(key_list[9], part), 10)
    features = noise(part_splits[0], (ATOMS, 49, C), 1.0, 6.0, ((0, 64),))
    cotangent = noise(part_splits[1], (ATOMS, 49, C), 1.0, 6.0, ((0, 64),))
    w_zero = noise(key_list[2], (7 * C, 7 * C), (7 * C) ** -0.5, 0.1875)
    w_one = noise(key_list[3], (2, 6 * C, 6 * C), (12 * C) ** -0.5, 0.15625)
    w_two = noise(key_list[4], (2, 5 * C, 5 * C), (10 * C) ** -0.5, 0.15625)
    radial_weight = noise(key_list[5], (RADIAL, C), (RADIAL // 12) ** -0.5, 1.0, (), jnp.float32)
    inner_edges = draw_inner_edges(jax.random.fold_in(jax.random.fold_in(key_list[9], part), 71), part)
    halo_edges = draw_halo_edges(jax.random.fold_in(jax.random.fold_in(key_list[9], part), 71), part)
    halo_counts = draw_halo_counts(jax.random.fold_in(jax.random.fold_in(key_list[9], part), 71), part)
    return dict(features=features, cotangent=cotangent, w_zero=w_zero, w_one=w_one, w_two=w_two, radial_weight=radial_weight, inner_edges=inner_edges, halo_edges=halo_edges, halo_counts=halo_counts)


neighbour_steps = ((-1, -1), (-1, 0), (-1, 1), (0, -1), (0, 1), (1, -1), (1, 0), (1, 1))
edge_scale = 0.25
angle_unit = 2.0 * math.pi / 4096.0
group_bounds = ((0, 7), (7, 13), (13, 19), (19, 24), (24, 29))

def harmonics(east, north, height):
    columns = np.zeros((height.shape[0], 49))
    real_part = np.ones(height.shape)
    imag_part = np.zeros(height.shape)
    for moment in range(7):
        if moment > 0:
            real_part, imag_part = (real_part * east - imag_part * north, real_part * north + imag_part * east)
        older = np.zeros(height.shape)
        newer = (-1.0) ** moment * float(np.prod(np.arange(1, 2 * moment, 2))) * np.ones(height.shape)
        for degree in range(moment, 7):
            if degree > moment:
                older, newer = (newer, ((2 * degree - 1) * height * newer - (degree + moment - 1) * older) / (degree - moment))
            factor = math.sqrt((2 * degree + 1) / (4.0 * math.pi) * math.factorial(degree - moment) / math.factorial(degree + moment))
            centre = degree * degree + degree
            if moment == 0:
                columns[:, centre] = factor * newer
            else:
                columns[:, centre + moment] = math.sqrt(2.0) * factor * newer * real_part
                columns[:, centre - moment] = math.sqrt(2.0) * factor * newer * imag_part
    return columns

def legendre_pair(order, points):
    older = np.ones(points.shape)
    newer = points * 1.0
    for degree in range(2, order + 1):
        older, newer = (newer, ((2 * degree - 1) * points * newer - (degree - 1) * older) / degree)
    slope = order * (points * newer - older) / (points * points - 1.0)
    return (newer, slope)

def gauss_nodes(order):
    nodes = np.cos(math.pi * (np.arange(order) + 0.75) / (order + 0.5))
    for sweep in range(20):
        value, slope = legendre_pair(order, nodes)
        nodes = nodes - value / slope
    value, slope = legendre_pair(order, nodes)
    return (nodes, 2.0 / ((1.0 - nodes * nodes) * slope * slope))

def tilt_table():
    nodes, node_weights = gauss_nodes(7)
    turns = 16
    azimuth = 2.0 * math.pi * np.arange(turns) / turns
    height = np.repeat(nodes, turns)
    weights = np.repeat(node_weights, turns) * (2.0 * math.pi / turns)
    spread = np.tile(azimuth, nodes.shape[0])
    radius = np.sqrt(np.maximum(1.0 - height * height, 0.0))
    east = radius * np.cos(spread)
    north = radius * np.sin(spread)
    before = harmonics(east, north, height)
    after = harmonics(east, -height, north)
    full = after.T @ (before * weights[:, None])
    table = np.zeros((49, 49))
    for degree in range(7):
        first_row = degree * degree
        last_row = first_row + 2 * degree + 1
        table[first_row:last_row, first_row:last_row] = full[first_row:last_row, first_row:last_row]
    return table

def coefficient_tables():
    moments = np.zeros(49)
    sine_signs = np.zeros(49)
    partner = np.zeros(49, dtype=np.int32)
    for degree in range(7):
        for moment in range(-degree, degree + 1):
            column = degree * degree + degree + moment
            moments[column] = abs(moment)
            sine_signs[column] = -1.0 if moment > 0 else 1.0 if moment < 0 else 0.0
            partner[column] = degree * degree + degree - moment
    framed = [degree * degree + degree + moment for moment in (0, 1, -1, 2, -2) for degree in range(abs(moment), 7)]
    quarter = tilt_table()
    return {'moments': jnp.asarray(moments, jnp.float32), 'sine_signs': jnp.asarray(sine_signs, jnp.float32), 'partner': partner, 'tilt': jnp.asarray(quarter, jnp.float32), 'tilt_back': jnp.asarray(quarter.T, jnp.float32), 'tilt_back_frame': jnp.asarray(quarter.T[framed], jnp.float32), 'tilt_frame': jnp.asarray(quarter[:, framed], jnp.float32)}

def spin_about(vectors, angle_codes, tables, direction):
    phases = angle_codes.astype(jnp.float32)[:, None] * (angle_unit * tables['moments'])[None, :]
    cosine = jnp.cos(phases)[:, :, None]
    sine_part = (direction * tables['sine_signs'][None, :] * jnp.sin(phases))[:, :, None]
    return cosine * vectors + sine_part * vectors[:, tables['partner'], :]

def mixing(table, vectors):
    return jnp.einsum('ij,ejc->eic', table, vectors, precision=lax.Precision.HIGHEST)

def to_frame(vectors, alpha_codes, beta_codes, tables):
    turned = spin_about(vectors.astype(jnp.float32), alpha_codes, tables, 1.0)
    turned = spin_about(mixing(tables['tilt'], turned), beta_codes, tables, 1.0)
    return mixing(tables['tilt_back_frame'], turned)

def from_frame(framed, alpha_codes, beta_codes, tables):
    turned = spin_about(mixing(tables['tilt_frame'], framed), beta_codes, tables, -1.0)
    return spin_about(mixing(tables['tilt_back'], turned), alpha_codes, tables, -1.0)

def radial_factor(length_codes, radial_weight):
    length = 0.5 + 5.5 * length_codes.astype(jnp.float32) / 1024.0
    functions = radial_weight.shape[0]
    centres = 0.5 + 5.5 * jnp.arange(functions, dtype=jnp.float32) / functions
    basis_rows = jnp.exp(-0.5 * ((length[:, None] - centres[None, :]) / 0.25) ** 2)
    return jnp.dot(basis_rows, radial_weight, precision=lax.Precision.HIGHEST)

def frame_edges(vectors, alpha_codes, beta_codes, radial, tables):
    return (to_frame(vectors, alpha_codes, beta_codes, tables) * radial[:, None, :]).astype(jnp.bfloat16)

def group_rows(framed, bounds):
    grouped = framed[:, bounds[0]:bounds[1], :]
    return grouped.reshape(grouped.shape[0], -1)

def product(left_side, right_side):
    return jnp.dot(left_side, right_side, preferred_element_type=jnp.float32)

def product_back(left_side, right_side):
    return lax.dot_general(left_side, right_side, (((1,), (1,)), ((), ())), preferred_element_type=jnp.float32)

def reassemble(outputs, channels):
    return jnp.concatenate([grouped.reshape(grouped.shape[0], -1, channels) for grouped in outputs], axis=1)

def convolve(framed, w_zero, w_one, w_two):
    pieces = [group_rows(framed, bounds) for bounds in group_bounds]
    outputs = [product(pieces[0], w_zero), product(pieces[1], w_one[0]) - product(pieces[2], w_one[1]), product(pieces[1], w_one[1]) + product(pieces[2], w_one[0]), product(pieces[3], w_two[0]) - product(pieces[4], w_two[1]), product(pieces[3], w_two[1]) + product(pieces[4], w_two[0])]
    return reassemble(outputs, framed.shape[2])

def convolve_back(grads, w_zero, w_one, w_two):
    pieces = [group_rows(grads, bounds) for bounds in group_bounds]
    outputs = [product_back(pieces[0], w_zero), product_back(pieces[1], w_one[0]) + product_back(pieces[2], w_one[1]), product_back(pieces[2], w_one[0]) - product_back(pieces[1], w_one[1]), product_back(pieces[3], w_two[0]) + product_back(pieces[4], w_two[1]), product_back(pieces[4], w_two[0]) - product_back(pieces[3], w_two[1])]
    return reassemble(outputs, grads.shape[2])

def destination_work(framed, alpha_codes, beta_codes, live_mask, targets, cotangent, w_zero, w_one, w_two, tables):
    values_pre = convolve(framed, w_zero, w_one, w_two)
    gate_open = jax.nn.sigmoid(values_pre[:, 0, :])
    message = from_frame(values_pre * gate_open[:, None, :], alpha_codes, beta_codes, tables) * live_mask[:, None, None]
    incoming = jnp.take(cotangent, targets, axis=0).astype(jnp.float32) * (edge_scale * live_mask)[:, None, None]
    upstream = to_frame(incoming, alpha_codes, beta_codes, tables)
    through = lax.optimization_barrier(jnp.sum(upstream * values_pre, axis=1)) * gate_open * (1.0 - gate_open)
    gate_grad = (upstream * gate_open[:, None, :]).at[:, 0, :].add(through).astype(jnp.bfloat16)
    framed_grad = convolve_back(gate_grad, w_zero, w_one, w_two).astype(jnp.bfloat16)
    return (message, framed_grad)

def reference(features, cotangent, w_zero, w_one, w_two, radial_weight, inner_edges, halo_edges, halo_counts):
    tables = coefficient_tables()
    atom_count = features.shape[0]
    steps_x = jnp.array([offset_pair[0] for offset_pair in neighbour_steps], jnp.int32)
    steps_y = jnp.array([offset_pair[1] for offset_pair in neighbour_steps], jnp.int32)
    slot_index = jnp.arange(CAP, dtype=jnp.int32)

    def per_domain(summed, domain):
        place_x = domain // DOMAINS_Y
        place_y = domain % DOMAINS_Y
        first_atom = domain * A_DEV
        own_rows = lax.dynamic_slice_in_dim(features, first_atom, A_DEV, 0)
        inner_list = inner_edges[domain]
        halo_list = halo_edges[domain]
        counts = halo_counts[domain]
        target_x = place_x + steps_x
        target_y = place_y + steps_y
        inside = (target_x >= 0) & (target_x < DOMAINS_X) & (target_y >= 0) & (target_y < DOMAINS_Y)
        live_halo = ((slot_index[None, :] < counts[:, None]) & inside[:, None]).reshape(-1)
        live_mask = jnp.concatenate([jnp.ones((INNER,), jnp.float32), live_halo.astype(jnp.float32)])
        sources = jnp.concatenate([inner_list[0], halo_list[:, 0].reshape(-1)]).astype(jnp.int32)
        halo_targets = (target_x * DOMAINS_Y + target_y)[:, None] * A_DEV + halo_list[:, 1]
        targets = jnp.concatenate([first_atom + inner_list[1], halo_targets.reshape(-1)])
        targets = jnp.where(live_mask > 0, targets, 0).astype(jnp.int32)
        alpha_codes = jnp.concatenate([inner_list[2], halo_list[:, 2].reshape(-1)])
        beta_codes = jnp.concatenate([inner_list[3], halo_list[:, 3].reshape(-1)])
        length_codes = jnp.concatenate([inner_list[4], halo_list[:, 4].reshape(-1)])
        radial = radial_factor(length_codes, radial_weight)
        framed = frame_edges(jnp.take(own_rows, sources, axis=0), alpha_codes, beta_codes, radial, tables)
        message, framed_grad = destination_work(framed, alpha_codes, beta_codes, live_mask, targets, cotangent, w_zero, w_one, w_two, tables)
        summed = summed + jax.ops.segment_sum(message, targets, num_segments=atom_count)
        edge_grad = from_frame(framed_grad.astype(jnp.float32) * radial[:, None, :], alpha_codes, beta_codes, tables)
        edge_grad = edge_grad.astype(jnp.bfloat16).astype(jnp.float32)
        grad_rows = jax.ops.segment_sum(edge_grad, sources, num_segments=A_DEV)
        return (summed, grad_rows.astype(jnp.bfloat16))
    summed, grad_rows = lax.scan(per_domain, jnp.zeros(features.shape, jnp.float32), jnp.arange(DOMAINS, dtype=jnp.int32))
    aggregate = (edge_scale * summed).astype(jnp.bfloat16)
    return (aggregate, grad_rows.reshape(features.shape))
```

```python
import functools
import math

import jax
import jax.numpy as jnp
import numpy as np
from jax import lax
from jax.experimental import pallas as pl
from jax.experimental.pallas import tpu as pltpu
from jax.sharding import PartitionSpec as P

MESH = pl.DeviceIdType.MESH
F32 = jnp.float32
BF16 = jnp.bfloat16

neighbour_steps = ((-1, -1), (-1, 0), (-1, 1), (0, -1), (0, 1), (1, -1), (1, 0), (1, 1))
BUCKETS = 8
CAP = 8
INNER = 96
HALO = BUCKETS * CAP
EDGES = INNER + HALO
ATOMS = 8
C = 128
RADIAL = 512

framed_rows = [(degree, order) for order in (0, 1, -1, 2, -2) for degree in range(abs(order), 7)]
low_rows = [f for f, (degree, order) in enumerate(framed_rows) if degree <= 4]
high_rows = [f for f, (degree, order) in enumerate(framed_rows) if degree > 4]
packed_rows = low_rows + high_rows
LOW = len(low_rows)
HIGH = len(high_rows)
FRAMED = LOW + HIGH
travel_rows = low_rows + [None] + high_rows
PAIRS = len(travel_rows) // 2
LOW_PAIRS = (LOW + 1) // 2
LOW_TRAVEL = LOW_PAIRS * 16
TRAVEL = PAIRS * 16
group_bounds = ((0, 7), (7, 13), (13, 19), (19, 24), (24, 29))


def harmonics(east, north, height):
    columns = np.zeros((height.shape[0], 49))
    real_part = np.ones(height.shape)
    imag_part = np.zeros(height.shape)
    for moment in range(7):
        if moment > 0:
            real_part, imag_part = (
                real_part * east - imag_part * north,
                real_part * north + imag_part * east,
            )
        older = np.zeros(height.shape)
        newer = (
            (-1.0) ** moment * float(np.prod(np.arange(1, 2 * moment, 2))) * np.ones(height.shape)
        )
        for degree in range(moment, 7):
            if degree > moment:
                older, newer = (
                    newer,
                    ((2 * degree - 1) * height * newer - (degree + moment - 1) * older)
                    / (degree - moment),
                )
            factor = math.sqrt(
                (2 * degree + 1)
                / (4.0 * math.pi)
                * math.factorial(degree - moment)
                / math.factorial(degree + moment)
            )
            centre = degree * degree + degree
            if moment == 0:
                columns[:, centre] = factor * newer
            else:
                columns[:, centre + moment] = math.sqrt(2.0) * factor * newer * real_part
                columns[:, centre - moment] = math.sqrt(2.0) * factor * newer * imag_part
    return columns


def legendre_pair(order, points):
    older = np.ones(points.shape)
    newer = points * 1.0
    for degree in range(2, order + 1):
        older, newer = (newer, ((2 * degree - 1) * points * newer - (degree - 1) * older) / degree)
    slope = order * (points * newer - older) / (points * points - 1.0)
    return (newer, slope)


def gauss_nodes(order):
    nodes = np.cos(math.pi * (np.arange(order) + 0.75) / (order + 0.5))
    for sweep in range(20):
        value, slope = legendre_pair(order, nodes)
        nodes = nodes - value / slope
    value, slope = legendre_pair(order, nodes)
    return (nodes, 2.0 / ((1.0 - nodes * nodes) * slope * slope))


def tilt_table():
    nodes, node_weights = gauss_nodes(7)
    turns = 16
    azimuth = 2.0 * math.pi * np.arange(turns) / turns
    height = np.repeat(nodes, turns)
    weights = np.repeat(node_weights, turns) * (2.0 * math.pi / turns)
    spread = np.tile(azimuth, nodes.shape[0])
    radius = np.sqrt(np.maximum(1.0 - height * height, 0.0))
    east = radius * np.cos(spread)
    north = radius * np.sin(spread)
    before = harmonics(east, north, height)
    after = harmonics(east, -height, north)
    full = after.T @ (before * weights[:, None])
    table = np.zeros((49, 49))
    for degree in range(7):
        first_row = degree * degree
        last_row = first_row + 2 * degree + 1
        table[first_row:last_row, first_row:last_row] = full[first_row:last_row, first_row:last_row]
    return table


def split_bf16(table):
    high = table.astype(jnp.bfloat16)
    low = (table - high.astype(np.float64)).astype(jnp.bfloat16)
    return high, low


@functools.lru_cache(maxsize=None)
def rotation_tables():
    tilt = tilt_table()
    degrees = np.array([l for l in range(7) for m in range(-l, l + 1)])
    orders = np.array([m for l in range(7) for m in range(-l, l + 1)])
    partner = degrees * degrees + degrees - orders
    signs = -np.sign(orders).astype(np.float64)
    matrix = np.zeros((16, 49, 49))
    for i in range(49):
        moment = abs(orders[i])
        matrix[moment] += np.outer(tilt[i], tilt[i])
        if moment > 0:
            matrix[6 + moment] += signs[i] * np.outer(tilt[i], tilt[partner[i]])
    swapped = matrix[:, :, partner] * (-signs)[None, None, :]
    first = np.zeros((16, FRAMED * 256))
    for place, f in enumerate(packed_rows):
        degree, order = framed_rows[f]
        row = degree * degree + degree + order
        start = 0 if degree <= 4 else 24
        for j in range(degree * degree, (degree + 1) * (degree + 1)):
            for atom in range(4):
                lane = place * 256 + atom * 32 + j - start
                first[:, lane] = matrix[:, row, j]
                first[:, lane + 128] = swapped[:, row, j]
    high, low = split_bf16(first)
    first = np.concatenate([high, low, high], axis=0)
    second = np.zeros((128, 512))
    for column, (lowest, highest, start) in enumerate(((0, 25, 0), (25, 49, 24))):
        for j in range(lowest, highest):
            moment = abs(orders[j])
            for atom in range(4):
                lane = column * 256 + atom * 32 + j - start
                for part in (64, 96):
                    second[part + moment, lane] = 1.0
                    if moment > 0:
                        second[part + 6 + moment, lane + 128] = 1.0
    return first, second.astype(jnp.bfloat16)


def place_tables():
    gather = np.zeros((ATOMS * 49, 512))
    for j in range(49):
        for atom in range(ATOMS):
            column = atom * 32 + j if j < 25 else 256 + atom * 32 + j - 24
            gather[j * ATOMS + atom, column] = 1.0
    return gather.astype(jnp.bfloat16), gather.T.astype(jnp.bfloat16)


def cosine_terms():
    points = 0.125 + 0.125 * np.cos(math.pi * (np.arange(200) + 0.5) / 200)
    fit = np.polynomial.chebyshev.Chebyshev.fit(
        points, np.cos(2.0 * math.pi * np.sqrt(points)), 8, domain=[0.0, 0.25]
    )
    return [float(term) for term in fit.convert(kind=np.polynomial.Polynomial).coef]


def column_of(columns, which):
    return columns[:, which : which + 1]


def dot(left, right):
    return jnp.dot(left, right, preferred_element_type=F32)


def dot_rows(left, right):
    return lax.dot_general(left, right, (((0,), (0,)), ((), ())), preferred_element_type=F32)


def dot_columns(left, right):
    return lax.dot_general(left, right, (((1,), (1,)), ((), ())), preferred_element_type=F32)


def angle_terms(alpha, beta):
    lane = lax.broadcasted_iota(jnp.int32, (1, 128), 1)
    term = lane & 15
    moment = jnp.where(term < 7, term, term - 6).astype(F32)
    shift = jnp.where(term < 7, 0.0, -0.25).astype(F32)
    code = jnp.where(lane < 64, beta, alpha)
    turns = code * (moment * (1.0 / 4096.0)) + shift
    turns = turns - jnp.floor(turns + 0.5)
    square = turns * turns
    terms = cosine_terms()
    value = terms[-1]
    for coefficient in terms[-2::-1]:
        value = value * square + coefficient
    high = value.astype(BF16).astype(F32)
    return jnp.where((lane & 63) < 32, high, value - high).astype(BF16)


def atom_masks(atoms):
    lane = lax.broadcasted_iota(jnp.int32, (1, 128), 1) >> 5
    lane = lane.astype(F32)
    return [jnp.where(atoms == lane + 4.0 * half, 1.0, 0.0).astype(BF16) for half in range(2)]


def coefficient_blocks(rows, spread):
    blocks = dot(spread, rows).astype(BF16)
    return blocks[0:256], blocks[256:512]


def atom_rows(gather, low_columns, high_columns):
    columns = jnp.concatenate([low_columns.astype(BF16), high_columns.astype(BF16)], axis=1)
    return dot_columns(gather, columns).astype(BF16)


def kernel(
    domains_x,
    domains_y,
    features_hbm,
    cotangent_hbm,
    w_zero_hbm,
    w_one_hbm,
    w_two_hbm,
    radial_hbm,
    first_hbm,
    second_hbm,
    gather_hbm,
    spread_hbm,
    inner_hbm,
    halo_hbm,
    counts_hbm,
    aggregate_ref,
    gradient_ref,
    features,
    cotangent,
    w_zero,
    w_one,
    w_two,
    radial_weight,
    first,
    second,
    gather,
    spread,
    inner_ref,
    halo_ref,
    counts_ref,
    codes_table,
    codes_out,
    codes_in,
    source_low,
    source_high,
    inner_low,
    inner_high,
    incoming_low,
    incoming_high,
    framed_zero,
    framed_one,
    framed_two,
    hidden,
    hidden_low,
    hidden_high,
    hidden_out,
    hidden_in,
    upstream,
    upstream_out,
    upstream_in,
    back_low,
    back_high,
    small_sems,
    load_sems,
    codes_send,
    codes_recv,
    upstream_send,
    upstream_recv,
    hidden_send,
    hidden_recv,
):
    place_x = lax.axis_index("gx")
    place_y = lax.axis_index("gy")
    image = lax.axis_index("img")

    small_loads = [
        pltpu.make_async_copy(source, target, small_sems.at[number])
        for number, (source, target) in enumerate(
            ((inner_hbm, inner_ref), (halo_hbm, halo_ref), (counts_hbm, counts_ref))
        )
    ]
    for load in small_loads:
        load.start()
    loads = [
        pltpu.make_async_copy(source, target, load_sems.at[number])
        for number, (source, target) in enumerate(
            (
                (first_hbm, first),
                (second_hbm, second),
                (features_hbm, features),
                (cotangent_hbm, cotangent),
                (radial_hbm, radial_weight),
                (spread_hbm, spread),
                (w_zero_hbm, w_zero),
                (w_one_hbm, w_one),
                (w_two_hbm, w_two),
                (gather_hbm, gather),
            )
        )
    ]
    for load in loads:
        load.start()

    def inside(step_x, step_y):
        x = place_x + step_x
        y = place_y + step_y
        return (x >= 0) & (x < domains_x) & (y >= 0) & (y < domains_y)

    def device_at(step_x, step_y):
        return (place_x + step_x, place_y + step_y, image)

    barrier = pltpu.get_barrier_semaphore()
    for step_x, step_y in neighbour_steps:

        @pl.when(inside(step_x, step_y))
        def _(step_x=step_x, step_y=step_y):
            pl.semaphore_signal(
                barrier, inc=1, device_id=device_at(step_x, step_y), device_id_type=MESH
            )

    for bucket, (step_x, step_y) in enumerate(neighbour_steps):

        @pl.when(jnp.logical_not(inside(-step_x, -step_y)))
        def _(bucket=bucket):
            codes_in[bucket] = jnp.full((CAP, 128), -1.0, F32)
            hidden_in[bucket] = jnp.zeros((TRAVEL, C), BF16)

        @pl.when(jnp.logical_not(inside(step_x, step_y)))
        def _(bucket=bucket):
            upstream_in[bucket] = jnp.zeros((TRAVEL, C), BF16)

    codes_table[...] = jnp.zeros((128, 128), F32)
    for load in small_loads:
        load.wait()
    counts = counts_ref[...].astype(F32)
    for which in range(5):
        codes_table[which * BUCKETS : (which + 1) * BUCKETS, 0:CAP] = halo_ref[which].astype(F32)
        codes_table[40 + which : 41 + which, 0:INNER] = inner_ref[which].astype(F32)
    turned_codes = codes_table[...].T
    inner_codes = turned_codes[0:INNER, 40:45]
    lane = lax.broadcasted_iota(jnp.int32, (CAP, 128), 1)
    slot = lax.broadcasted_iota(jnp.int32, (CAP, 1), 0).astype(F32)
    halo_codes = [
        [column_of(turned_codes[0:CAP], which * BUCKETS + bucket) for bucket in range(BUCKETS)]
        for which in range(5)
    ]
    for bucket in range(BUCKETS):
        target = jnp.where(slot < column_of(counts, bucket), halo_codes[1][bucket], -1.0)
        codes_out[bucket] = jnp.where(
            lane == 0, target, jnp.where(lane == 1, halo_codes[2][bucket], halo_codes[3][bucket])
        )
    own_codes = [
        jnp.concatenate([column_of(inner_codes, which)] + halo_codes[which], axis=0)
        for which in range(5)
    ]

    def exchange(source, target, send, recv, bucket, step_x, step_y):
        return pltpu.make_async_remote_copy(
            src_ref=source.at[bucket],
            dst_ref=target.at[bucket],
            send_sem=send.at[bucket],
            recv_sem=recv.at[bucket],
            device_id=device_at(step_x, step_y),
            device_id_type=MESH,
        )

    def start_all(source, target, send, recv, way):
        for bucket, (step_x, step_y) in enumerate(neighbour_steps):

            @pl.when(inside(way * step_x, way * step_y))
            def _(bucket=bucket, step_x=way * step_x, step_y=way * step_y):
                exchange(source, target, send, recv, bucket, step_x, step_y).start()

    def await_arrivals(source, target, send, recv, way):
        for bucket, (step_x, step_y) in enumerate(neighbour_steps):

            @pl.when(inside(-way * step_x, -way * step_y))
            def _(bucket=bucket, step_x=-way * step_x, step_y=-way * step_y):
                exchange(source, target, send, recv, bucket, step_x, step_y).wait_recv()

    def await_sent(source, target, send, recv, way):
        for bucket, (step_x, step_y) in enumerate(neighbour_steps):

            @pl.when(inside(way * step_x, way * step_y))
            def _(bucket=bucket, step_x=way * step_x, step_y=way * step_y):
                exchange(source, target, send, recv, bucket, step_x, step_y).wait_send()

    beside_x = jnp.where(place_x > 0, 2, 1) + jnp.where(place_x < domains_x - 1, 1, 0)
    beside_y = jnp.where(place_y > 0, 2, 1) + jnp.where(place_y < domains_y - 1, 1, 0)
    pl.semaphore_wait(barrier, beside_x * beside_y - 1)

    codes_move = (codes_out, codes_in, codes_send, codes_recv, 1)
    upstream_move = (upstream_out, upstream_in, upstream_send, upstream_recv, -1)
    hidden_move = (hidden_out, hidden_in, hidden_send, hidden_recv, 1)
    start_all(*codes_move)

    def spin_factors(terms):
        both = dot(terms, second[...])
        return [(both[:, 256 * k : 256 * k + 128], both[:, 256 * k + 128 : 256 * k + 256]) for k in range(2)]

    def rotation_row(terms, factors, place):
        cosine, sine = factors[0 if place < LOW else 1]
        both = dot(terms, first[:, place * 256 : place * 256 + 256])
        return cosine * both[:, 0:128] + sine * both[:, 128:256]

    own_terms = angle_terms(own_codes[2], own_codes[3])
    loads[0].wait()
    loads[1].wait()
    own_factors = spin_factors(own_terms)
    own_terms = own_terms[:, 0:48]
    source_masks = atom_masks(own_codes[0])
    inner_masks = atom_masks(column_of(inner_codes, 1))
    for place in range(FRAMED):
        row = rotation_row(own_terms, own_factors, place).astype(BF16)
        of_set = place if place < LOW else place - LOW
        source_rows = source_low if place < LOW else source_high
        inner_rows = inner_low if place < LOW else inner_high
        for half in range(2):
            columns = slice(128 * half, 128 * half + 128)
            source_rows[of_set * EDGES : (of_set + 1) * EDGES, columns] = row * source_masks[half]
            inner_rows[of_set * INNER : (of_set + 1) * INNER, columns] = (
                row[0:INNER] * inner_masks[half]
            )

    await_arrivals(*codes_move)
    arrived = codes_in[...].reshape(HALO, 128)
    in_terms = angle_terms(column_of(arrived, 1), column_of(arrived, 2))
    in_factors = spin_factors(in_terms)
    in_terms = in_terms[:, 0:48]
    in_masks = atom_masks(column_of(arrived, 0))
    wide_masks = []
    for half in range(2):
        mask = in_masks[half].astype(F32)
        wide_masks.append(
            [
                jnp.concatenate([mask[b * CAP : (b + 1) * CAP]] * 2, axis=0).astype(BF16)
                for b in range(BUCKETS)
            ]
        )
    for pair in range(PAIRS):
        rows = []
        for f in travel_rows[2 * pair : 2 * pair + 2]:
            if f is None:
                rows.append(jnp.zeros((HALO, 128), F32))
            else:
                rows.append(rotation_row(in_terms, in_factors, packed_rows.index(f)))
        for bucket in range(BUCKETS):
            slots = slice(bucket * CAP, (bucket + 1) * CAP)
            joined = jnp.concatenate([rows[0][slots], rows[1][slots]], axis=0).astype(BF16)
            for half in range(2):
                columns = slice(128 * half, 128 * half + 128)
                masked = joined * wide_masks[half][bucket]
                if pair < LOW_PAIRS:
                    incoming_low[bucket, 16 * pair : 16 * pair + 16, columns] = masked
                else:
                    at = 16 * (pair - LOW_PAIRS)
                    incoming_high[bucket, at : at + 16, columns] = masked
    loads[3].wait()
    loads[5].wait()
    cot_low, cot_high = coefficient_blocks(cotangent[...], spread[...])
    for bucket in range(BUCKETS):
        upstream_out[bucket, 0:LOW_TRAVEL, :] = dot(incoming_low[bucket], cot_low).astype(BF16)
        upstream_out[bucket, LOW_TRAVEL:TRAVEL, :] = dot(incoming_high[bucket], cot_high).astype(BF16)
    start_all(*upstream_move)

    loads[4].wait()
    centre = lax.broadcasted_iota(jnp.int32, (1, RADIAL), 1).astype(F32) * 2.0
    distance = (own_codes[4] - centre) * (22.0 / 1024.0)
    basis = jnp.exp(-0.5 * (distance * distance))
    basis_high = basis.astype(BF16)
    basis_low = (basis - basis_high.astype(F32)).astype(BF16)
    weight = radial_weight[...]
    weight_high = weight.astype(BF16)
    weight_low = (weight - weight_high.astype(F32)).astype(BF16)
    radial = dot(basis_high, weight_high) + (
        dot(basis_high, weight_low) + dot(basis_low, weight_high)
    )

    def put_grouped(f, block):
        if f < 7:
            framed_zero[:, f * C : (f + 1) * C] = block
        elif f < 19:
            minus = (f - 7) // 6
            at = (f - 7) % 6
            framed_one[minus * EDGES : (minus + 1) * EDGES, at * C : (at + 1) * C] = block
        else:
            minus = (f - 19) // 5
            at = (f - 19) % 5
            framed_two[minus * EDGES : (minus + 1) * EDGES, at * C : (at + 1) * C] = block

    loads[2].wait()
    feature_low, feature_high = coefficient_blocks(features[...], spread[...])
    for place, f in enumerate(packed_rows):
        if place < LOW:
            rows = source_low[place * EDGES : (place + 1) * EDGES, :]
            turned = dot(rows, feature_low)
        else:
            rows = source_high[(place - LOW) * EDGES : (place - LOW + 1) * EDGES, :]
            turned = dot(rows, feature_high)
        put_grouped(f, (turned * radial).astype(BF16))

    def put_hidden(f, block):
        hidden[f] = block
        place = packed_rows.index(f)
        narrow = block[0:INNER].astype(BF16)
        if place < LOW:
            hidden_low[place * INNER : (place + 1) * INNER, :] = narrow
        else:
            hidden_high[(place - LOW) * INNER : (place - LOW + 1) * INNER, :] = narrow

    def chunks(rows):
        return [(at, min(at + 2, rows)) for at in range(0, rows, 2)]

    loads[6].wait()
    gate = None
    for begin, end in chunks(7):
        value = dot(framed_zero[...], w_zero[:, begin * C : end * C])
        if gate is None:
            gate = 1.0 / (1.0 + jnp.exp(-value[:, 0:C]))
        for f in range(begin, end):
            put_hidden(f, value[:, (f - begin) * C : (f - begin + 1) * C] * gate)
    for number, (grouped, weights, size, at_plus, at_minus) in enumerate(
        ((framed_one, w_one, 6, 7, 13), (framed_two, w_two, 5, 19, 24))
    ):
        loads[7 + number].wait()
        for begin, end in chunks(size):
            real = dot(grouped[...], weights[0, :, begin * C : end * C])
            imag = dot(grouped[...], weights[1, :, begin * C : end * C])
            plus = real[0:EDGES] - imag[EDGES:]
            minus = imag[0:EDGES] + real[EDGES:]
            for f in range(begin, end):
                columns = slice((f - begin) * C, (f - begin + 1) * C)
                put_hidden(at_plus + f, plus[:, columns] * gate)
                put_hidden(at_minus + f, minus[:, columns] * gate)
    for pair in range(PAIRS):
        f, g = travel_rows[2 * pair : 2 * pair + 2]
        for bucket in range(BUCKETS):
            slots = slice(INNER + bucket * CAP, INNER + (bucket + 1) * CAP)
            upper = hidden[f, slots, :]
            lower = jnp.zeros((CAP, C), F32) if g is None else hidden[g, slots, :]
            hidden_out[bucket, 16 * pair : 16 * pair + 16, :] = jnp.concatenate(
                [upper, lower], axis=0
            ).astype(BF16)
    start_all(*hidden_move)

    for place, f in enumerate(packed_rows):
        if place < LOW:
            rows = inner_low[place * INNER : (place + 1) * INNER, :]
            upstream[f, 0:INNER, :] = dot(rows, cot_low)
        else:
            rows = inner_high[(place - LOW) * INNER : (place - LOW + 1) * INNER, :]
            upstream[f, 0:INNER, :] = dot(rows, cot_high)
    await_arrivals(*upstream_move)
    for pair in range(PAIRS):
        f, g = travel_rows[2 * pair : 2 * pair + 2]
        for bucket in range(BUCKETS):
            slots = slice(INNER + bucket * CAP, INNER + (bucket + 1) * CAP)
            both = upstream_in[bucket, 16 * pair : 16 * pair + 16, :].astype(F32)
            upstream[f, slots, :] = both[0:CAP]
            if g is not None:
                upstream[g, slots, :] = both[CAP:]

    total = upstream[0] * hidden[0]
    for f in range(1, FRAMED):
        total = total + upstream[f] * hidden[f]
    through = total * (0.25 * (1.0 - gate))
    scaled_gate = 0.25 * gate
    for f in range(FRAMED):
        block = upstream[f] * scaled_gate
        if f == 0:
            block = block + through
        put_grouped(f, block.astype(BF16))

    def put_back(f, block):
        place = packed_rows.index(f)
        narrow = (block * radial).astype(BF16)
        if place < LOW:
            back_low[place * EDGES : (place + 1) * EDGES, :] = narrow
        else:
            back_high[(place - LOW) * EDGES : (place - LOW + 1) * EDGES, :] = narrow

    for begin, end in chunks(7):
        value = dot_columns(framed_zero[...], w_zero[begin * C : end * C, :])
        for f in range(begin, end):
            put_back(f, value[:, (f - begin) * C : (f - begin + 1) * C])
    for grouped, weights, size, at_plus, at_minus in (
        (framed_one, w_one, 6, 7, 13),
        (framed_two, w_two, 5, 19, 24),
    ):
        for begin, end in chunks(size):
            real = dot_columns(grouped[...], weights[0, begin * C : end * C, :])
            imag = dot_columns(grouped[...], weights[1, begin * C : end * C, :])
            plus = real[0:EDGES] + imag[EDGES:]
            minus = real[EDGES:] - imag[0:EDGES]
            for f in range(begin, end):
                columns = slice((f - begin) * C, (f - begin + 1) * C)
                put_back(at_plus + f, plus[:, columns])
                put_back(at_minus + f, minus[:, columns])
    loads[9].wait()
    gradient_ref[...] = atom_rows(
        gather[...],
        dot_rows(back_low[...], source_low[...]),
        dot_rows(back_high[...], source_high[...]),
    )

    low = dot_rows(hidden_low[...], inner_low[...])
    high = dot_rows(hidden_high[...], inner_high[...])
    await_arrivals(*hidden_move)
    low = low + dot_rows(
        hidden_in[:, 0:LOW_TRAVEL, :].reshape(BUCKETS * LOW_TRAVEL, C),
        incoming_low[...].reshape(BUCKETS * LOW_TRAVEL, 256),
    )
    high = high + dot_rows(
        hidden_in[:, LOW_TRAVEL:TRAVEL, :].reshape(BUCKETS * (TRAVEL - LOW_TRAVEL), C),
        incoming_high[...].reshape(BUCKETS * (TRAVEL - LOW_TRAVEL), 256),
    )
    aggregate_ref[...] = atom_rows(gather[...], 0.25 * low, 0.25 * high)

    await_sent(*codes_move)
    await_sent(*upstream_move)
    await_sent(*hidden_move)


def on_device(
    domains_x,
    domains_y,
    features,
    cotangent,
    w_zero,
    w_one,
    w_two,
    radial_weight,
    inner_edges,
    halo_edges,
    halo_counts,
):
    first, second = rotation_tables()
    gather, spread = place_tables()
    tables = [jnp.asarray(table) for table in (first, second, gather, spread)]
    features = features.transpose(1, 0, 2).reshape(49 * ATOMS, C)
    cotangent = cotangent.transpose(1, 0, 2).reshape(49 * ATOMS, C)
    inner_edges = inner_edges.transpose(1, 0, 2)
    halo_edges = halo_edges.transpose(0, 2, 1, 3).reshape(5, BUCKETS, CAP)
    remote = pl.BlockSpec(memory_space=pltpu.HBM)
    vmem = pl.BlockSpec(memory_space=pltpu.VMEM)
    scratch = [
        (features.shape, BF16),
        (cotangent.shape, BF16),
        (w_zero.shape, BF16),
        (w_one.shape, BF16),
        (w_two.shape, BF16),
        (radial_weight.shape, F32),
        (first.shape, BF16),
        (second.shape, BF16),
        (gather.shape, BF16),
        (spread.shape, BF16),
        (inner_edges.shape, jnp.int32),
        (halo_edges.shape, jnp.int32),
        (halo_counts.shape, jnp.int32),
        ((128, 128), F32),
        ((BUCKETS, CAP, 128), F32),
        ((BUCKETS, CAP, 128), F32),
        ((LOW * EDGES, 256), BF16),
        ((HIGH * EDGES, 256), BF16),
        ((LOW * INNER, 256), BF16),
        ((HIGH * INNER, 256), BF16),
        ((BUCKETS, LOW_TRAVEL, 256), BF16),
        ((BUCKETS, TRAVEL - LOW_TRAVEL, 256), BF16),
        ((EDGES, 7 * C), BF16),
        ((2 * EDGES, 6 * C), BF16),
        ((2 * EDGES, 5 * C), BF16),
        ((FRAMED, EDGES, C), F32),
        ((LOW * INNER, C), BF16),
        ((HIGH * INNER, C), BF16),
        ((BUCKETS, TRAVEL, C), BF16),
        ((BUCKETS, TRAVEL, C), BF16),
        ((FRAMED, EDGES, C), F32),
        ((BUCKETS, TRAVEL, C), BF16),
        ((BUCKETS, TRAVEL, C), BF16),
        ((LOW * EDGES, C), BF16),
        ((HIGH * EDGES, C), BF16),
    ]
    aggregate, gradient = pl.pallas_call(
        functools.partial(kernel, domains_x, domains_y),
        out_shape=(
            jax.ShapeDtypeStruct(features.shape, BF16),
            jax.ShapeDtypeStruct(features.shape, BF16),
        ),
        in_specs=[remote] * 13,
        out_specs=(vmem, vmem),
        scratch_shapes=[pltpu.VMEM(shape, dtype) for shape, dtype in scratch]
        + [pltpu.SemaphoreType.DMA((3,)), pltpu.SemaphoreType.DMA((10,))]
        + [pltpu.SemaphoreType.DMA((BUCKETS,))] * 6,
        compiler_params=pltpu.CompilerParams(
            collective_id=0, has_side_effects=True, vmem_limit_bytes=60 * 1024 * 1024
        ),
        cost_estimate=pl.CostEstimate(
            flops=6 * 10**9, bytes_accessed=8 * 10**6, transcendentals=10**5
        ),
        name="message_layer",
    )(
        features,
        cotangent,
        w_zero,
        w_one,
        w_two,
        radial_weight,
        *tables,
        inner_edges,
        halo_edges,
        halo_counts,
    )
    return tuple(
        rows.reshape(49, ATOMS, C).transpose(1, 0, 2) for rows in (aggregate, gradient)
    )


def solution(mesh):
    return jax.shard_map(
        functools.partial(on_device, mesh.shape["gx"], mesh.shape["gy"]),
        mesh=mesh,
        in_specs=(
            P(("img", "gx", "gy"), None, None),
            P(("img", "gx", "gy"), None, None),
            P(),
            P(),
            P(),
            P(),
            P(("img", "gx", "gy"), None, None),
            P(("img", "gx", "gy"), None, None, None),
            P(("img", "gx", "gy"), None),
        ),
        out_specs=(P(("img", "gx", "gy"), None, None), P(("img", "gx", "gy"), None, None)),
        check_vma=False,
    )
```

```python
import functools
import math

import jax
import jax.numpy as jnp
import numpy as np
from jax import lax
from jax.experimental import pallas as pl
from jax.experimental.pallas import tpu as pltpu
from jax.sharding import PartitionSpec as P

MESH = pl.DeviceIdType.MESH
F32 = jnp.float32
BF16 = jnp.bfloat16

neighbour_steps = ((-1, -1), (-1, 0), (-1, 1), (0, -1), (0, 1), (1, -1), (1, 0), (1, 1))
BUCKETS = 8
CAP = 8
INNER = 96
HALO = BUCKETS * CAP
EDGES = INNER + HALO
ATOMS = 8
C = 128
RADIAL = 512

framed_rows = [(degree, order) for order in (0, 1, -1, 2, -2) for degree in range(abs(order), 7)]
low_rows = [f for f, (degree, order) in enumerate(framed_rows) if degree <= 4]
high_rows = [f for f, (degree, order) in enumerate(framed_rows) if degree > 4]
packed_rows = low_rows + high_rows
LOW = len(low_rows)
HIGH = len(high_rows)
FRAMED = LOW + HIGH
travel_rows = low_rows + [None] + high_rows
PAIRS = len(travel_rows) // 2
LOW_PAIRS = (LOW + 1) // 2
LOW_TRAVEL = LOW_PAIRS * 16
TRAVEL = PAIRS * 16
group_bounds = ((0, 7), (7, 13), (13, 19), (19, 24), (24, 29))


def harmonics(east, north, height):
    columns = np.zeros((height.shape[0], 49))
    real_part = np.ones(height.shape)
    imag_part = np.zeros(height.shape)
    for moment in range(7):
        if moment > 0:
            real_part, imag_part = (
                real_part * east - imag_part * north,
                real_part * north + imag_part * east,
            )
        older = np.zeros(height.shape)
        newer = (
            (-1.0) ** moment * float(np.prod(np.arange(1, 2 * moment, 2))) * np.ones(height.shape)
        )
        for degree in range(moment, 7):
            if degree > moment:
                older, newer = (
                    newer,
                    ((2 * degree - 1) * height * newer - (degree + moment - 1) * older)
                    / (degree - moment),
                )
            factor = math.sqrt(
                (2 * degree + 1)
                / (4.0 * math.pi)
                * math.factorial(degree - moment)
                / math.factorial(degree + moment)
            )
            centre = degree * degree + degree
            if moment == 0:
                columns[:, centre] = factor * newer
            else:
                columns[:, centre + moment] = math.sqrt(2.0) * factor * newer * real_part
                columns[:, centre - moment] = math.sqrt(2.0) * factor * newer * imag_part
    return columns


def legendre_pair(order, points):
    older = np.ones(points.shape)
    newer = points * 1.0
    for degree in range(2, order + 1):
        older, newer = (newer, ((2 * degree - 1) * points * newer - (degree - 1) * older) / degree)
    slope = order * (points * newer - older) / (points * points - 1.0)
    return (newer, slope)


def gauss_nodes(order):
    nodes = np.cos(math.pi * (np.arange(order) + 0.75) / (order + 0.5))
    for sweep in range(20):
        value, slope = legendre_pair(order, nodes)
        nodes = nodes - value / slope
    value, slope = legendre_pair(order, nodes)
    return (nodes, 2.0 / ((1.0 - nodes * nodes) * slope * slope))


def tilt_table():
    nodes, node_weights = gauss_nodes(7)
    turns = 16
    azimuth = 2.0 * math.pi * np.arange(turns) / turns
    height = np.repeat(nodes, turns)
    weights = np.repeat(node_weights, turns) * (2.0 * math.pi / turns)
    spread = np.tile(azimuth, nodes.shape[0])
    radius = np.sqrt(np.maximum(1.0 - height * height, 0.0))
    east = radius * np.cos(spread)
    north = radius * np.sin(spread)
    before = harmonics(east, north, height)
    after = harmonics(east, -height, north)
    full = after.T @ (before * weights[:, None])
    table = np.zeros((49, 49))
    for degree in range(7):
        first_row = degree * degree
        last_row = first_row + 2 * degree + 1
        table[first_row:last_row, first_row:last_row] = full[first_row:last_row, first_row:last_row]
    return table


def split_bf16(table):
    high = table.astype(jnp.bfloat16)
    low = (table - high.astype(np.float64)).astype(jnp.bfloat16)
    return high, low


@functools.lru_cache(maxsize=None)
def rotation_tables():
    tilt = tilt_table()
    degrees = np.array([l for l in range(7) for m in range(-l, l + 1)])
    orders = np.array([m for l in range(7) for m in range(-l, l + 1)])
    partner = degrees * degrees + degrees - orders
    signs = -np.sign(orders).astype(np.float64)
    matrix = np.zeros((16, 49, 49))
    for i in range(49):
        moment = abs(orders[i])
        matrix[moment] += np.outer(tilt[i], tilt[i])
        if moment > 0:
            matrix[6 + moment] += signs[i] * np.outer(tilt[i], tilt[partner[i]])
    swapped = matrix[:, :, partner] * (-signs)[None, None, :]
    first = np.zeros((16, FRAMED * 256))
    for place, f in enumerate(packed_rows):
        degree, order = framed_rows[f]
        row = degree * degree + degree + order
        start = 0 if degree <= 4 else 24
        for j in range(degree * degree, (degree + 1) * (degree + 1)):
            for atom in range(4):
                lane = place * 256 + atom * 32 + j - start
                first[:, lane] = matrix[:, row, j]
                first[:, lane + 128] = swapped[:, row, j]
    high, low = split_bf16(first)
    first = np.concatenate([high, low, high], axis=0)
    second = np.zeros((128, 512))
    for column, (lowest, highest, start) in enumerate(((0, 25, 0), (25, 49, 24))):
        for j in range(lowest, highest):
            moment = abs(orders[j])
            for atom in range(4):
                lane = column * 256 + atom * 32 + j - start
                for part in (64, 96):
                    second[part + moment, lane] = 1.0
                    if moment > 0:
                        second[part + 6 + moment, lane + 128] = 1.0
    return first, second.astype(jnp.bfloat16)


LOW_PART = slice(0, 25 * ATOMS)
HIGH_PART = slice(24 * ATOMS, 49 * ATOMS)


def place_tables():
    gather = np.zeros((25 * ATOMS, 256))
    for place in range(25):
        for atom in range(ATOMS):
            gather[place * ATOMS + atom, atom * 32 + place] = 1.0
    return gather.astype(jnp.bfloat16), gather.T.astype(jnp.bfloat16)


def cosine_terms():
    points = 0.125 + 0.125 * np.cos(math.pi * (np.arange(200) + 0.5) / 200)
    fit = np.polynomial.chebyshev.Chebyshev.fit(
        points, np.cos(2.0 * math.pi * np.sqrt(points)), 8, domain=[0.0, 0.25]
    )
    return [float(term) for term in fit.convert(kind=np.polynomial.Polynomial).coef]


def column_of(columns, which):
    return columns[:, which : which + 1]


def dot(left, right):
    return jnp.dot(left, right, preferred_element_type=F32)


def dot_rows(left, right):
    return lax.dot_general(left, right, (((0,), (0,)), ((), ())), preferred_element_type=F32)


def dot_columns(left, right):
    return lax.dot_general(left, right, (((1,), (1,)), ((), ())), preferred_element_type=F32)


def angle_terms(alpha, beta):
    lane = lax.broadcasted_iota(jnp.int32, (1, 128), 1)
    term = lane & 15
    moment = jnp.where(term < 7, term, term - 6).astype(F32)
    shift = jnp.where(term < 7, 0.0, -0.25).astype(F32)
    code = jnp.where(lane < 64, beta, alpha)
    turns = code * (moment * (1.0 / 4096.0)) + shift
    turns = turns - jnp.floor(turns + 0.5)
    square = turns * turns
    terms = cosine_terms()
    value = terms[-1]
    for coefficient in terms[-2::-1]:
        value = value * square + coefficient
    high = value.astype(BF16).astype(F32)
    return jnp.where((lane & 63) < 32, high, value - high).astype(BF16)


def atom_masks(atoms):
    lane = lax.broadcasted_iota(jnp.int32, (1, 128), 1) >> 5
    lane = lane.astype(F32)
    return [jnp.where(atoms == lane + 4.0 * half, 1.0, 0.0).astype(BF16) for half in range(2)]


def coefficient_blocks(refs, spread):
    return [
        dot(spread, jnp.concatenate([ref[part, :] for ref in refs], axis=1)).astype(BF16)
        for part in (LOW_PART, HIGH_PART)
    ]


def atom_rows(gather, low_columns, high_columns):
    low = dot_columns(gather, low_columns.astype(BF16))
    high = dot_columns(gather, high_columns.astype(BF16))
    return jnp.concatenate(
        [low[0:192], low[192:200] + high[0:ATOMS], high[ATOMS:200]], axis=0
    ).astype(BF16)


def kernel(
    domains_x,
    domains_y,
    features_hbm,
    cotangent_hbm,
    w_zero_hbm,
    w_one_hbm,
    w_two_hbm,
    radial_hbm,
    first_hbm,
    second_hbm,
    gather_hbm,
    spread_hbm,
    inner_hbm,
    halo_hbm,
    counts_hbm,
    aggregate_ref,
    gradient_ref,
    features,
    cotangent,
    w_zero,
    w_one,
    w_two,
    radial_weight,
    first,
    second,
    gather,
    spread,
    inner_ref,
    halo_ref,
    counts_ref,
    codes_table,
    codes_out,
    codes_in,
    source_low,
    source_high,
    inner_low,
    inner_high,
    incoming_low,
    incoming_high,
    target_low,
    target_high,
    framed_zero,
    framed_one,
    framed_two,
    hidden,
    hidden_low,
    hidden_high,
    hidden_out,
    hidden_in,
    upstream,
    cotangent_in,
    back_low,
    back_high,
    small_sems,
    load_sems,
    codes_send,
    codes_recv,
    cotangent_send,
    cotangent_recv,
    hidden_send,
    hidden_recv,
):
    place_x = lax.axis_index("gx")
    place_y = lax.axis_index("gy")
    image = lax.axis_index("img")

    small_loads = [
        pltpu.make_async_copy(source, target, small_sems.at[number])
        for number, (source, target) in enumerate(
            ((inner_hbm, inner_ref), (halo_hbm, halo_ref), (counts_hbm, counts_ref))
        )
    ]
    for load in small_loads:
        load.start()
    loads = [
        pltpu.make_async_copy(source, target, load_sems.at[number])
        for number, (source, target) in enumerate(
            (
                (first_hbm, first),
                (second_hbm, second),
                (features_hbm, features),
                (cotangent_hbm, cotangent),
                (radial_hbm, radial_weight),
                (spread_hbm, spread),
                (w_zero_hbm, w_zero),
                (w_one_hbm, w_one),
                (w_two_hbm, w_two),
                (gather_hbm, gather),
            )
        )
    ]
    for load in loads:
        load.start()

    def inside(step_x, step_y):
        x = place_x + step_x
        y = place_y + step_y
        return (x >= 0) & (x < domains_x) & (y >= 0) & (y < domains_y)

    def device_at(step_x, step_y):
        return (place_x + step_x, place_y + step_y, image)

    barrier = pltpu.get_barrier_semaphore()
    for step_x, step_y in neighbour_steps:

        @pl.when(inside(step_x, step_y))
        def _(step_x=step_x, step_y=step_y):
            pl.semaphore_signal(
                barrier, inc=1, device_id=device_at(step_x, step_y), device_id_type=MESH
            )

    for bucket, (step_x, step_y) in enumerate(neighbour_steps):

        @pl.when(jnp.logical_not(inside(-step_x, -step_y)))
        def _(bucket=bucket):
            codes_in[bucket] = jnp.full((CAP, 128), -1.0, F32)
            hidden_in[bucket] = jnp.zeros((TRAVEL, C), BF16)

        @pl.when(jnp.logical_not(inside(step_x, step_y)))
        def _(bucket=bucket):
            cotangent_in[bucket] = jnp.zeros((ATOMS * 49, C), BF16)

    codes_table[...] = jnp.zeros((128, 128), F32)
    for load in small_loads:
        load.wait()
    counts = counts_ref[...].astype(F32)
    for which in range(5):
        codes_table[which * BUCKETS : (which + 1) * BUCKETS, 0:CAP] = halo_ref[which].astype(F32)
        codes_table[40 + which : 41 + which, 0:INNER] = inner_ref[which].astype(F32)
    turned_codes = codes_table[...].T
    inner_codes = turned_codes[0:INNER, 40:45]
    lane = lax.broadcasted_iota(jnp.int32, (CAP, 128), 1)
    slot = lax.broadcasted_iota(jnp.int32, (CAP, 1), 0).astype(F32)
    halo_codes = [
        [column_of(turned_codes[0:CAP], which * BUCKETS + bucket) for bucket in range(BUCKETS)]
        for which in range(5)
    ]
    halo_targets = []
    for bucket in range(BUCKETS):
        target = jnp.where(slot < column_of(counts, bucket), halo_codes[1][bucket], -1.0)
        codes_out[bucket] = jnp.where(
            lane == 0, target, jnp.where(lane == 1, halo_codes[2][bucket], halo_codes[3][bucket])
        )
        halo_targets.append(target)
    own_codes = [
        jnp.concatenate([column_of(inner_codes, which)] + halo_codes[which], axis=0)
        for which in range(5)
    ]

    def exchange(source, target, send, recv, bucket, step_x, step_y):
        return pltpu.make_async_remote_copy(
            src_ref=source if source is cotangent_hbm else source.at[bucket],
            dst_ref=target.at[bucket],
            send_sem=send.at[bucket],
            recv_sem=recv.at[bucket],
            device_id=device_at(step_x, step_y),
            device_id_type=MESH,
        )

    def start_all(source, target, send, recv, way):
        for bucket, (step_x, step_y) in enumerate(neighbour_steps):

            @pl.when(inside(way * step_x, way * step_y))
            def _(bucket=bucket, step_x=way * step_x, step_y=way * step_y):
                exchange(source, target, send, recv, bucket, step_x, step_y).start()

    def await_arrivals(source, target, send, recv, way):
        for bucket, (step_x, step_y) in enumerate(neighbour_steps):

            @pl.when(inside(-way * step_x, -way * step_y))
            def _(bucket=bucket, step_x=-way * step_x, step_y=-way * step_y):
                exchange(source, target, send, recv, bucket, step_x, step_y).wait_recv()

    def await_sent(source, target, send, recv, way):
        for bucket, (step_x, step_y) in enumerate(neighbour_steps):

            @pl.when(inside(way * step_x, way * step_y))
            def _(bucket=bucket, step_x=way * step_x, step_y=way * step_y):
                exchange(source, target, send, recv, bucket, step_x, step_y).wait_send()

    beside_x = jnp.where(place_x > 0, 2, 1) + jnp.where(place_x < domains_x - 1, 1, 0)
    beside_y = jnp.where(place_y > 0, 2, 1) + jnp.where(place_y < domains_y - 1, 1, 0)
    pl.semaphore_wait(barrier, beside_x * beside_y - 1)

    codes_move = (codes_out, codes_in, codes_send, codes_recv, 1)
    cotangent_move = (cotangent_hbm, cotangent_in, cotangent_send, cotangent_recv, -1)
    hidden_move = (hidden_out, hidden_in, hidden_send, hidden_recv, 1)
    start_all(*codes_move)
    start_all(*cotangent_move)

    def spin_factors(terms):
        both = dot(terms, second[...])
        return [(both[:, 256 * k : 256 * k + 128], both[:, 256 * k + 128 : 256 * k + 256]) for k in range(2)]

    def rotation_row(terms, factors, place):
        cosine, sine = factors[0 if place < LOW else 1]
        both = dot(terms, first[:, place * 256 : place * 256 + 256])
        return cosine * both[:, 0:128] + sine * both[:, 128:256]

    own_terms = angle_terms(own_codes[2], own_codes[3])
    loads[0].wait()
    loads[1].wait()
    own_factors = spin_factors(own_terms)
    own_terms = own_terms[:, 0:48]
    source_masks = atom_masks(own_codes[0])
    inner_masks = atom_masks(column_of(inner_codes, 1))
    def wide_masks(atoms):
        masks = [mask.astype(F32) for mask in atom_masks(atoms)]
        return [
            [
                jnp.concatenate([mask[b * CAP : (b + 1) * CAP]] * 2, axis=0).astype(BF16)
                for b in range(BUCKETS)
            ]
            for mask in masks
        ]

    def put_pair(pair, rows, masks, low, high):
        for bucket in range(BUCKETS):
            slots = slice(bucket * CAP, (bucket + 1) * CAP)
            joined = jnp.concatenate([rows[0][slots], rows[1][slots]], axis=0).astype(BF16)
            for half in range(2):
                columns = slice(128 * half, 128 * half + 128)
                masked = joined * masks[half][bucket]
                if pair < LOW_PAIRS:
                    low[bucket, 16 * pair : 16 * pair + 16, columns] = masked
                else:
                    at = 16 * (pair - LOW_PAIRS)
                    high[bucket, at : at + 16, columns] = masked

    target_masks = wide_masks(jnp.concatenate(halo_targets, axis=0))
    for pair in range(PAIRS):
        halo_rows = []
        for f in travel_rows[2 * pair : 2 * pair + 2]:
            if f is None:
                halo_rows.append(jnp.zeros((HALO, 128), F32))
                continue
            place = packed_rows.index(f)
            wide = rotation_row(own_terms, own_factors, place)
            halo_rows.append(wide[INNER:])
            row = wide.astype(BF16)
            of_set = place if place < LOW else place - LOW
            source_rows = source_low if place < LOW else source_high
            inner_rows = inner_low if place < LOW else inner_high
            for half in range(2):
                columns = slice(128 * half, 128 * half + 128)
                source_rows[of_set * EDGES : (of_set + 1) * EDGES, columns] = (
                    row * source_masks[half]
                )
                inner_rows[of_set * INNER : (of_set + 1) * INNER, columns] = (
                    row[0:INNER] * inner_masks[half]
                )
        put_pair(pair, halo_rows, target_masks, target_low, target_high)

    loads[4].wait()
    centre = lax.broadcasted_iota(jnp.int32, (1, RADIAL), 1).astype(F32) * 2.0
    distance = (own_codes[4] - centre) * (22.0 / 1024.0)
    basis = jnp.exp(-0.5 * (distance * distance))
    basis_high = basis.astype(BF16)
    basis_low = (basis - basis_high.astype(F32)).astype(BF16)
    weight = radial_weight[...]
    weight_high = weight.astype(BF16)
    weight_low = (weight - weight_high.astype(F32)).astype(BF16)
    radial = dot(basis_high, weight_high) + (
        dot(basis_high, weight_low) + dot(basis_low, weight_high)
    )

    def put_grouped(f, block, sign):
        if f < 7:
            framed_zero[:, f * C : (f + 1) * C] = block
            return
        grouped, size, at = (framed_one, 6, f - 7) if f < 19 else (framed_two, 5, f - 19)
        minus, at = at // size, at % size
        own = slice(minus * EDGES, (minus + 1) * EDGES)
        other = slice((1 - minus) * EDGES, (2 - minus) * EDGES)
        grouped[own, at * C : (at + 1) * C] = block
        grouped[other, (size + at) * C : (size + at + 1) * C] = (
            block if (sign > 0) == (minus == 1) else -block
        )

    loads[2].wait()
    loads[5].wait()
    feature_low, feature_high = coefficient_blocks([features], spread[...])
    for place, f in enumerate(packed_rows):
        if place < LOW:
            rows = source_low[place * EDGES : (place + 1) * EDGES, :]
            turned = dot(rows, feature_low)
        else:
            rows = source_high[(place - LOW) * EDGES : (place - LOW + 1) * EDGES, :]
            turned = dot(rows, feature_high)
        put_grouped(f, (turned * radial).astype(BF16), -1)

    def put_hidden(f, block):
        hidden[f] = block
        place = packed_rows.index(f)
        narrow = block[0:INNER].astype(BF16)
        if place < LOW:
            hidden_low[place * INNER : (place + 1) * INNER, :] = narrow
        else:
            hidden_high[(place - LOW) * INNER : (place - LOW + 1) * INNER, :] = narrow

    def chunks(rows):
        return [(at, min(at + 2, rows)) for at in range(0, rows, 2)]

    loads[6].wait()
    gate = None
    for begin, end in chunks(7):
        value = dot(framed_zero[...], w_zero[:, begin * C : end * C])
        if gate is None:
            gate = 1.0 / (1.0 + jnp.exp(-value[:, 0:C]))
        for f in range(begin, end):
            put_hidden(f, value[:, (f - begin) * C : (f - begin + 1) * C] * gate)
    for number, (grouped, weights, size, at_plus, at_minus) in enumerate(
        ((framed_one, w_one, 6, 7, 13), (framed_two, w_two, 5, 19, 24))
    ):
        loads[7 + number].wait()
        for begin, end in chunks(size):
            value = dot(grouped[...], weights[:, begin * C : end * C])
            for f in range(begin, end):
                columns = slice((f - begin) * C, (f - begin + 1) * C)
                put_hidden(at_plus + f, value[0:EDGES, columns] * gate)
                put_hidden(at_minus + f, value[EDGES:, columns] * gate)
    for pair in range(PAIRS):
        f, g = travel_rows[2 * pair : 2 * pair + 2]
        for bucket in range(BUCKETS):
            slots = slice(INNER + bucket * CAP, INNER + (bucket + 1) * CAP)
            upper = hidden[f, slots, :]
            lower = jnp.zeros((CAP, C), F32) if g is None else hidden[g, slots, :]
            hidden_out[bucket, 16 * pair : 16 * pair + 16, :] = jnp.concatenate(
                [upper, lower], axis=0
            ).astype(BF16)
    start_all(*hidden_move)

    await_arrivals(*codes_move)
    arrived = codes_in[...].reshape(HALO, 128)
    in_terms = angle_terms(column_of(arrived, 1), column_of(arrived, 2))
    in_factors = spin_factors(in_terms)
    in_terms = in_terms[:, 0:48]
    in_masks = wide_masks(column_of(arrived, 0))
    for pair in range(PAIRS):
        rows = [
            jnp.zeros((HALO, 128), F32)
            if f is None
            else rotation_row(in_terms, in_factors, packed_rows.index(f))
            for f in travel_rows[2 * pair : 2 * pair + 2]
        ]
        put_pair(pair, rows, in_masks, incoming_low, incoming_high)

    low = dot_rows(hidden_low[...], inner_low[...])
    high = dot_rows(hidden_high[...], inner_high[...])

    loads[3].wait()
    cot_low, cot_high = coefficient_blocks([cotangent], spread[...])
    for place, f in enumerate(packed_rows):
        if place < LOW:
            rows = inner_low[place * INNER : (place + 1) * INNER, :]
            upstream[f, 0:INNER, :] = dot(rows, cot_low)
        else:
            rows = inner_high[(place - LOW) * INNER : (place - LOW + 1) * INNER, :]
            upstream[f, 0:INNER, :] = dot(rows, cot_high)
    await_arrivals(*cotangent_move)
    for bucket in range(BUCKETS):
        slots = slice(INNER + bucket * CAP, INNER + (bucket + 1) * CAP)
        if bucket % 2 == 0:
            both_low, both_high = coefficient_blocks(
                [cotangent_in.at[bucket], cotangent_in.at[bucket + 1]], spread[...]
            )
        columns = slice(bucket % 2 * C, (bucket % 2 + 1) * C)
        turned = (
            dot(target_low[bucket], both_low[:, columns]),
            dot(target_high[bucket], both_high[:, columns]),
        )
        for pair in range(PAIRS):
            of_set = turned[0 if pair < LOW_PAIRS else 1]
            at = 16 * (pair if pair < LOW_PAIRS else pair - LOW_PAIRS)
            for half, f in enumerate(travel_rows[2 * pair : 2 * pair + 2]):
                if f is not None:
                    upstream[f, slots, :] = of_set[at + CAP * half : at + CAP * (half + 1)]

    total = upstream[0] * hidden[0]
    for f in range(1, FRAMED):
        total = total + upstream[f] * hidden[f]
    through = total * (0.25 * (1.0 - gate))
    scaled_gate = 0.25 * gate
    for f in range(FRAMED):
        block = upstream[f] * scaled_gate
        if f == 0:
            block = block + through
        put_grouped(f, block.astype(BF16), 1)

    def put_back(f, block):
        place = packed_rows.index(f)
        narrow = (block * radial).astype(BF16)
        if place < LOW:
            back_low[place * EDGES : (place + 1) * EDGES, :] = narrow
        else:
            back_high[(place - LOW) * EDGES : (place - LOW + 1) * EDGES, :] = narrow

    for begin, end in chunks(7):
        value = dot_columns(framed_zero[...], w_zero[begin * C : end * C, :])
        for f in range(begin, end):
            put_back(f, value[:, (f - begin) * C : (f - begin + 1) * C])
    for grouped, weights, size, at_plus, at_minus in (
        (framed_one, w_one, 6, 7, 13),
        (framed_two, w_two, 5, 19, 24),
    ):
        for begin, end in chunks(size):
            rows = slice(begin * C, end * C)
            rows_after = slice((size + begin) * C, (size + end) * C)
            value = dot_columns(
                grouped[...], jnp.concatenate([weights[rows, :], weights[rows_after, :]], axis=1)
            )
            for f in range(begin, end):
                columns = slice((f - begin) * C, (f - begin + 1) * C)
                put_back(at_plus + f, value[0:EDGES, columns])
                put_back(at_minus + f, value[EDGES:, columns])
    loads[9].wait()
    gradient_ref[...] = atom_rows(
        gather[...],
        dot_rows(back_low[...], source_low[...]),
        dot_rows(back_high[...], source_high[...]),
    )

    await_arrivals(*hidden_move)
    low = low + dot_rows(
        hidden_in[:, 0:LOW_TRAVEL, :].reshape(BUCKETS * LOW_TRAVEL, C),
        incoming_low[...].reshape(BUCKETS * LOW_TRAVEL, 256),
    )
    high = high + dot_rows(
        hidden_in[:, LOW_TRAVEL:TRAVEL, :].reshape(BUCKETS * (TRAVEL - LOW_TRAVEL), C),
        incoming_high[...].reshape(BUCKETS * (TRAVEL - LOW_TRAVEL), 256),
    )
    aggregate_ref[...] = atom_rows(gather[...], 0.25 * low, 0.25 * high)

    await_sent(*codes_move)
    await_sent(*cotangent_move)
    await_sent(*hidden_move)


def on_device(
    domains_x,
    domains_y,
    features,
    cotangent,
    w_zero,
    w_one,
    w_two,
    radial_weight,
    inner_edges,
    halo_edges,
    halo_counts,
):
    first, second = rotation_tables()
    gather, spread = place_tables()
    tables = [jnp.asarray(table) for table in (first, second, gather, spread)]
    features = features.transpose(1, 0, 2).reshape(49 * ATOMS, C)
    cotangent = cotangent.transpose(1, 0, 2).reshape(49 * ATOMS, C)
    w_one = w_one.reshape(12 * C, 6 * C)
    w_two = w_two.reshape(10 * C, 5 * C)
    inner_edges = inner_edges.transpose(1, 0, 2)
    halo_edges = halo_edges.transpose(0, 2, 1, 3).reshape(5, BUCKETS, CAP)
    remote = pl.BlockSpec(memory_space=pltpu.HBM)
    vmem = pl.BlockSpec(memory_space=pltpu.VMEM)
    scratch = [
        (features.shape, BF16),
        (cotangent.shape, BF16),
        (w_zero.shape, BF16),
        (w_one.shape, BF16),
        (w_two.shape, BF16),
        (radial_weight.shape, F32),
        (first.shape, BF16),
        (second.shape, BF16),
        (gather.shape, BF16),
        (spread.shape, BF16),
        (inner_edges.shape, jnp.int32),
        (halo_edges.shape, jnp.int32),
        (halo_counts.shape, jnp.int32),
        ((128, 128), F32),
        ((BUCKETS, CAP, 128), F32),
        ((BUCKETS, CAP, 128), F32),
        ((LOW * EDGES, 256), BF16),
        ((HIGH * EDGES, 256), BF16),
        ((LOW * INNER, 256), BF16),
        ((HIGH * INNER, 256), BF16),
        ((BUCKETS, LOW_TRAVEL, 256), BF16),
        ((BUCKETS, TRAVEL - LOW_TRAVEL, 256), BF16),
        ((BUCKETS, LOW_TRAVEL, 256), BF16),
        ((BUCKETS, TRAVEL - LOW_TRAVEL, 256), BF16),
        ((EDGES, 7 * C), BF16),
        ((2 * EDGES, 12 * C), BF16),
        ((2 * EDGES, 10 * C), BF16),
        ((FRAMED, EDGES, C), F32),
        ((LOW * INNER, C), BF16),
        ((HIGH * INNER, C), BF16),
        ((BUCKETS, TRAVEL, C), BF16),
        ((BUCKETS, TRAVEL, C), BF16),
        ((FRAMED, EDGES, C), F32),
        ((BUCKETS,) + cotangent.shape, BF16),
        ((LOW * EDGES, C), BF16),
        ((HIGH * EDGES, C), BF16),
    ]
    aggregate, gradient = pl.pallas_call(
        functools.partial(kernel, domains_x, domains_y),
        out_shape=(
            jax.ShapeDtypeStruct(features.shape, BF16),
            jax.ShapeDtypeStruct(features.shape, BF16),
        ),
        in_specs=[remote] * 13,
        out_specs=(vmem, vmem),
        scratch_shapes=[pltpu.VMEM(shape, dtype) for shape, dtype in scratch]
        + [pltpu.SemaphoreType.DMA((3,)), pltpu.SemaphoreType.DMA((10,))]
        + [pltpu.SemaphoreType.DMA((BUCKETS,))] * 6,
        compiler_params=pltpu.CompilerParams(
            collective_id=0, has_side_effects=True, vmem_limit_bytes=60 * 1024 * 1024
        ),
        cost_estimate=pl.CostEstimate(
            flops=6 * 10**9, bytes_accessed=8 * 10**6, transcendentals=10**5
        ),
        name="message_layer",
    )(
        features,
        cotangent,
        w_zero,
        w_one,
        w_two,
        radial_weight,
        *tables,
        inner_edges,
        halo_edges,
        halo_counts,
    )
    return tuple(
        rows.reshape(49, ATOMS, C).transpose(1, 0, 2) for rows in (aggregate, gradient)
    )


def solution(mesh):
    return jax.shard_map(
        functools.partial(on_device, mesh.shape["gx"], mesh.shape["gy"]),
        mesh=mesh,
        in_specs=(
            P(("img", "gx", "gy"), None, None),
            P(("img", "gx", "gy"), None, None),
            P(),
            P(),
            P(),
            P(),
            P(("img", "gx", "gy"), None, None),
            P(("img", "gx", "gy"), None, None, None),
            P(("img", "gx", "gy"), None),
        ),
        out_specs=(P(("img", "gx", "gy"), None, None), P(("img", "gx", "gy"), None, None)),
        check_vma=False,
    )
```

```python
import collections
import functools
import math

import jax
import jax.numpy as jnp
import numpy as np
from jax import lax
from jax.experimental import pallas as pl
from jax.experimental.pallas import tpu as pltpu
from jax.sharding import PartitionSpec as P

MESH = pl.DeviceIdType.MESH
F32 = jnp.float32
BF16 = jnp.bfloat16

neighbour_steps = ((-1, -1), (-1, 0), (-1, 1), (0, -1), (0, 1), (1, -1), (1, 0), (1, 1))
BUCKETS = 8
CAP = 8
INNER = 96
HALO = BUCKETS * CAP
EDGES = INNER + HALO
ATOMS = 8
C = 128
RADIAL = 512

framed_rows = [(degree, order) for order in (0, 1, -1, 2, -2) for degree in range(abs(order), 7)]
low_rows = [f for f, (degree, order) in enumerate(framed_rows) if degree <= 4]
high_rows = [f for f, (degree, order) in enumerate(framed_rows) if degree > 4]
packed_rows = low_rows + high_rows
LOW = len(low_rows)
HIGH = len(high_rows)
FRAMED = LOW + HIGH
travel_rows = low_rows + [None] + high_rows
PAIRS = len(travel_rows) // 2
LOW_PAIRS = (LOW + 1) // 2
LOW_TRAVEL = LOW_PAIRS * 16
TRAVEL = PAIRS * 16
group_bounds = ((0, 7), (7, 13), (13, 19), (19, 24), (24, 29))


def harmonics(east, north, height):
    columns = np.zeros((height.shape[0], 49))
    real_part = np.ones(height.shape)
    imag_part = np.zeros(height.shape)
    for moment in range(7):
        if moment > 0:
            real_part, imag_part = (
                real_part * east - imag_part * north,
                real_part * north + imag_part * east,
            )
        older = np.zeros(height.shape)
        newer = (
            (-1.0) ** moment * float(np.prod(np.arange(1, 2 * moment, 2))) * np.ones(height.shape)
        )
        for degree in range(moment, 7):
            if degree > moment:
                older, newer = (
                    newer,
                    ((2 * degree - 1) * height * newer - (degree + moment - 1) * older)
                    / (degree - moment),
                )
            factor = math.sqrt(
                (2 * degree + 1)
                / (4.0 * math.pi)
                * math.factorial(degree - moment)
                / math.factorial(degree + moment)
            )
            centre = degree * degree + degree
            if moment == 0:
                columns[:, centre] = factor * newer
            else:
                columns[:, centre + moment] = math.sqrt(2.0) * factor * newer * real_part
                columns[:, centre - moment] = math.sqrt(2.0) * factor * newer * imag_part
    return columns


def legendre_pair(order, points):
    older = np.ones(points.shape)
    newer = points * 1.0
    for degree in range(2, order + 1):
        older, newer = (newer, ((2 * degree - 1) * points * newer - (degree - 1) * older) / degree)
    slope = order * (points * newer - older) / (points * points - 1.0)
    return (newer, slope)


def gauss_nodes(order):
    nodes = np.cos(math.pi * (np.arange(order) + 0.75) / (order + 0.5))
    for sweep in range(20):
        value, slope = legendre_pair(order, nodes)
        nodes = nodes - value / slope
    value, slope = legendre_pair(order, nodes)
    return (nodes, 2.0 / ((1.0 - nodes * nodes) * slope * slope))


def tilt_table():
    nodes, node_weights = gauss_nodes(7)
    turns = 16
    azimuth = 2.0 * math.pi * np.arange(turns) / turns
    height = np.repeat(nodes, turns)
    weights = np.repeat(node_weights, turns) * (2.0 * math.pi / turns)
    spread = np.tile(azimuth, nodes.shape[0])
    radius = np.sqrt(np.maximum(1.0 - height * height, 0.0))
    east = radius * np.cos(spread)
    north = radius * np.sin(spread)
    before = harmonics(east, north, height)
    after = harmonics(east, -height, north)
    full = after.T @ (before * weights[:, None])
    table = np.zeros((49, 49))
    for degree in range(7):
        first_row = degree * degree
        last_row = first_row + 2 * degree + 1
        table[first_row:last_row, first_row:last_row] = full[first_row:last_row, first_row:last_row]
    return table


def split_bf16(table):
    high = table.astype(jnp.bfloat16)
    low = (table - high.astype(np.float64)).astype(jnp.bfloat16)
    return high, low


@functools.lru_cache(maxsize=None)
def rotation_tables():
    tilt = tilt_table()
    degrees = np.array([l for l in range(7) for m in range(-l, l + 1)])
    orders = np.array([m for l in range(7) for m in range(-l, l + 1)])
    partner = degrees * degrees + degrees - orders
    signs = -np.sign(orders).astype(np.float64)
    matrix = np.zeros((16, 49, 49))
    for i in range(49):
        moment = abs(orders[i])
        matrix[moment] += np.outer(tilt[i], tilt[i])
        if moment > 0:
            matrix[6 + moment] += signs[i] * np.outer(tilt[i], tilt[partner[i]])
    swapped = matrix[:, :, partner] * (-signs)[None, None, :]
    first = np.zeros((16, FRAMED * 256))
    for place, f in enumerate(packed_rows):
        degree, order = framed_rows[f]
        row = degree * degree + degree + order
        start = 0 if degree <= 4 else 24
        for j in range(degree * degree, (degree + 1) * (degree + 1)):
            for atom in range(4):
                lane = place * 256 + atom * 32 + j - start
                first[:, lane] = matrix[:, row, j]
                first[:, lane + 128] = swapped[:, row, j]
    high, low = split_bf16(first)
    first = np.concatenate([high, low, high], axis=0)
    second = np.zeros((128, 512))
    for column, (lowest, highest, start) in enumerate(((0, 25, 0), (25, 49, 24))):
        for j in range(lowest, highest):
            moment = abs(orders[j])
            for atom in range(4):
                lane = column * 256 + atom * 32 + j - start
                for part in (64, 96):
                    second[part + moment, lane] = 1.0
                    if moment > 0:
                        second[part + 6 + moment, lane + 128] = 1.0
    return first, second.astype(jnp.bfloat16)


LOW_PART = slice(0, 25 * ATOMS)
HIGH_PART = slice(24 * ATOMS, 49 * ATOMS)


def place_tables():
    gather = np.zeros((25 * ATOMS, 256))
    for place in range(25):
        for atom in range(ATOMS):
            gather[place * ATOMS + atom, atom * 32 + place] = 1.0
    return gather.astype(jnp.bfloat16), gather.T.astype(jnp.bfloat16)


def cosine_terms():
    points = 0.125 + 0.125 * np.cos(math.pi * (np.arange(200) + 0.5) / 200)
    fit = np.polynomial.chebyshev.Chebyshev.fit(
        points, np.cos(2.0 * math.pi * np.sqrt(points)), 8, domain=[0.0, 0.25]
    )
    return [float(term) for term in fit.convert(kind=np.polynomial.Polynomial).coef]


def column_of(columns, which):
    return columns[:, which : which + 1]


def dot(left, right):
    return jnp.dot(left, right, preferred_element_type=F32)


def dot_rows(left, right):
    return lax.dot_general(left, right, (((0,), (0,)), ((), ())), preferred_element_type=F32)


def dot_columns(left, right):
    return lax.dot_general(left, right, (((1,), (1,)), ((), ())), preferred_element_type=F32)


def angle_terms(alpha, beta):
    lane = lax.broadcasted_iota(jnp.int32, (1, 128), 1)
    term = lane & 15
    moment = jnp.where(term < 7, term, term - 6).astype(F32)
    shift = jnp.where(term < 7, 0.0, -0.25).astype(F32)
    code = jnp.where(lane < 64, beta, alpha)
    turns = code * (moment * (1.0 / 4096.0)) + shift
    turns = turns - jnp.floor(turns + 0.5)
    square = turns * turns
    terms = cosine_terms()
    value = terms[-1]
    for coefficient in terms[-2::-1]:
        value = value * square + coefficient
    high = value.astype(BF16).astype(F32)
    return jnp.where((lane & 63) < 32, high, value - high).astype(BF16)


def atom_masks(atoms):
    lane = lax.broadcasted_iota(jnp.int32, (1, 128), 1) >> 5
    lane = lane.astype(F32)
    return [jnp.where(atoms == lane + 4.0 * half, 1.0, 0.0).astype(BF16) for half in range(2)]


def coefficient_blocks(refs, spread):
    return [
        dot(spread, jnp.concatenate([ref[part, :] for ref in refs], axis=1)).astype(BF16)
        for part in (LOW_PART, HIGH_PART)
    ]


def atom_rows(gather, low_columns, high_columns):
    low = dot_columns(gather, low_columns.astype(BF16))
    high = dot_columns(gather, high_columns.astype(BF16))
    return jnp.concatenate(
        [low[0:192], low[192:200] + high[0:ATOMS], high[ATOMS:200]], axis=0
    ).astype(BF16)


GROUP = (
    "source_low",
    "source_high",
    "framed_zero",
    "framed_one",
    "framed_two",
    "hidden",
    "upstream",
    "back_low",
    "back_high",
)
Group = collections.namedtuple("Group", ("edges",) + GROUP)


def group_scratch(edges):
    return [
        ((LOW * edges, 256), BF16),
        ((HIGH * edges, 256), BF16),
        ((edges, 7 * C), BF16),
        ((2 * edges, 12 * C), BF16),
        ((2 * edges, 10 * C), BF16),
        ((FRAMED, edges, C), F32),
        ((FRAMED, edges, C), F32),
        ((LOW * edges, C), BF16),
        ((HIGH * edges, C), BF16),
    ]


def of_place(place, edges, low, high):
    if place < LOW:
        return low, slice(place * edges, (place + 1) * edges)
    return high, slice((place - LOW) * edges, (place - LOW + 1) * edges)


def put_grouped(group, f, block, sign):
    if f < 7:
        group.framed_zero[:, f * C : (f + 1) * C] = block
        return
    grouped, size, at = (group.framed_one, 6, f - 7) if f < 19 else (group.framed_two, 5, f - 19)
    minus, at = at // size, at % size
    own = slice(minus * group.edges, (minus + 1) * group.edges)
    other = slice((1 - minus) * group.edges, (2 - minus) * group.edges)
    grouped[own, at * C : (at + 1) * C] = block
    grouped[other, (size + at) * C : (size + at + 1) * C] = (
        block if (sign > 0) == (minus == 1) else -block
    )


def chunks(rows):
    return [(at, min(at + 2, rows)) for at in range(0, rows, 2)]


def convolve(group, w_zero, w_one, w_two, loads):
    loads[0].wait()
    gate = None
    for begin, end in chunks(7):
        value = dot(group.framed_zero[...], w_zero[:, begin * C : end * C])
        if gate is None:
            gate = 1.0 / (1.0 + jnp.exp(-value[:, 0:C]))
        for f in range(begin, end):
            group.hidden[f] = value[:, (f - begin) * C : (f - begin + 1) * C] * gate
    for number, (grouped, weights, size, plus, minus) in enumerate(
        ((group.framed_one, w_one, 6, 7, 13), (group.framed_two, w_two, 5, 19, 24))
    ):
        loads[1 + number].wait()
        for begin, end in chunks(size):
            value = dot(grouped[...], weights[:, begin * C : end * C])
            for f in range(begin, end):
                columns = slice((f - begin) * C, (f - begin + 1) * C)
                group.hidden[plus + f] = value[0 : group.edges, columns] * gate
                group.hidden[minus + f] = value[group.edges :, columns] * gate
    return gate


def back_through_gate(group, gate):
    total = group.upstream[0] * group.hidden[0]
    for f in range(1, FRAMED):
        total = total + group.upstream[f] * group.hidden[f]
    through = total * (0.25 * (1.0 - gate))
    scaled_gate = 0.25 * gate
    for f in range(FRAMED):
        block = group.upstream[f] * scaled_gate
        if f == 0:
            block = block + through
        put_grouped(group, f, block.astype(BF16), 1)


def convolve_back(group, radial, w_zero, w_one, w_two):
    def put_back(f, block):
        rows, at = of_place(packed_rows.index(f), group.edges, group.back_low, group.back_high)
        rows[at, :] = (block * radial).astype(BF16)

    for begin, end in chunks(7):
        value = dot_columns(group.framed_zero[...], w_zero[begin * C : end * C, :])
        for f in range(begin, end):
            put_back(f, value[:, (f - begin) * C : (f - begin + 1) * C])
    for grouped, weights, size, plus, minus in (
        (group.framed_one, w_one, 6, 7, 13),
        (group.framed_two, w_two, 5, 19, 24),
    ):
        for begin, end in chunks(size):
            rows = slice(begin * C, end * C)
            rows_after = slice((size + begin) * C, (size + end) * C)
            value = dot_columns(
                grouped[...], jnp.concatenate([weights[rows, :], weights[rows_after, :]], axis=1)
            )
            for f in range(begin, end):
                columns = slice((f - begin) * C, (f - begin + 1) * C)
                put_back(plus + f, value[0 : group.edges, columns])
                put_back(minus + f, value[group.edges :, columns])


def gradient_columns(group):
    return (
        dot_rows(group.back_low[...], group.source_low[...]),
        dot_rows(group.back_high[...], group.source_high[...]),
    )


def radial_rows(codes, weight_high, weight_low):
    centre = lax.broadcasted_iota(jnp.int32, (1, RADIAL), 1).astype(F32) * 2.0
    distance = (codes - centre) * (22.0 / 1024.0)
    basis = jnp.exp(-0.5 * (distance * distance))
    basis_high = basis.astype(BF16)
    basis_low = (basis - basis_high.astype(F32)).astype(BF16)
    return dot(basis_high, weight_high) + (
        dot(basis_high, weight_low) + dot(basis_low, weight_high)
    )


def wide_masks(atoms):
    masks = [mask.astype(F32) for mask in atom_masks(atoms)]
    return [
        [
            jnp.concatenate([mask[b * CAP : (b + 1) * CAP]] * 2, axis=0).astype(BF16)
            for b in range(BUCKETS)
        ]
        for mask in masks
    ]


def put_pair(pair, rows, masks, low, high):
    for bucket in range(BUCKETS):
        slots = slice(bucket * CAP, (bucket + 1) * CAP)
        joined = jnp.concatenate([rows[0][slots], rows[1][slots]], axis=0).astype(BF16)
        for half in range(2):
            columns = slice(128 * half, 128 * half + 128)
            masked = joined * masks[half][bucket]
            if pair < LOW_PAIRS:
                low[bucket, 16 * pair : 16 * pair + 16, columns] = masked
            else:
                at = 16 * (pair - LOW_PAIRS)
                high[bucket, at : at + 16, columns] = masked


def kernel(domains_x, domains_y, names, *refs):
    refs = collections.namedtuple("Refs", names)(*refs)
    halo = Group(HALO, *(getattr(refs, "halo_" + name) for name in GROUP))
    inner = Group(INNER, *(getattr(refs, "inner_" + name) for name in GROUP))
    place_x = lax.axis_index("gx")
    place_y = lax.axis_index("gy")
    image = lax.axis_index("img")

    def inside(step_x, step_y):
        x = place_x + step_x
        y = place_y + step_y
        return (x >= 0) & (x < domains_x) & (y >= 0) & (y < domains_y)

    def device_at(step_x, step_y):
        return (place_x + step_x, place_y + step_y, image)

    barrier = pltpu.get_barrier_semaphore()
    for step_x, step_y in neighbour_steps:

        @pl.when(inside(step_x, step_y))
        def _(step_x=step_x, step_y=step_y):
            pl.semaphore_signal(
                barrier, inc=1, device_id=device_at(step_x, step_y), device_id_type=MESH
            )

    loads = {}
    for number, name in enumerate(LOADED):
        loads[name] = pltpu.make_async_copy(
            getattr(refs, name + "_hbm"), getattr(refs, name), refs.load_sems.at[number]
        )
        loads[name].start()

    class Once:
        def __init__(self, name):
            self.name = name

        def wait(self):
            if self.name in loads:
                loads.pop(self.name).wait()

    for bucket, (step_x, step_y) in enumerate(neighbour_steps):

        @pl.when(jnp.logical_not(inside(-step_x, -step_y)))
        def _(bucket=bucket):
            refs.codes_in[bucket] = jnp.full((CAP, 128), -1.0, F32)
            refs.hidden_in[bucket] = jnp.zeros((TRAVEL, C), BF16)

        @pl.when(jnp.logical_not(inside(step_x, step_y)))
        def _(bucket=bucket):
            refs.cotangent_in[bucket] = jnp.zeros((ATOMS * 49, C), BF16)

    def exchange(move, bucket, way):
        source, target, send, recv = move
        step_x, step_y = neighbour_steps[bucket]
        return pltpu.make_async_remote_copy(
            src_ref=source if source is refs.cotangent_hbm else source.at[bucket],
            dst_ref=target.at[bucket],
            send_sem=send.at[bucket],
            recv_sem=recv.at[bucket],
            device_id=device_at(way * step_x, way * step_y),
            device_id_type=MESH,
        )

    def each(move, way, buckets, act):
        for bucket in buckets:
            step_x, step_y = neighbour_steps[bucket]

            @pl.when(inside(way * step_x, way * step_y))
            def _(bucket=bucket):
                act(exchange(move, bucket, way))

    def start(move, way, buckets=BUCKET_ORDER):
        each(move, way, buckets, lambda copy: copy.start())

    def await_sent(move, way):
        each(move, way, BUCKET_ORDER, lambda copy: copy.wait_send())

    def await_arrivals(move, way, buckets=BUCKET_ORDER):
        each(move, -way, buckets, lambda copy: copy.wait_recv())

    codes_move = (refs.codes_out, refs.codes_in, refs.codes_send, refs.codes_recv)
    cotangent_move = (
        refs.cotangent_hbm,
        refs.cotangent_in,
        refs.cotangent_send,
        refs.cotangent_recv,
    )
    hidden_move = (refs.hidden_out, refs.hidden_in, refs.hidden_send, refs.hidden_recv)

    beside_x = jnp.where(place_x > 0, 2, 1) + jnp.where(place_x < domains_x - 1, 1, 0)
    beside_y = jnp.where(place_y > 0, 2, 1) + jnp.where(place_y < domains_y - 1, 1, 0)
    pl.semaphore_wait(barrier, beside_x * beside_y - 1)
    start(cotangent_move, -1)

    refs.codes_table[...] = jnp.zeros((128, 128), F32)
    for name in ("inner_edges", "halo_edges", "halo_counts"):
        Once(name).wait()
    counts = refs.halo_counts[...].astype(F32)
    for which in range(5):
        refs.codes_table[which * BUCKETS : (which + 1) * BUCKETS, 0:CAP] = refs.halo_edges[
            which
        ].astype(F32)
        refs.codes_table[40 + which : 41 + which, 0:INNER] = refs.inner_edges[which].astype(F32)
    turned_codes = refs.codes_table[...].T
    inner_codes = [column_of(turned_codes[0:INNER], 40 + which) for which in range(5)]
    lane = lax.broadcasted_iota(jnp.int32, (CAP, 128), 1)
    slot = lax.broadcasted_iota(jnp.int32, (CAP, 1), 0).astype(F32)
    slot_codes = [
        [column_of(turned_codes[0:CAP], which * BUCKETS + bucket) for bucket in range(BUCKETS)]
        for which in range(5)
    ]
    halo_targets = []
    for bucket in range(BUCKETS):
        target = jnp.where(slot < column_of(counts, bucket), slot_codes[1][bucket], -1.0)
        refs.codes_out[bucket] = jnp.where(
            lane == 0, target, jnp.where(lane == 1, slot_codes[2][bucket], slot_codes[3][bucket])
        )
        halo_targets.append(target)
    halo_codes = [jnp.concatenate(columns, axis=0) for columns in slot_codes]

    start(codes_move, 1)

    def spin_factors(terms):
        both = dot(terms, refs.second[...])
        return [
            (both[:, 256 * k : 256 * k + 128], both[:, 256 * k + 128 : 256 * k + 256])
            for k in range(2)
        ]

    def rotation_row(terms, factors, place):
        cosine, sine = factors[0 if place < LOW else 1]
        both = dot(terms, refs.first[:, place * 256 : place * 256 + 256])
        return cosine * both[:, 0:128] + sine * both[:, 128:256]

    def frame(group, codes, radial, put_row, put_rows):
        terms = angle_terms(codes[2], codes[3])
        factors = spin_factors(terms)
        terms = terms[:, 0:48]
        masks = atom_masks(codes[0])
        for pair in range(PAIRS):
            pair_rows = []
            for f in travel_rows[2 * pair : 2 * pair + 2]:
                if f is None:
                    pair_rows.append(jnp.zeros((group.edges, 128), F32))
                    continue
                place = packed_rows.index(f)
                wide = rotation_row(terms, factors, place)
                pair_rows.append(wide)
                row = wide.astype(BF16)
                put_row(place, row)
                masked = jnp.concatenate([row * masks[0], row * masks[1]], axis=1)
                rows, at = of_place(place, group.edges, group.source_low, group.source_high)
                rows[at, :] = masked
                turned = dot(masked, feature_low if place < LOW else feature_high)
                put_grouped(group, f, (turned * radial).astype(BF16), -1)
            put_rows(pair, pair_rows)

    for name in ("first", "second", "features", "spread", "radial"):
        Once(name).wait()
    feature_low, feature_high = coefficient_blocks([refs.features], refs.spread[...])
    weight = refs.radial[...]
    weight_high = weight.astype(BF16)
    weight_low = (weight - weight_high.astype(F32)).astype(BF16)
    halo_radial = radial_rows(halo_codes[4], weight_high, weight_low)
    target_masks = wide_masks(jnp.concatenate(halo_targets, axis=0))
    frame(
        halo,
        halo_codes,
        halo_radial,
        lambda place, row: None,
        lambda pair, rows: put_pair(pair, rows, target_masks, refs.target_low, refs.target_high),
    )
    weights = (refs.w_zero, refs.w_one, refs.w_two)
    weight_loads = [Once(name) for name in ("w_zero", "w_one", "w_two")]
    halo_gate = convolve(halo, *weights, weight_loads)
    for pair in range(PAIRS):
        f, g = travel_rows[2 * pair : 2 * pair + 2]
        for bucket in range(BUCKETS):
            slots = slice(bucket * CAP, (bucket + 1) * CAP)
            upper = halo.hidden[f, slots, :]
            lower = jnp.zeros((CAP, C), F32) if g is None else halo.hidden[g, slots, :]
            refs.hidden_out[bucket, 16 * pair : 16 * pair + 16, :] = jnp.concatenate(
                [upper, lower], axis=0
            ).astype(BF16)

    inner_radial = radial_rows(inner_codes[4], weight_high, weight_low)
    inner_masks = atom_masks(inner_codes[1])

    def put_inner(place, row):
        rows, at = of_place(place, INNER, refs.inner_target_low, refs.inner_target_high)
        rows[at, :] = jnp.concatenate([row * inner_masks[0], row * inner_masks[1]], axis=1)

    frame(inner, inner_codes, inner_radial, put_inner, lambda pair, rows: None)
    inner_gate = convolve(inner, *weights, weight_loads)
    Once("cotangent").wait()
    cot_low, cot_high = coefficient_blocks([refs.cotangent], refs.spread[...])
    for place, f in enumerate(packed_rows):
        rows, at = of_place(place, INNER, refs.inner_target_low, refs.inner_target_high)
        inner.upstream[f] = dot(rows[at, :], cot_low if place < LOW else cot_high)
        rows, at = of_place(place, INNER, refs.inner_hidden_low, refs.inner_hidden_high)
        rows[at, :] = inner.hidden[f].astype(BF16)
    back_through_gate(inner, inner_gate)
    convolve_back(inner, inner_radial, *weights)
    gradient_low, gradient_high = gradient_columns(inner)
    low = dot_rows(refs.inner_hidden_low[...], refs.inner_target_low[...])
    high = dot_rows(refs.inner_hidden_high[...], refs.inner_target_high[...])

    await_sent(cotangent_move, -1)
    start(hidden_move, 1)

    await_arrivals(codes_move, 1)
    arrived = refs.codes_in[...].reshape(HALO, 128)
    in_terms = angle_terms(column_of(arrived, 1), column_of(arrived, 2))
    in_factors = spin_factors(in_terms)
    in_terms = in_terms[:, 0:48]
    in_masks = wide_masks(column_of(arrived, 0))
    for pair in range(PAIRS):
        rows = [
            jnp.zeros((HALO, 128), F32)
            if f is None
            else rotation_row(in_terms, in_factors, packed_rows.index(f))
            for f in travel_rows[2 * pair : 2 * pair + 2]
        ]
        put_pair(pair, rows, in_masks, refs.incoming_low, refs.incoming_high)

    for natural, target in (
        (refs.natural_low, refs.target_low),
        (refs.natural_high, refs.target_high),
    ):
        for bucket in range(BUCKETS):
            natural[bucket] = dot(target[bucket], refs.spread[...]).astype(BF16)

    for couple in range(0, BUCKETS, 2):
        buckets = BUCKET_ORDER[couple : couple + 2]
        await_arrivals(cotangent_move, -1, buckets)
        for bucket in buckets:
            slots = slice(bucket * CAP, (bucket + 1) * CAP)
            turned = (
                dot(refs.natural_low[bucket], refs.cotangent_in[bucket, LOW_PART, :]),
                dot(refs.natural_high[bucket], refs.cotangent_in[bucket, HIGH_PART, :]),
            )
            for pair in range(PAIRS):
                of_set = turned[0 if pair < LOW_PAIRS else 1]
                at = 16 * (pair if pair < LOW_PAIRS else pair - LOW_PAIRS)
                for half, f in enumerate(travel_rows[2 * pair : 2 * pair + 2]):
                    if f is not None:
                        halo.upstream[f, slots, :] = of_set[
                            at + CAP * half : at + CAP * (half + 1)
                        ]
    back_through_gate(halo, halo_gate)
    convolve_back(halo, halo_radial, *weights)
    halo_low, halo_high = gradient_columns(halo)
    Once("gather").wait()
    refs.gradient[...] = atom_rows(
        refs.gather[...], gradient_low + halo_low, gradient_high + halo_high
    )
    gradient_store = pltpu.make_async_copy(
        refs.gradient, refs.result_hbm.at[1], refs.store_sems.at[1]
    )
    gradient_store.start()

    await_arrivals(hidden_move, 1)
    low = low + dot_rows(
        refs.hidden_in[:, 0:LOW_TRAVEL, :].reshape(BUCKETS * LOW_TRAVEL, C),
        refs.incoming_low[...].reshape(BUCKETS * LOW_TRAVEL, 256),
    )
    high = high + dot_rows(
        refs.hidden_in[:, LOW_TRAVEL:TRAVEL, :].reshape(BUCKETS * (TRAVEL - LOW_TRAVEL), C),
        refs.incoming_high[...].reshape(BUCKETS * (TRAVEL - LOW_TRAVEL), 256),
    )
    refs.aggregate[...] = atom_rows(refs.gather[...], 0.25 * low, 0.25 * high)
    aggregate_store = pltpu.make_async_copy(
        refs.aggregate, refs.result_hbm.at[0], refs.store_sems.at[0]
    )
    aggregate_store.start()
    await_sent(codes_move, 1)
    await_sent(hidden_move, 1)
    gradient_store.wait()
    aggregate_store.wait()


LOADED = (
    "inner_edges",
    "halo_edges",
    "halo_counts",
    "first",
    "second",
    "features",
    "spread",
    "radial",
    "w_zero",
    "w_one",
    "w_two",
    "cotangent",
    "gather",
)
BUCKET_ORDER = (1, 6, 3, 4, 0, 2, 5, 7)


def on_device(
    domains_x,
    domains_y,
    features,
    cotangent,
    w_zero,
    w_one,
    w_two,
    radial_weight,
    inner_edges,
    halo_edges,
    halo_counts,
):
    first, second = rotation_tables()
    gather, spread = place_tables()
    arrays = dict(
        inner_edges=inner_edges.transpose(1, 0, 2),
        halo_edges=halo_edges.transpose(0, 2, 1, 3).reshape(5, BUCKETS, CAP),
        halo_counts=halo_counts,
        first=jnp.asarray(first),
        second=jnp.asarray(second),
        features=features.transpose(1, 0, 2).reshape(49 * ATOMS, C),
        spread=jnp.asarray(spread),
        radial=radial_weight,
        w_zero=w_zero,
        w_one=w_one.reshape(12 * C, 6 * C),
        w_two=w_two.reshape(10 * C, 5 * C),
        cotangent=cotangent.transpose(1, 0, 2).reshape(49 * ATOMS, C),
        gather=jnp.asarray(gather),
    )
    scratch = {name: (arrays[name].shape, arrays[name].dtype) for name in LOADED}
    high_travel = TRAVEL - LOW_TRAVEL
    scratch.update(
        codes_table=((128, 128), F32),
        codes_out=((BUCKETS, CAP, 128), F32),
        codes_in=((BUCKETS, CAP, 128), F32),
        inner_target_low=((LOW * INNER, 256), BF16),
        inner_target_high=((HIGH * INNER, 256), BF16),
        inner_hidden_low=((LOW * INNER, C), BF16),
        inner_hidden_high=((HIGH * INNER, C), BF16),
        target_low=((BUCKETS, LOW_TRAVEL, 256), BF16),
        target_high=((BUCKETS, high_travel, 256), BF16),
        natural_low=((BUCKETS, LOW_TRAVEL, 25 * ATOMS), BF16),
        natural_high=((BUCKETS, high_travel, 25 * ATOMS), BF16),
        incoming_low=((BUCKETS, LOW_TRAVEL, 256), BF16),
        incoming_high=((BUCKETS, high_travel, 256), BF16),
        hidden_out=((BUCKETS, TRAVEL, C), BF16),
        hidden_in=((BUCKETS, TRAVEL, C), BF16),
        cotangent_in=((BUCKETS, 49 * ATOMS, C), BF16),
        aggregate=((49 * ATOMS, C), BF16),
        gradient=((49 * ATOMS, C), BF16),
    )
    for prefix, edges in (("halo_", HALO), ("inner_", INNER)):
        for name, shape in zip(GROUP, group_scratch(edges)):
            scratch[prefix + name] = shape
    semaphores = dict(load_sems=len(LOADED), store_sems=2)
    for move in ("codes", "cotangent", "hidden"):
        semaphores[move + "_send"] = BUCKETS
        semaphores[move + "_recv"] = BUCKETS
    names = [name + "_hbm" for name in LOADED] + ["result_hbm"] + list(scratch) + list(semaphores)
    result = pl.pallas_call(
        functools.partial(kernel, domains_x, domains_y, tuple(names)),
        out_shape=jax.ShapeDtypeStruct((2, 49 * ATOMS, C), BF16),
        in_specs=[pl.BlockSpec(memory_space=pltpu.HBM)] * len(LOADED),
        out_specs=pl.BlockSpec(memory_space=pltpu.HBM),
        scratch_shapes=[pltpu.VMEM(shape, dtype) for shape, dtype in scratch.values()]
        + [pltpu.SemaphoreType.DMA((count,)) for count in semaphores.values()],
        compiler_params=pltpu.CompilerParams(
            collective_id=0, has_side_effects=True, vmem_limit_bytes=60 * 1024 * 1024
        ),
        cost_estimate=pl.CostEstimate(
            flops=6 * 10**9, bytes_accessed=8 * 10**6, transcendentals=10**5
        ),
        name="message_layer",
    )(*[arrays[name] for name in LOADED])
    return tuple(rows.reshape(49, ATOMS, C).transpose(1, 0, 2) for rows in (result[0], result[1]))


def solution(mesh):
    return jax.shard_map(
        functools.partial(on_device, mesh.shape["gx"], mesh.shape["gy"]),
        mesh=mesh,
        in_specs=(
            P(("img", "gx", "gy"), None, None),
            P(("img", "gx", "gy"), None, None),
            P(),
            P(),
            P(),
            P(),
            P(("img", "gx", "gy"), None, None),
            P(("img", "gx", "gy"), None, None, None),
            P(("img", "gx", "gy"), None),
        ),
        out_specs=(P(("img", "gx", "gy"), None, None), P(("img", "gx", "gy"), None, None)),
        check_vma=False,
    )
```

```python
import collections
import functools
import math

import jax
import jax.numpy as jnp
import numpy as np
from jax import lax
from jax.experimental import pallas as pl
from jax.experimental.pallas import tpu as pltpu
from jax.sharding import PartitionSpec as P

MESH = pl.DeviceIdType.MESH
F32 = jnp.float32
BF16 = jnp.bfloat16

neighbour_steps = ((-1, -1), (-1, 0), (-1, 1), (0, -1), (0, 1), (1, -1), (1, 0), (1, 1))
BUCKETS = 8
CAP = 8
INNER = 96
HALO = BUCKETS * CAP
EDGES = INNER + HALO
ATOMS = 8
C = 128
RADIAL = 512

framed_rows = [(degree, order) for order in (0, 1, -1, 2, -2) for degree in range(abs(order), 7)]
low_rows = [f for f, (degree, order) in enumerate(framed_rows) if degree <= 4]
high_rows = [f for f, (degree, order) in enumerate(framed_rows) if degree > 4]
packed_rows = low_rows + high_rows
LOW = len(low_rows)
HIGH = len(high_rows)
FRAMED = LOW + HIGH
travel_rows = low_rows + [None] + high_rows
PAIRS = len(travel_rows) // 2
LOW_PAIRS = (LOW + 1) // 2
LOW_TRAVEL = LOW_PAIRS * 16
TRAVEL = PAIRS * 16
group_bounds = ((0, 7), (7, 13), (13, 19), (19, 24), (24, 29))


def harmonics(east, north, height):
    columns = np.zeros((height.shape[0], 49))
    real_part = np.ones(height.shape)
    imag_part = np.zeros(height.shape)
    for moment in range(7):
        if moment > 0:
            real_part, imag_part = (
                real_part * east - imag_part * north,
                real_part * north + imag_part * east,
            )
        older = np.zeros(height.shape)
        newer = (
            (-1.0) ** moment * float(np.prod(np.arange(1, 2 * moment, 2))) * np.ones(height.shape)
        )
        for degree in range(moment, 7):
            if degree > moment:
                older, newer = (
                    newer,
                    ((2 * degree - 1) * height * newer - (degree + moment - 1) * older)
                    / (degree - moment),
                )
            factor = math.sqrt(
                (2 * degree + 1)
                / (4.0 * math.pi)
                * math.factorial(degree - moment)
                / math.factorial(degree + moment)
            )
            centre = degree * degree + degree
            if moment == 0:
                columns[:, centre] = factor * newer
            else:
                columns[:, centre + moment] = math.sqrt(2.0) * factor * newer * real_part
                columns[:, centre - moment] = math.sqrt(2.0) * factor * newer * imag_part
    return columns


def legendre_pair(order, points):
    older = np.ones(points.shape)
    newer = points * 1.0
    for degree in range(2, order + 1):
        older, newer = (newer, ((2 * degree - 1) * points * newer - (degree - 1) * older) / degree)
    slope = order * (points * newer - older) / (points * points - 1.0)
    return (newer, slope)


def gauss_nodes(order):
    nodes = np.cos(math.pi * (np.arange(order) + 0.75) / (order + 0.5))
    for sweep in range(20):
        value, slope = legendre_pair(order, nodes)
        nodes = nodes - value / slope
    value, slope = legendre_pair(order, nodes)
    return (nodes, 2.0 / ((1.0 - nodes * nodes) * slope * slope))


def tilt_table():
    nodes, node_weights = gauss_nodes(7)
    turns = 16
    azimuth = 2.0 * math.pi * np.arange(turns) / turns
    height = np.repeat(nodes, turns)
    weights = np.repeat(node_weights, turns) * (2.0 * math.pi / turns)
    spread = np.tile(azimuth, nodes.shape[0])
    radius = np.sqrt(np.maximum(1.0 - height * height, 0.0))
    east = radius * np.cos(spread)
    north = radius * np.sin(spread)
    before = harmonics(east, north, height)
    after = harmonics(east, -height, north)
    full = after.T @ (before * weights[:, None])
    table = np.zeros((49, 49))
    for degree in range(7):
        first_row = degree * degree
        last_row = first_row + 2 * degree + 1
        table[first_row:last_row, first_row:last_row] = full[first_row:last_row, first_row:last_row]
    return table


def split_bf16(table):
    high = table.astype(jnp.bfloat16)
    low = (table - high.astype(np.float64)).astype(jnp.bfloat16)
    return high, low


@functools.lru_cache(maxsize=None)
def rotation_tables():
    tilt = tilt_table()
    degrees = np.array([l for l in range(7) for m in range(-l, l + 1)])
    orders = np.array([m for l in range(7) for m in range(-l, l + 1)])
    partner = degrees * degrees + degrees - orders
    signs = -np.sign(orders).astype(np.float64)
    matrix = np.zeros((16, 49, 49))
    for i in range(49):
        moment = abs(orders[i])
        matrix[moment] += np.outer(tilt[i], tilt[i])
        if moment > 0:
            matrix[6 + moment] += signs[i] * np.outer(tilt[i], tilt[partner[i]])
    swapped = matrix[:, :, partner] * (-signs)[None, None, :]
    first = np.zeros((16, FRAMED * 256))
    for place, f in enumerate(packed_rows):
        degree, order = framed_rows[f]
        row = degree * degree + degree + order
        start = 0 if degree <= 4 else 24
        for j in range(degree * degree, (degree + 1) * (degree + 1)):
            for atom in range(4):
                lane = place * 256 + atom * 32 + j - start
                first[:, lane] = matrix[:, row, j]
                first[:, lane + 128] = swapped[:, row, j]
    high, low = split_bf16(first)
    first = np.concatenate([high, low, high], axis=0)
    second = np.zeros((128, 512))
    for column, (lowest, highest, start) in enumerate(((0, 25, 0), (25, 49, 24))):
        for j in range(lowest, highest):
            moment = abs(orders[j])
            for atom in range(4):
                lane = column * 256 + atom * 32 + j - start
                for part in (64, 96):
                    second[part + moment, lane] = 1.0
                    if moment > 0:
                        second[part + 6 + moment, lane + 128] = 1.0
    return first, second.astype(jnp.bfloat16)


LOW_PART = slice(0, 25 * ATOMS)
HIGH_PART = slice(24 * ATOMS, 49 * ATOMS)


def place_tables():
    gather = np.zeros((25 * ATOMS, 256))
    for place in range(25):
        for atom in range(ATOMS):
            gather[place * ATOMS + atom, atom * 32 + place] = 1.0
    return gather.astype(jnp.bfloat16), gather.T.astype(jnp.bfloat16)


def cosine_terms():
    points = 0.125 + 0.125 * np.cos(math.pi * (np.arange(200) + 0.5) / 200)
    fit = np.polynomial.chebyshev.Chebyshev.fit(
        points, np.cos(2.0 * math.pi * np.sqrt(points)), 8, domain=[0.0, 0.25]
    )
    return [float(term) for term in fit.convert(kind=np.polynomial.Polynomial).coef]


def column_of(columns, which):
    return columns[:, which : which + 1]


def dot(left, right):
    return jnp.dot(left, right, preferred_element_type=F32)


def dot_rows(left, right):
    return lax.dot_general(left, right, (((0,), (0,)), ((), ())), preferred_element_type=F32)


def dot_columns(left, right):
    return lax.dot_general(left, right, (((1,), (1,)), ((), ())), preferred_element_type=F32)


def angle_terms(alpha, beta):
    lane = lax.broadcasted_iota(jnp.int32, (1, 128), 1)
    term = lane & 15
    moment = jnp.where(term < 7, term, term - 6).astype(F32)
    shift = jnp.where(term < 7, 0.0, -0.25).astype(F32)
    code = jnp.where(lane < 64, beta, alpha)
    turns = code * (moment * (1.0 / 4096.0)) + shift
    turns = turns - jnp.floor(turns + 0.5)
    square = turns * turns
    terms = cosine_terms()
    value = terms[-1]
    for coefficient in terms[-2::-1]:
        value = value * square + coefficient
    high = value.astype(BF16).astype(F32)
    return jnp.where((lane & 63) < 32, high, value - high).astype(BF16)


def atom_masks(atoms):
    lane = lax.broadcasted_iota(jnp.int32, (1, 128), 1) >> 5
    lane = lane.astype(F32)
    return [jnp.where(atoms == lane + 4.0 * half, 1.0, 0.0).astype(BF16) for half in range(2)]


def coefficient_blocks(refs, spread):
    return [
        dot(spread, jnp.concatenate([ref[part, :] for ref in refs], axis=1)).astype(BF16)
        for part in (LOW_PART, HIGH_PART)
    ]


def atom_rows(gather, low_columns, high_columns):
    low = dot_columns(gather, low_columns.astype(BF16))
    high = dot_columns(gather, high_columns.astype(BF16))
    return jnp.concatenate(
        [low[0:192], low[192:200] + high[0:ATOMS], high[ATOMS:200]], axis=0
    ).astype(BF16)


GROUP = (
    "source_low",
    "source_high",
    "framed_zero",
    "framed_one",
    "framed_two",
    "hidden",
    "upstream",
    "back_low",
    "back_high",
)
Group = collections.namedtuple("Group", ("edges",) + GROUP)


def group_scratch(edges):
    return [
        ((LOW * edges, 256), BF16),
        ((HIGH * edges, 256), BF16),
        ((edges, 7 * C), BF16),
        ((2 * edges, 12 * C), BF16),
        ((2 * edges, 10 * C), BF16),
        ((FRAMED, edges, C), F32),
        ((FRAMED, edges, C), F32),
        ((LOW * edges, C), BF16),
        ((HIGH * edges, C), BF16),
    ]


def of_place(place, edges, low, high):
    if place < LOW:
        return low, slice(place * edges, (place + 1) * edges)
    return high, slice((place - LOW) * edges, (place - LOW + 1) * edges)


def put_grouped(group, f, block, sign):
    if f < 7:
        group.framed_zero[:, f * C : (f + 1) * C] = block
        return
    grouped, size, at = (group.framed_one, 6, f - 7) if f < 19 else (group.framed_two, 5, f - 19)
    minus, at = at // size, at % size
    own = slice(minus * group.edges, (minus + 1) * group.edges)
    other = slice((1 - minus) * group.edges, (2 - minus) * group.edges)
    grouped[own, at * C : (at + 1) * C] = block
    grouped[other, (size + at) * C : (size + at + 1) * C] = (
        block if (sign > 0) == (minus == 1) else -block
    )


def chunks(rows):
    return [(at, min(at + 2, rows)) for at in range(0, rows, 2)]


def convolve(group, w_zero, w_one, w_two, loads):
    loads[0].wait()
    gate = None
    for begin, end in chunks(7):
        value = dot(group.framed_zero[...], w_zero[:, begin * C : end * C])
        if gate is None:
            gate = 1.0 / (1.0 + jnp.exp(-value[:, 0:C]))
        for f in range(begin, end):
            group.hidden[f] = value[:, (f - begin) * C : (f - begin + 1) * C] * gate
    for number, (grouped, weights, size, plus, minus) in enumerate(
        ((group.framed_one, w_one, 6, 7, 13), (group.framed_two, w_two, 5, 19, 24))
    ):
        loads[1 + number].wait()
        for begin, end in chunks(size):
            value = dot(grouped[...], weights[:, begin * C : end * C])
            for f in range(begin, end):
                columns = slice((f - begin) * C, (f - begin + 1) * C)
                group.hidden[plus + f] = value[0 : group.edges, columns] * gate
                group.hidden[minus + f] = value[group.edges :, columns] * gate
    return gate


def back_through_gate(group, gate):
    total = group.upstream[0] * group.hidden[0]
    for f in range(1, FRAMED):
        total = total + group.upstream[f] * group.hidden[f]
    through = total * (0.25 * (1.0 - gate))
    scaled_gate = 0.25 * gate
    for f in range(FRAMED):
        block = group.upstream[f] * scaled_gate
        if f == 0:
            block = block + through
        put_grouped(group, f, block.astype(BF16), 1)


def convolve_back(group, radial, w_zero, w_one, w_two):
    def put_back(f, block):
        rows, at = of_place(packed_rows.index(f), group.edges, group.back_low, group.back_high)
        rows[at, :] = (block * radial).astype(BF16)

    for begin, end in chunks(7):
        value = dot(group.framed_zero[...], w_zero[:, begin * C : end * C])
        for f in range(begin, end):
            put_back(f, value[:, (f - begin) * C : (f - begin + 1) * C])
    for grouped, weights, size, plus, minus in (
        (group.framed_one, w_one, 6, 7, 13),
        (group.framed_two, w_two, 5, 19, 24),
    ):
        for begin, end in chunks(size):
            value = dot(grouped[...], weights[:, begin * C : end * C])
            for f in range(begin, end):
                columns = slice((f - begin) * C, (f - begin + 1) * C)
                put_back(plus + f, value[0 : group.edges, columns])
                put_back(minus + f, value[group.edges :, columns])


def gradient_columns(group):
    return (
        dot_rows(group.back_low[...], group.source_low[...]),
        dot_rows(group.back_high[...], group.source_high[...]),
    )


def radial_rows(codes, weight_high, weight_low):
    centre = lax.broadcasted_iota(jnp.int32, (1, RADIAL), 1).astype(F32) * 2.0
    distance = (codes - centre) * (22.0 / 1024.0)
    basis = jnp.exp(-0.5 * (distance * distance))
    basis_high = basis.astype(BF16)
    basis_low = (basis - basis_high.astype(F32)).astype(BF16)
    return dot(basis_high, weight_high) + (
        dot(basis_high, weight_low) + dot(basis_low, weight_high)
    )


def wide_masks(atoms):
    masks = [mask.astype(F32) for mask in atom_masks(atoms)]
    return [
        [
            jnp.concatenate([mask[b * CAP : (b + 1) * CAP]] * 2, axis=0).astype(BF16)
            for b in range(BUCKETS)
        ]
        for mask in masks
    ]


def put_pair(pair, rows, masks, low, high):
    for bucket in range(BUCKETS):
        slots = slice(bucket * CAP, (bucket + 1) * CAP)
        joined = jnp.concatenate([rows[0][slots], rows[1][slots]], axis=0).astype(BF16)
        for half in range(2):
            columns = slice(128 * half, 128 * half + 128)
            masked = joined * masks[half][bucket]
            if pair < LOW_PAIRS:
                low[bucket, 16 * pair : 16 * pair + 16, columns] = masked
            else:
                at = 16 * (pair - LOW_PAIRS)
                high[bucket, at : at + 16, columns] = masked


def kernel(domains_x, domains_y, names, *refs):
    refs = collections.namedtuple("Refs", names)(*refs)
    halo = Group(HALO, *(getattr(refs, "halo_" + name) for name in GROUP))
    inner = Group(INNER, *(getattr(refs, "inner_" + name) for name in GROUP))
    place_x = lax.axis_index("gx")
    place_y = lax.axis_index("gy")
    image = lax.axis_index("img")

    def inside(step_x, step_y):
        x = place_x + step_x
        y = place_y + step_y
        return (x >= 0) & (x < domains_x) & (y >= 0) & (y < domains_y)

    def device_at(step_x, step_y):
        return (place_x + step_x, place_y + step_y, image)

    barrier = pltpu.get_barrier_semaphore()
    for step_x, step_y in neighbour_steps:

        @pl.when(inside(step_x, step_y))
        def _(step_x=step_x, step_y=step_y):
            pl.semaphore_signal(
                barrier, inc=1, device_id=device_at(step_x, step_y), device_id_type=MESH
            )

    loads = {}
    for number, name in enumerate(LOADED):
        loads[name] = pltpu.make_async_copy(
            getattr(refs, name + "_hbm"), getattr(refs, name), refs.load_sems.at[number]
        )
        loads[name].start()

    class Once:
        def __init__(self, name):
            self.name = name

        def wait(self):
            if self.name in loads:
                loads.pop(self.name).wait()

    for bucket, (step_x, step_y) in enumerate(neighbour_steps):

        @pl.when(jnp.logical_not(inside(-step_x, -step_y)))
        def _(bucket=bucket):
            refs.codes_in[bucket] = jnp.full((CAP, 128), -1.0, F32)
            refs.hidden_in[bucket] = jnp.zeros((TRAVEL, C), BF16)

        @pl.when(jnp.logical_not(inside(step_x, step_y)))
        def _(bucket=bucket):
            refs.cotangent_in[bucket] = jnp.zeros((ATOMS * 49, C), BF16)

    def exchange(move, bucket, way):
        source, target, send, recv = move
        step_x, step_y = neighbour_steps[bucket]
        return pltpu.make_async_remote_copy(
            src_ref=source if source is refs.cotangent_hbm else source.at[bucket],
            dst_ref=target.at[bucket],
            send_sem=send.at[bucket],
            recv_sem=recv.at[bucket],
            device_id=device_at(way * step_x, way * step_y),
            device_id_type=MESH,
        )

    def each(move, way, buckets, act):
        for bucket in buckets:
            step_x, step_y = neighbour_steps[bucket]

            @pl.when(inside(way * step_x, way * step_y))
            def _(bucket=bucket):
                act(exchange(move, bucket, way))

    def start(move, way, buckets=BUCKET_ORDER):
        each(move, way, buckets, lambda copy: copy.start())

    def await_sent(move, way, buckets=BUCKET_ORDER):
        each(move, way, buckets, lambda copy: copy.wait_send())

    def await_arrivals(move, way, buckets=BUCKET_ORDER):
        each(move, -way, buckets, lambda copy: copy.wait_recv())

    codes_move = (refs.codes_out, refs.codes_in, refs.codes_send, refs.codes_recv)
    cotangent_move = (
        refs.cotangent_hbm,
        refs.cotangent_in,
        refs.cotangent_send,
        refs.cotangent_recv,
    )
    hidden_move = (refs.hidden_out, refs.hidden_in, refs.hidden_send, refs.hidden_recv)

    beside_x = jnp.where(place_x > 0, 2, 1) + jnp.where(place_x < domains_x - 1, 1, 0)
    beside_y = jnp.where(place_y > 0, 2, 1) + jnp.where(place_y < domains_y - 1, 1, 0)

    refs.codes_table[...] = jnp.zeros((128, 128), F32)
    for name in ("inner_edges", "halo_edges", "halo_counts"):
        Once(name).wait()
    counts = refs.halo_counts[...].astype(F32)
    for which in range(5):
        refs.codes_table[which * BUCKETS : (which + 1) * BUCKETS, 0:CAP] = refs.halo_edges[
            which
        ].astype(F32)
        refs.codes_table[40 + which : 41 + which, 0:INNER] = refs.inner_edges[which].astype(F32)
    turned_codes = refs.codes_table[...].T
    inner_codes = [column_of(turned_codes[0:INNER], 40 + which) for which in range(5)]
    lane = lax.broadcasted_iota(jnp.int32, (CAP, 128), 1)
    slot = lax.broadcasted_iota(jnp.int32, (CAP, 1), 0).astype(F32)
    slot_codes = [
        [column_of(turned_codes[0:CAP], which * BUCKETS + bucket) for bucket in range(BUCKETS)]
        for which in range(5)
    ]
    halo_targets = []
    for bucket in range(BUCKETS):
        target = jnp.where(slot < column_of(counts, bucket), slot_codes[1][bucket], -1.0)
        refs.codes_out[bucket] = jnp.where(
            lane == 0, target, jnp.where(lane == 1, slot_codes[2][bucket], slot_codes[3][bucket])
        )
        halo_targets.append(target)
    halo_codes = [jnp.concatenate(columns, axis=0) for columns in slot_codes]
    pl.semaphore_wait(barrier, beside_x * beside_y - 1)
    start(cotangent_move, -1, BUCKET_ORDER[0:4])
    start(codes_move, 1)
    start(cotangent_move, -1, BUCKET_ORDER[4:8])

    def spin_factors(terms):
        both = dot(terms, refs.second[...])
        return [
            (both[:, 256 * k : 256 * k + 128], both[:, 256 * k + 128 : 256 * k + 256])
            for k in range(2)
        ]

    def rotation_row(terms, factors, place):
        cosine, sine = factors[0 if place < LOW else 1]
        both = dot(terms, refs.first[:, place * 256 : place * 256 + 256])
        return cosine * both[:, 0:128] + sine * both[:, 128:256]

    def frame(group, codes, radial, put_row, put_rows):
        terms = angle_terms(codes[2], codes[3])
        factors = spin_factors(terms)
        terms = terms[:, 0:48]
        masks = atom_masks(codes[0])
        for pair in range(PAIRS):
            pair_rows = []
            for f in travel_rows[2 * pair : 2 * pair + 2]:
                if f is None:
                    pair_rows.append(jnp.zeros((group.edges, 128), F32))
                    continue
                place = packed_rows.index(f)
                wide = rotation_row(terms, factors, place)
                pair_rows.append(wide)
                row = wide.astype(BF16)
                put_row(place, row)
                masked = jnp.concatenate([row * masks[0], row * masks[1]], axis=1)
                rows, at = of_place(place, group.edges, group.source_low, group.source_high)
                rows[at, :] = masked
                turned = dot(masked, feature_low if place < LOW else feature_high)
                put_grouped(group, f, (turned * radial).astype(BF16), -1)
            put_rows(pair, pair_rows)

    for name in ("first", "second", "features", "spread", "radial"):
        Once(name).wait()
    feature_low, feature_high = coefficient_blocks([refs.features], refs.spread[...])
    weight = refs.radial[...]
    weight_high = weight.astype(BF16)
    weight_low = (weight - weight_high.astype(F32)).astype(BF16)
    halo_radial = radial_rows(halo_codes[4], weight_high, weight_low)
    target_masks = wide_masks(jnp.concatenate(halo_targets, axis=0))
    frame(
        halo,
        halo_codes,
        halo_radial,
        lambda place, row: None,
        lambda pair, rows: put_pair(pair, rows, target_masks, refs.target_low, refs.target_high),
    )
    weights = (refs.w_zero, refs.w_one, refs.w_two)
    weight_loads = [Once(name) for name in ("w_zero", "w_one", "w_two")]
    halo_gate = convolve(halo, *weights, weight_loads)
    for pair in range(PAIRS):
        f, g = travel_rows[2 * pair : 2 * pair + 2]
        for bucket in range(BUCKETS):
            slots = slice(bucket * CAP, (bucket + 1) * CAP)
            upper = halo.hidden[f, slots, :]
            lower = jnp.zeros((CAP, C), F32) if g is None else halo.hidden[g, slots, :]
            refs.hidden_out[bucket, 16 * pair : 16 * pair + 16, :] = jnp.concatenate(
                [upper, lower], axis=0
            ).astype(BF16)

    back_weights = (refs.back_zero, refs.back_one, refs.back_two)
    for matrix, turned, size in zip(weights, back_weights, (7 * C, 6 * C, 5 * C)):
        for begin in range(0, matrix.shape[0], size):
            turned[begin : begin + size, :] = matrix[begin : begin + size, :].T

    inner_radial = radial_rows(inner_codes[4], weight_high, weight_low)
    inner_masks = atom_masks(inner_codes[1])

    def put_inner(place, row):
        rows, at = of_place(place, INNER, refs.inner_target_low, refs.inner_target_high)
        rows[at, :] = jnp.concatenate([row * inner_masks[0], row * inner_masks[1]], axis=1)

    frame(inner, inner_codes, inner_radial, put_inner, lambda pair, rows: None)
    inner_gate = convolve(inner, *weights, weight_loads)
    Once("cotangent").wait()
    cot_low, cot_high = coefficient_blocks([refs.cotangent], refs.spread[...])
    for place, f in enumerate(packed_rows):
        rows, at = of_place(place, INNER, refs.inner_target_low, refs.inner_target_high)
        inner.upstream[f] = dot(rows[at, :], cot_low if place < LOW else cot_high)
        rows, at = of_place(place, INNER, refs.inner_hidden_low, refs.inner_hidden_high)
        rows[at, :] = inner.hidden[f].astype(BF16)
    back_through_gate(inner, inner_gate)
    convolve_back(inner, inner_radial, *back_weights)
    gradient_low, gradient_high = gradient_columns(inner)
    low = dot_rows(refs.inner_hidden_low[...], refs.inner_target_low[...])
    high = dot_rows(refs.inner_hidden_high[...], refs.inner_target_high[...])

    await_sent(cotangent_move, -1)
    start(hidden_move, 1)

    for natural, target in (
        (refs.natural_low, refs.target_low),
        (refs.natural_high, refs.target_high),
    ):
        for bucket in range(BUCKETS):
            natural[bucket] = dot(target[bucket], refs.spread[...]).astype(BF16)

    await_arrivals(codes_move, 1)
    arrived = refs.codes_in[...].reshape(HALO, 128)
    in_terms = angle_terms(column_of(arrived, 1), column_of(arrived, 2))
    in_factors = spin_factors(in_terms)
    in_terms = in_terms[:, 0:48]
    in_masks = wide_masks(column_of(arrived, 0))
    for pair in range(PAIRS):
        rows = [
            jnp.zeros((HALO, 128), F32)
            if f is None
            else rotation_row(in_terms, in_factors, packed_rows.index(f))
            for f in travel_rows[2 * pair : 2 * pair + 2]
        ]
        put_pair(pair, rows, in_masks, refs.incoming_low, refs.incoming_high)

    for couple in range(0, BUCKETS, 2):
        buckets = BUCKET_ORDER[couple : couple + 2]
        await_arrivals(cotangent_move, -1, buckets)
        for bucket in buckets:
            slots = slice(bucket * CAP, (bucket + 1) * CAP)
            turned = (
                dot(refs.natural_low[bucket], refs.cotangent_in[bucket, LOW_PART, :]),
                dot(refs.natural_high[bucket], refs.cotangent_in[bucket, HIGH_PART, :]),
            )
            for pair in range(PAIRS):
                of_set = turned[0 if pair < LOW_PAIRS else 1]
                at = 16 * (pair if pair < LOW_PAIRS else pair - LOW_PAIRS)
                for half, f in enumerate(travel_rows[2 * pair : 2 * pair + 2]):
                    if f is not None:
                        halo.upstream[f, slots, :] = of_set[
                            at + CAP * half : at + CAP * (half + 1)
                        ]
    back_through_gate(halo, halo_gate)
    convolve_back(halo, halo_radial, *back_weights)
    halo_low, halo_high = gradient_columns(halo)
    Once("gather").wait()
    refs.gradient[...] = atom_rows(
        refs.gather[...], gradient_low + halo_low, gradient_high + halo_high
    )
    gradient_store = pltpu.make_async_copy(
        refs.gradient, refs.result_hbm.at[1], refs.store_sems.at[1]
    )
    gradient_store.start()

    for begin, end in ((0, 4), (4, BUCKETS)):
        await_arrivals(hidden_move, 1, BUCKET_ORDER[begin:end])
        for bucket in BUCKET_ORDER[begin:end]:
            low = low + dot_rows(refs.hidden_in[bucket, 0:LOW_TRAVEL, :], refs.incoming_low[bucket])
            high = high + dot_rows(
                refs.hidden_in[bucket, LOW_TRAVEL:TRAVEL, :], refs.incoming_high[bucket]
            )
    refs.aggregate[...] = atom_rows(refs.gather[...], 0.25 * low, 0.25 * high)
    aggregate_store = pltpu.make_async_copy(
        refs.aggregate, refs.result_hbm.at[0], refs.store_sems.at[0]
    )
    aggregate_store.start()
    await_sent(codes_move, 1)
    await_sent(hidden_move, 1)
    gradient_store.wait()
    aggregate_store.wait()


LOADED = (
    "inner_edges",
    "halo_edges",
    "halo_counts",
    "first",
    "second",
    "features",
    "spread",
    "radial",
    "w_zero",
    "w_one",
    "w_two",
    "cotangent",
    "gather",
)
BUCKET_ORDER = (0, 2, 5, 7, 1, 6, 3, 4)


def on_device(
    domains_x,
    domains_y,
    features,
    cotangent,
    w_zero,
    w_one,
    w_two,
    radial_weight,
    inner_edges,
    halo_edges,
    halo_counts,
):
    first, second = rotation_tables()
    gather, spread = place_tables()
    arrays = dict(
        inner_edges=inner_edges.transpose(1, 0, 2),
        halo_edges=halo_edges.transpose(0, 2, 1, 3).reshape(5, BUCKETS, CAP),
        halo_counts=halo_counts,
        first=jnp.asarray(first),
        second=jnp.asarray(second),
        features=features.transpose(1, 0, 2).reshape(49 * ATOMS, C),
        spread=jnp.asarray(spread),
        radial=radial_weight,
        w_zero=w_zero,
        w_one=w_one.reshape(12 * C, 6 * C),
        w_two=w_two.reshape(10 * C, 5 * C),
        cotangent=cotangent.transpose(1, 0, 2).reshape(49 * ATOMS, C),
        gather=jnp.asarray(gather),
    )
    scratch = {name: (arrays[name].shape, arrays[name].dtype) for name in LOADED}
    high_travel = TRAVEL - LOW_TRAVEL
    scratch.update(
        back_zero=scratch["w_zero"],
        back_one=scratch["w_one"],
        back_two=scratch["w_two"],
        codes_table=((128, 128), F32),
        codes_out=((BUCKETS, CAP, 128), F32),
        codes_in=((BUCKETS, CAP, 128), F32),
        inner_target_low=((LOW * INNER, 256), BF16),
        inner_target_high=((HIGH * INNER, 256), BF16),
        inner_hidden_low=((LOW * INNER, C), BF16),
        inner_hidden_high=((HIGH * INNER, C), BF16),
        target_low=((BUCKETS, LOW_TRAVEL, 256), BF16),
        target_high=((BUCKETS, high_travel, 256), BF16),
        natural_low=((BUCKETS, LOW_TRAVEL, 25 * ATOMS), BF16),
        natural_high=((BUCKETS, high_travel, 25 * ATOMS), BF16),
        incoming_low=((BUCKETS, LOW_TRAVEL, 256), BF16),
        incoming_high=((BUCKETS, high_travel, 256), BF16),
        hidden_out=((BUCKETS, TRAVEL, C), BF16),
        hidden_in=((BUCKETS, TRAVEL, C), BF16),
        cotangent_in=((BUCKETS, 49 * ATOMS, C), BF16),
        aggregate=((49 * ATOMS, C), BF16),
        gradient=((49 * ATOMS, C), BF16),
    )
    for prefix, edges in (("halo_", HALO), ("inner_", INNER)):
        for name, shape in zip(GROUP, group_scratch(edges)):
            scratch[prefix + name] = shape
    semaphores = dict(load_sems=len(LOADED), store_sems=2)
    for move in ("codes", "cotangent", "hidden"):
        semaphores[move + "_send"] = BUCKETS
        semaphores[move + "_recv"] = BUCKETS
    names = [name + "_hbm" for name in LOADED] + ["result_hbm"] + list(scratch) + list(semaphores)
    result = pl.pallas_call(
        functools.partial(kernel, domains_x, domains_y, tuple(names)),
        out_shape=jax.ShapeDtypeStruct((2, 49 * ATOMS, C), BF16),
        in_specs=[pl.BlockSpec(memory_space=pltpu.HBM)] * len(LOADED),
        out_specs=pl.BlockSpec(memory_space=pltpu.HBM),
        scratch_shapes=[pltpu.VMEM(shape, dtype) for shape, dtype in scratch.values()]
        + [pltpu.SemaphoreType.DMA((count,)) for count in semaphores.values()],
        compiler_params=pltpu.CompilerParams(
            collective_id=0, has_side_effects=True, vmem_limit_bytes=60 * 1024 * 1024
        ),
        cost_estimate=pl.CostEstimate(
            flops=6 * 10**9, bytes_accessed=8 * 10**6, transcendentals=10**5
        ),
        name="message_layer",
    )(*[arrays[name] for name in LOADED])
    return tuple(rows.reshape(49, ATOMS, C).transpose(1, 0, 2) for rows in (result[0], result[1]))


def solution(mesh):
    return jax.shard_map(
        functools.partial(on_device, mesh.shape["gx"], mesh.shape["gy"]),
        mesh=mesh,
        in_specs=(
            P(("img", "gx", "gy"), None, None),
            P(("img", "gx", "gy"), None, None),
            P(),
            P(),
            P(),
            P(),
            P(("img", "gx", "gy"), None, None),
            P(("img", "gx", "gy"), None, None, None),
            P(("img", "gx", "gy"), None),
        ),
        out_specs=(P(("img", "gx", "gy"), None, None), P(("img", "gx", "gy"), None, None)),
        check_vma=False,
    )
```

```python
import collections
import functools
import math

import jax
import jax.numpy as jnp
import numpy as np
from jax import lax
from jax.experimental import pallas as pl
from jax.experimental.pallas import tpu as pltpu
from jax.sharding import PartitionSpec as P

MESH = pl.DeviceIdType.MESH
F32 = jnp.float32
BF16 = jnp.bfloat16

neighbour_steps = ((-1, -1), (-1, 0), (-1, 1), (0, -1), (0, 1), (1, -1), (1, 0), (1, 1))
BUCKETS = 8
CAP = 8
INNER = 96
HALO = BUCKETS * CAP
EDGES = INNER + HALO
ATOMS = 8
C = 128
RADIAL = 512

framed_rows = [(degree, order) for order in (0, 1, -1, 2, -2) for degree in range(abs(order), 7)]
low_rows = [f for f, (degree, order) in enumerate(framed_rows) if degree <= 4]
high_rows = [f for f, (degree, order) in enumerate(framed_rows) if degree > 4]
packed_rows = low_rows + high_rows
LOW = len(low_rows)
HIGH = len(high_rows)
FRAMED = LOW + HIGH
travel_rows = low_rows + [None] + high_rows
PAIRS = len(travel_rows) // 2
LOW_PAIRS = (LOW + 1) // 2
LOW_TRAVEL = LOW_PAIRS * 16
TRAVEL = PAIRS * 16
group_bounds = ((0, 7), (7, 13), (13, 19), (19, 24), (24, 29))


def harmonics(east, north, height):
    columns = np.zeros((height.shape[0], 49))
    real_part = np.ones(height.shape)
    imag_part = np.zeros(height.shape)
    for moment in range(7):
        if moment > 0:
            real_part, imag_part = (
                real_part * east - imag_part * north,
                real_part * north + imag_part * east,
            )
        older = np.zeros(height.shape)
        newer = (
            (-1.0) ** moment * float(np.prod(np.arange(1, 2 * moment, 2))) * np.ones(height.shape)
        )
        for degree in range(moment, 7):
            if degree > moment:
                older, newer = (
                    newer,
                    ((2 * degree - 1) * height * newer - (degree + moment - 1) * older)
                    / (degree - moment),
                )
            factor = math.sqrt(
                (2 * degree + 1)
                / (4.0 * math.pi)
                * math.factorial(degree - moment)
                / math.factorial(degree + moment)
            )
            centre = degree * degree + degree
            if moment == 0:
                columns[:, centre] = factor * newer
            else:
                columns[:, centre + moment] = math.sqrt(2.0) * factor * newer * real_part
                columns[:, centre - moment] = math.sqrt(2.0) * factor * newer * imag_part
    return columns


def legendre_pair(order, points):
    older = np.ones(points.shape)
    newer = points * 1.0
    for degree in range(2, order + 1):
        older, newer = (newer, ((2 * degree - 1) * points * newer - (degree - 1) * older) / degree)
    slope = order * (points * newer - older) / (points * points - 1.0)
    return (newer, slope)


def gauss_nodes(order):
    nodes = np.cos(math.pi * (np.arange(order) + 0.75) / (order + 0.5))
    for sweep in range(20):
        value, slope = legendre_pair(order, nodes)
        nodes = nodes - value / slope
    value, slope = legendre_pair(order, nodes)
    return (nodes, 2.0 / ((1.0 - nodes * nodes) * slope * slope))


def tilt_table():
    nodes, node_weights = gauss_nodes(7)
    turns = 16
    azimuth = 2.0 * math.pi * np.arange(turns) / turns
    height = np.repeat(nodes, turns)
    weights = np.repeat(node_weights, turns) * (2.0 * math.pi / turns)
    spread = np.tile(azimuth, nodes.shape[0])
    radius = np.sqrt(np.maximum(1.0 - height * height, 0.0))
    east = radius * np.cos(spread)
    north = radius * np.sin(spread)
    before = harmonics(east, north, height)
    after = harmonics(east, -height, north)
    full = after.T @ (before * weights[:, None])
    table = np.zeros((49, 49))
    for degree in range(7):
        first_row = degree * degree
        last_row = first_row + 2 * degree + 1
        table[first_row:last_row, first_row:last_row] = full[first_row:last_row, first_row:last_row]
    return table


def split_bf16(table):
    high = table.astype(jnp.bfloat16)
    low = (table - high.astype(np.float64)).astype(jnp.bfloat16)
    return high, low


@functools.lru_cache(maxsize=None)
def rotation_tables():
    tilt = tilt_table()
    degrees = np.array([l for l in range(7) for m in range(-l, l + 1)])
    orders = np.array([m for l in range(7) for m in range(-l, l + 1)])
    partner = degrees * degrees + degrees - orders
    signs = -np.sign(orders).astype(np.float64)
    matrix = np.zeros((16, 49, 49))
    for i in range(49):
        moment = abs(orders[i])
        matrix[moment] += np.outer(tilt[i], tilt[i])
        if moment > 0:
            matrix[6 + moment] += signs[i] * np.outer(tilt[i], tilt[partner[i]])
    swapped = matrix[:, :, partner] * (-signs)[None, None, :]
    first = np.zeros((16, FRAMED * 256))
    for place, f in enumerate(packed_rows):
        degree, order = framed_rows[f]
        row = degree * degree + degree + order
        start = 0 if degree <= 4 else 24
        for j in range(degree * degree, (degree + 1) * (degree + 1)):
            for atom in range(4):
                lane = place * 256 + atom * 32 + j - start
                first[:, lane] = matrix[:, row, j]
                first[:, lane + 128] = swapped[:, row, j]
    high, low = split_bf16(first)
    first = np.concatenate([high, low, high], axis=0)
    second = np.zeros((128, 512))
    for column, (lowest, highest, start) in enumerate(((0, 25, 0), (25, 49, 24))):
        for j in range(lowest, highest):
            moment = abs(orders[j])
            for atom in range(4):
                lane = column * 256 + atom * 32 + j - start
                for part in (64, 96):
                    second[part + moment, lane] = 1.0
                    if moment > 0:
                        second[part + 6 + moment, lane + 128] = 1.0
    return first, second.astype(jnp.bfloat16)


LOW_PART = slice(0, 25 * ATOMS)
HIGH_PART = slice(24 * ATOMS, 49 * ATOMS)


def place_tables():
    gather = np.zeros((25 * ATOMS, 256))
    for place in range(25):
        for atom in range(ATOMS):
            gather[place * ATOMS + atom, atom * 32 + place] = 1.0
    return gather.astype(jnp.bfloat16), gather.T.astype(jnp.bfloat16)


def cosine_terms():
    points = 0.125 + 0.125 * np.cos(math.pi * (np.arange(200) + 0.5) / 200)
    fit = np.polynomial.chebyshev.Chebyshev.fit(
        points, np.cos(2.0 * math.pi * np.sqrt(points)), 8, domain=[0.0, 0.25]
    )
    return [float(term) for term in fit.convert(kind=np.polynomial.Polynomial).coef]


def column_of(columns, which):
    return columns[:, which : which + 1]


def dot(left, right):
    return jnp.dot(left, right, preferred_element_type=F32)


def dot_rows(left, right):
    return lax.dot_general(left, right, (((0,), (0,)), ((), ())), preferred_element_type=F32)


def dot_columns(left, right):
    return lax.dot_general(left, right, (((1,), (1,)), ((), ())), preferred_element_type=F32)


def angle_terms(alpha, beta):
    lane = lax.broadcasted_iota(jnp.int32, (1, 128), 1)
    term = lane & 15
    moment = jnp.where(term < 7, term, term - 6).astype(F32)
    shift = jnp.where(term < 7, 0.0, -0.25).astype(F32)
    code = jnp.where(lane < 64, beta, alpha)
    turns = code * (moment * (1.0 / 4096.0)) + shift
    turns = turns - jnp.floor(turns + 0.5)
    square = turns * turns
    terms = cosine_terms()
    value = terms[-1]
    for coefficient in terms[-2::-1]:
        value = value * square + coefficient
    high = value.astype(BF16).astype(F32)
    return jnp.where((lane & 63) < 32, high, value - high).astype(BF16)


def atom_masks(atoms):
    lane = lax.broadcasted_iota(jnp.int32, (1, 128), 1) >> 5
    lane = lane.astype(F32)
    return [jnp.where(atoms == lane + 4.0 * half, 1.0, 0.0).astype(BF16) for half in range(2)]


def coefficient_blocks(refs, spread):
    return [
        dot(spread, jnp.concatenate([ref[part, :] for ref in refs], axis=1)).astype(BF16)
        for part in (LOW_PART, HIGH_PART)
    ]


def place_rows(gather, columns):
    high = columns.astype(BF16)
    low = (columns - high.astype(F32)).astype(BF16)
    return dot_columns(gather, high) + dot_columns(gather, low)


def join_sets(low, high):
    return jnp.concatenate(
        [low[0:192], low[192:200] + high[0:ATOMS], high[ATOMS:200]], axis=0
    ).astype(BF16)


GROUP = (
    "source_low",
    "source_high",
    "framed_zero",
    "framed_one",
    "framed_two",
    "hidden",
    "upstream",
    "back_low",
    "back_high",
)
Group = collections.namedtuple("Group", ("edges",) + GROUP)


def group_scratch(edges):
    return [
        ((LOW * edges, 256), BF16),
        ((HIGH * edges, 256), BF16),
        ((edges, 7 * C), BF16),
        ((2 * edges, 12 * C), BF16),
        ((2 * edges, 10 * C), BF16),
        ((FRAMED, edges, C), F32),
        ((FRAMED, edges, C), F32),
        ((LOW * edges, C), BF16),
        ((HIGH * edges, C), BF16),
    ]


def of_place(place, edges, low, high):
    if place < LOW:
        return low, slice(place * edges, (place + 1) * edges)
    return high, slice((place - LOW) * edges, (place - LOW + 1) * edges)


def put_grouped(group, f, block, sign):
    if f < 7:
        group.framed_zero[:, f * C : (f + 1) * C] = block
        return
    grouped, size, at = (group.framed_one, 6, f - 7) if f < 19 else (group.framed_two, 5, f - 19)
    minus, at = at // size, at % size
    own = slice(minus * group.edges, (minus + 1) * group.edges)
    other = slice((1 - minus) * group.edges, (2 - minus) * group.edges)
    grouped[own, at * C : (at + 1) * C] = block
    grouped[other, (size + at) * C : (size + at + 1) * C] = (
        block if (sign > 0) == (minus == 1) else -block
    )


def chunks(rows):
    return [(at, min(at + 2, rows)) for at in range(0, rows, 2)]


def convolve(group, w_zero, w_one, w_two, loads):
    loads[0].wait()
    gate = None
    for begin, end in chunks(7):
        value = dot(group.framed_zero[...], w_zero[:, begin * C : end * C])
        if gate is None:
            gate = 1.0 / (1.0 + jnp.exp(-value[:, 0:C]))
        for f in range(begin, end):
            group.hidden[f] = value[:, (f - begin) * C : (f - begin + 1) * C] * gate
    for number, (grouped, weights, size, plus, minus) in enumerate(
        ((group.framed_one, w_one, 6, 7, 13), (group.framed_two, w_two, 5, 19, 24))
    ):
        loads[1 + number].wait()
        for begin, end in chunks(size):
            value = dot(grouped[...], weights[:, begin * C : end * C])
            for f in range(begin, end):
                columns = slice((f - begin) * C, (f - begin + 1) * C)
                group.hidden[plus + f] = value[0 : group.edges, columns] * gate
                group.hidden[minus + f] = value[group.edges :, columns] * gate
    return gate


def back_through_gate(group, gate):
    total = group.upstream[0] * group.hidden[0]
    for f in range(1, FRAMED):
        total = total + group.upstream[f] * group.hidden[f]
    through = total * (0.25 * (1.0 - gate))
    scaled_gate = 0.25 * gate
    for f in range(FRAMED):
        block = group.upstream[f] * scaled_gate
        if f == 0:
            block = block + through
        put_grouped(group, f, block.astype(BF16), 1)


def convolve_back(group, radial, w_zero, w_one, w_two):
    def put_back(f, block):
        rows, at = of_place(packed_rows.index(f), group.edges, group.back_low, group.back_high)
        rows[at, :] = (block * radial).astype(BF16)

    for begin, end in chunks(7):
        value = dot(group.framed_zero[...], w_zero[:, begin * C : end * C])
        for f in range(begin, end):
            put_back(f, value[:, (f - begin) * C : (f - begin + 1) * C])
    for grouped, weights, size, plus, minus in (
        (group.framed_one, w_one, 6, 7, 13),
        (group.framed_two, w_two, 5, 19, 24),
    ):
        for begin, end in chunks(size):
            value = dot(grouped[...], weights[:, begin * C : end * C])
            for f in range(begin, end):
                columns = slice((f - begin) * C, (f - begin + 1) * C)
                put_back(plus + f, value[0 : group.edges, columns])
                put_back(minus + f, value[group.edges :, columns])


def gradient_columns(group):
    return (
        dot_rows(group.back_low[...], group.source_low[...]),
        dot_rows(group.back_high[...], group.source_high[...]),
    )


def radial_rows(codes, weight_high, weight_low):
    centre = lax.broadcasted_iota(jnp.int32, (1, RADIAL), 1).astype(F32) * 2.0
    distance = (codes - centre) * (22.0 / 1024.0)
    basis = jnp.exp(-0.5 * (distance * distance))
    basis_high = basis.astype(BF16)
    basis_low = (basis - basis_high.astype(F32)).astype(BF16)
    return dot(basis_high, weight_high) + (
        dot(basis_high, weight_low) + dot(basis_low, weight_high)
    )


def wide_masks(atoms):
    masks = [mask.astype(F32) for mask in atom_masks(atoms)]
    return [
        [
            jnp.concatenate([mask[b * CAP : (b + 1) * CAP]] * 2, axis=0).astype(BF16)
            for b in range(BUCKETS)
        ]
        for mask in masks
    ]


def put_pair(pair, rows, masks, low, high):
    for bucket in range(BUCKETS):
        slots = slice(bucket * CAP, (bucket + 1) * CAP)
        joined = jnp.concatenate([rows[0][slots], rows[1][slots]], axis=0).astype(BF16)
        for half in range(2):
            columns = slice(128 * half, 128 * half + 128)
            masked = joined * masks[half][bucket]
            if pair < LOW_PAIRS:
                low[bucket, 16 * pair : 16 * pair + 16, columns] = masked
            else:
                at = 16 * (pair - LOW_PAIRS)
                high[bucket, at : at + 16, columns] = masked


def kernel(domains_x, domains_y, names, *refs):
    refs = collections.namedtuple("Refs", names)(*refs)
    halo = Group(HALO, *(getattr(refs, "halo_" + name) for name in GROUP))
    inner = Group(INNER, *(getattr(refs, "inner_" + name) for name in GROUP))
    place_x = lax.axis_index("gx")
    place_y = lax.axis_index("gy")
    image = lax.axis_index("img")

    def inside(step_x, step_y):
        x = place_x + step_x
        y = place_y + step_y
        return (x >= 0) & (x < domains_x) & (y >= 0) & (y < domains_y)

    def device_at(step_x, step_y):
        return (place_x + step_x, place_y + step_y, image)

    barrier = pltpu.get_barrier_semaphore()
    for step_x, step_y in reversed(neighbour_steps):

        @pl.when(inside(step_x, step_y))
        def _(step_x=step_x, step_y=step_y):
            pl.semaphore_signal(
                barrier, inc=1, device_id=device_at(step_x, step_y), device_id_type=MESH
            )

    loads = {}
    for number, name in enumerate(LOADED):
        loads[name] = pltpu.make_async_copy(
            getattr(refs, name + "_hbm"), getattr(refs, name), refs.load_sems.at[number]
        )
        loads[name].start()

    class Once:
        def __init__(self, name):
            self.name = name

        def wait(self):
            if self.name in loads:
                loads.pop(self.name).wait()

    for bucket, (step_x, step_y) in enumerate(neighbour_steps):

        @pl.when(jnp.logical_not(inside(-step_x, -step_y)))
        def _(bucket=bucket):
            refs.codes_in[bucket] = jnp.full((CAP, 128), -1.0, F32)
            refs.hidden_in[bucket] = jnp.zeros((TRAVEL, C), BF16)

        @pl.when(jnp.logical_not(inside(step_x, step_y)))
        def _(bucket=bucket):
            refs.cotangent_in[bucket] = jnp.zeros((ATOMS * 49, C), BF16)

    def exchange(move, bucket, way):
        source, target, send, recv = move
        step_x, step_y = neighbour_steps[bucket]
        return pltpu.make_async_remote_copy(
            src_ref=source if source is refs.cotangent_hbm else source.at[bucket],
            dst_ref=target.at[bucket],
            send_sem=send.at[bucket],
            recv_sem=recv.at[bucket],
            device_id=device_at(way * step_x, way * step_y),
            device_id_type=MESH,
        )

    def each(move, way, buckets, act):
        for bucket in buckets:
            step_x, step_y = neighbour_steps[bucket]

            @pl.when(inside(way * step_x, way * step_y))
            def _(bucket=bucket):
                act(exchange(move, bucket, way))

    def start(move, way, buckets=BUCKET_ORDER):
        each(move, way, buckets, lambda copy: copy.start())

    def await_sent(move, way, buckets=BUCKET_ORDER):
        each(move, way, buckets, lambda copy: copy.wait_send())

    def await_arrivals(move, way, buckets=BUCKET_ORDER):
        each(move, -way, buckets, lambda copy: copy.wait_recv())

    codes_move = (refs.codes_out, refs.codes_in, refs.codes_send, refs.codes_recv)
    cotangent_move = (
        refs.cotangent_hbm,
        refs.cotangent_in,
        refs.cotangent_send,
        refs.cotangent_recv,
    )
    hidden_move = (refs.hidden_out, refs.hidden_in, refs.hidden_send, refs.hidden_recv)

    beside_x = jnp.where(place_x > 0, 2, 1) + jnp.where(place_x < domains_x - 1, 1, 0)
    beside_y = jnp.where(place_y > 0, 2, 1) + jnp.where(place_y < domains_y - 1, 1, 0)

    refs.codes_table[...] = jnp.zeros((128, 128), F32)
    for name in ("inner_edges", "halo_edges", "halo_counts"):
        Once(name).wait()
    counts = refs.halo_counts[...].astype(F32)
    for which in range(5):
        refs.codes_table[which * BUCKETS : (which + 1) * BUCKETS, 0:CAP] = refs.halo_edges[
            which
        ].astype(F32)
        refs.codes_table[40 + which : 41 + which, 0:INNER] = refs.inner_edges[which].astype(F32)
    turned_codes = refs.codes_table[...].T
    inner_codes = [column_of(turned_codes[0:INNER], 40 + which) for which in range(5)]
    lane = lax.broadcasted_iota(jnp.int32, (CAP, 128), 1)
    slot = lax.broadcasted_iota(jnp.int32, (CAP, 1), 0).astype(F32)
    slot_codes = [
        [column_of(turned_codes[0:CAP], which * BUCKETS + bucket) for bucket in range(BUCKETS)]
        for which in range(5)
    ]
    halo_targets = []
    for bucket in range(BUCKETS):
        target = jnp.where(slot < column_of(counts, bucket), slot_codes[1][bucket], -1.0)
        refs.codes_out[bucket] = jnp.where(
            lane == 0, target, jnp.where(lane == 1, slot_codes[2][bucket], slot_codes[3][bucket])
        )
        halo_targets.append(target)
    halo_codes = [jnp.concatenate(columns, axis=0) for columns in slot_codes]
    pl.semaphore_wait(barrier, beside_x * beside_y - 1)
    start(cotangent_move, -1, BUCKET_ORDER[0:4])
    start(codes_move, 1)
    start(cotangent_move, -1, BUCKET_ORDER[4:8])

    def spin_factors(terms):
        both = dot(terms, refs.second[...])
        return [
            (both[:, 256 * k : 256 * k + 128], both[:, 256 * k + 128 : 256 * k + 256])
            for k in range(2)
        ]

    def rotation_row(terms, factors, place):
        cosine, sine = factors[0 if place < LOW else 1]
        both = dot(terms, refs.first[:, place * 256 : place * 256 + 256])
        return cosine * both[:, 0:128] + sine * both[:, 128:256]

    def frame(group, codes, radial, put_row, put_rows):
        terms = angle_terms(codes[2], codes[3])
        factors = spin_factors(terms)
        terms = terms[:, 0:48]
        masks = atom_masks(codes[0])
        for pair in range(PAIRS):
            pair_rows = []
            for f in travel_rows[2 * pair : 2 * pair + 2]:
                if f is None:
                    pair_rows.append(jnp.zeros((group.edges, 128), F32))
                    continue
                place = packed_rows.index(f)
                wide = rotation_row(terms, factors, place)
                pair_rows.append(wide)
                row = wide.astype(BF16)
                put_row(place, row)
                masked = jnp.concatenate([row * masks[0], row * masks[1]], axis=1)
                rows, at = of_place(place, group.edges, group.source_low, group.source_high)
                rows[at, :] = masked
                turned = dot(masked, feature_low if place < LOW else feature_high)
                put_grouped(group, f, (turned * radial).astype(BF16), -1)
            put_rows(pair, pair_rows)

    for name in ("first", "second", "features", "spread", "radial"):
        Once(name).wait()
    feature_low, feature_high = coefficient_blocks([refs.features], refs.spread[...])
    weight = refs.radial[...]
    weight_high = weight.astype(BF16)
    weight_low = (weight - weight_high.astype(F32)).astype(BF16)
    halo_radial = radial_rows(halo_codes[4], weight_high, weight_low)
    target_masks = wide_masks(jnp.concatenate(halo_targets, axis=0))
    frame(
        halo,
        halo_codes,
        halo_radial,
        lambda place, row: None,
        lambda pair, rows: put_pair(pair, rows, target_masks, refs.target_low, refs.target_high),
    )
    weights = (refs.w_zero, refs.w_one, refs.w_two)
    weight_loads = [Once(name) for name in ("w_zero", "w_one", "w_two")]
    halo_gate = convolve(halo, *weights, weight_loads)
    for pair in range(PAIRS):
        f, g = travel_rows[2 * pair : 2 * pair + 2]
        for bucket in range(BUCKETS):
            slots = slice(bucket * CAP, (bucket + 1) * CAP)
            upper = halo.hidden[f, slots, :]
            lower = jnp.zeros((CAP, C), F32) if g is None else halo.hidden[g, slots, :]
            refs.hidden_out[bucket, 16 * pair : 16 * pair + 16, :] = jnp.concatenate(
                [upper, lower], axis=0
            ).astype(BF16)

    back_weights = (refs.back_zero, refs.back_one, refs.back_two)
    for matrix, turned, size in zip(weights, back_weights, (7 * C, 6 * C, 5 * C)):
        for begin in range(0, matrix.shape[0], size):
            turned[begin : begin + size, :] = matrix[begin : begin + size, :].T

    inner_radial = radial_rows(inner_codes[4], weight_high, weight_low)
    inner_masks = atom_masks(inner_codes[1])

    def put_inner(place, row):
        rows, at = of_place(place, INNER, refs.inner_target_low, refs.inner_target_high)
        rows[at, :] = jnp.concatenate([row * inner_masks[0], row * inner_masks[1]], axis=1)

    frame(inner, inner_codes, inner_radial, put_inner, lambda pair, rows: None)
    inner_gate = convolve(inner, *weights, weight_loads)
    Once("cotangent").wait()
    cot_low, cot_high = coefficient_blocks([refs.cotangent], refs.spread[...])
    for place, f in enumerate(packed_rows):
        rows, at = of_place(place, INNER, refs.inner_target_low, refs.inner_target_high)
        inner.upstream[f] = dot(rows[at, :], cot_low if place < LOW else cot_high)
        rows, at = of_place(place, INNER, refs.inner_hidden_low, refs.inner_hidden_high)
        rows[at, :] = inner.hidden[f].astype(BF16)
    back_through_gate(inner, inner_gate)
    convolve_back(inner, inner_radial, *back_weights)
    gradient_low, gradient_high = gradient_columns(inner)
    low = dot_rows(refs.inner_hidden_low[...], refs.inner_target_low[...])
    high = dot_rows(refs.inner_hidden_high[...], refs.inner_target_high[...])

    await_sent(cotangent_move, -1)
    start(hidden_move, 1)

    for natural, target in (
        (refs.natural_low, refs.target_low),
        (refs.natural_high, refs.target_high),
    ):
        for bucket in range(BUCKETS):
            natural[bucket] = dot(target[bucket], refs.spread[...]).astype(BF16)

    Once("gather").wait()

    await_arrivals(codes_move, 1)
    arrived = refs.codes_in[...].reshape(HALO, 128)
    in_terms = angle_terms(column_of(arrived, 1), column_of(arrived, 2))
    in_factors = spin_factors(in_terms)
    in_terms = in_terms[:, 0:48]
    in_masks = wide_masks(column_of(arrived, 0))
    for pair in range(PAIRS):
        rows = [
            jnp.zeros((HALO, 128), F32)
            if f is None
            else rotation_row(in_terms, in_factors, packed_rows.index(f))
            for f in travel_rows[2 * pair : 2 * pair + 2]
        ]
        put_pair(pair, rows, in_masks, refs.incoming_low, refs.incoming_high)

    for bucket in range(BUCKETS):
        refs.turned_low[bucket] = dot_columns(refs.gather[...], refs.incoming_low[bucket]).astype(
            BF16
        )
        refs.turned_high[bucket] = dot_columns(
            refs.gather[...], refs.incoming_high[bucket]
        ).astype(BF16)
    low = place_rows(refs.gather[...], low)
    high = place_rows(refs.gather[...], high)

    for couple in range(0, BUCKETS, 2):
        buckets = BUCKET_ORDER[couple : couple + 2]
        await_arrivals(cotangent_move, -1, buckets)
        for bucket in buckets:
            slots = slice(bucket * CAP, (bucket + 1) * CAP)
            turned = (
                dot(refs.natural_low[bucket], refs.cotangent_in[bucket, LOW_PART, :]),
                dot(refs.natural_high[bucket], refs.cotangent_in[bucket, HIGH_PART, :]),
            )
            for pair in range(PAIRS):
                of_set = turned[0 if pair < LOW_PAIRS else 1]
                at = 16 * (pair if pair < LOW_PAIRS else pair - LOW_PAIRS)
                for half, f in enumerate(travel_rows[2 * pair : 2 * pair + 2]):
                    if f is not None:
                        halo.upstream[f, slots, :] = of_set[
                            at + CAP * half : at + CAP * (half + 1)
                        ]
    back_through_gate(halo, halo_gate)
    convolve_back(halo, halo_radial, *back_weights)
    halo_low, halo_high = gradient_columns(halo)
    refs.gradient[...] = join_sets(
        place_rows(refs.gather[...], gradient_low + halo_low),
        place_rows(refs.gather[...], gradient_high + halo_high),
    )
    gradient_store = pltpu.make_async_copy(
        refs.gradient, refs.result_hbm.at[1], refs.store_sems.at[1]
    )
    gradient_store.start()

    for begin, end in ((0, 4), (4, BUCKETS)):
        await_arrivals(hidden_move, 1, BUCKET_ORDER[begin:end])
        for bucket in BUCKET_ORDER[begin:end]:
            low = low + dot(refs.turned_low[bucket], refs.hidden_in[bucket, 0:LOW_TRAVEL, :])
            high = high + dot(
                refs.turned_high[bucket], refs.hidden_in[bucket, LOW_TRAVEL:TRAVEL, :]
            )
    refs.aggregate[...] = join_sets(0.25 * low, 0.25 * high)
    aggregate_store = pltpu.make_async_copy(
        refs.aggregate, refs.result_hbm.at[0], refs.store_sems.at[0]
    )
    aggregate_store.start()
    await_sent(codes_move, 1)
    await_sent(hidden_move, 1)
    gradient_store.wait()
    aggregate_store.wait()


LOADED = (
    "inner_edges",
    "halo_edges",
    "halo_counts",
    "first",
    "second",
    "features",
    "spread",
    "radial",
    "w_zero",
    "w_one",
    "w_two",
    "cotangent",
    "gather",
)
BUCKET_ORDER = (0, 2, 5, 7, 1, 6, 3, 4)


def on_device(
    domains_x,
    domains_y,
    features,
    cotangent,
    w_zero,
    w_one,
    w_two,
    radial_weight,
    inner_edges,
    halo_edges,
    halo_counts,
):
    first, second = rotation_tables()
    gather, spread = place_tables()
    arrays = dict(
        inner_edges=inner_edges.transpose(1, 0, 2),
        halo_edges=halo_edges.transpose(0, 2, 1, 3).reshape(5, BUCKETS, CAP),
        halo_counts=halo_counts,
        first=jnp.asarray(first),
        second=jnp.asarray(second),
        features=features.transpose(1, 0, 2).reshape(49 * ATOMS, C),
        spread=jnp.asarray(spread),
        radial=radial_weight,
        w_zero=w_zero,
        w_one=w_one.reshape(12 * C, 6 * C),
        w_two=w_two.reshape(10 * C, 5 * C),
        cotangent=cotangent.transpose(1, 0, 2).reshape(49 * ATOMS, C),
        gather=jnp.asarray(gather),
    )
    scratch = {name: (arrays[name].shape, arrays[name].dtype) for name in LOADED}
    high_travel = TRAVEL - LOW_TRAVEL
    scratch.update(
        back_zero=scratch["w_zero"],
        back_one=scratch["w_one"],
        back_two=scratch["w_two"],
        codes_table=((128, 128), F32),
        codes_out=((BUCKETS, CAP, 128), F32),
        codes_in=((BUCKETS, CAP, 128), F32),
        inner_target_low=((LOW * INNER, 256), BF16),
        inner_target_high=((HIGH * INNER, 256), BF16),
        inner_hidden_low=((LOW * INNER, C), BF16),
        inner_hidden_high=((HIGH * INNER, C), BF16),
        target_low=((BUCKETS, LOW_TRAVEL, 256), BF16),
        target_high=((BUCKETS, high_travel, 256), BF16),
        natural_low=((BUCKETS, LOW_TRAVEL, 25 * ATOMS), BF16),
        natural_high=((BUCKETS, high_travel, 25 * ATOMS), BF16),
        incoming_low=((BUCKETS, LOW_TRAVEL, 256), BF16),
        incoming_high=((BUCKETS, high_travel, 256), BF16),
        turned_low=((BUCKETS, 25 * ATOMS, LOW_TRAVEL), BF16),
        turned_high=((BUCKETS, 25 * ATOMS, high_travel), BF16),
        hidden_out=((BUCKETS, TRAVEL, C), BF16),
        hidden_in=((BUCKETS, TRAVEL, C), BF16),
        cotangent_in=((BUCKETS, 49 * ATOMS, C), BF16),
        aggregate=((49 * ATOMS, C), BF16),
        gradient=((49 * ATOMS, C), BF16),
    )
    for prefix, edges in (("halo_", HALO), ("inner_", INNER)):
        for name, shape in zip(GROUP, group_scratch(edges)):
            scratch[prefix + name] = shape
    semaphores = dict(load_sems=len(LOADED), store_sems=2)
    for move in ("codes", "cotangent", "hidden"):
        semaphores[move + "_send"] = BUCKETS
        semaphores[move + "_recv"] = BUCKETS
    names = [name + "_hbm" for name in LOADED] + ["result_hbm"] + list(scratch) + list(semaphores)
    result = pl.pallas_call(
        functools.partial(kernel, domains_x, domains_y, tuple(names)),
        out_shape=jax.ShapeDtypeStruct((2, 49 * ATOMS, C), BF16),
        in_specs=[pl.BlockSpec(memory_space=pltpu.HBM)] * len(LOADED),
        out_specs=pl.BlockSpec(memory_space=pltpu.HBM),
        scratch_shapes=[pltpu.VMEM(shape, dtype) for shape, dtype in scratch.values()]
        + [pltpu.SemaphoreType.DMA((count,)) for count in semaphores.values()],
        compiler_params=pltpu.CompilerParams(
            collective_id=0, has_side_effects=True, vmem_limit_bytes=60 * 1024 * 1024
        ),
        cost_estimate=pl.CostEstimate(
            flops=6 * 10**9, bytes_accessed=8 * 10**6, transcendentals=10**5
        ),
        name="message_layer",
    )(*[arrays[name] for name in LOADED])
    return tuple(rows.reshape(49, ATOMS, C).transpose(1, 0, 2) for rows in (result[0], result[1]))


def solution(mesh):
    return jax.shard_map(
        functools.partial(on_device, mesh.shape["gx"], mesh.shape["gy"]),
        mesh=mesh,
        in_specs=(
            P(("img", "gx", "gy"), None, None),
            P(("img", "gx", "gy"), None, None),
            P(),
            P(),
            P(),
            P(),
            P(("img", "gx", "gy"), None, None),
            P(("img", "gx", "gy"), None, None, None),
            P(("img", "gx", "gy"), None),
        ),
        out_specs=(P(("img", "gx", "gy"), None, None), P(("img", "gx", "gy"), None, None)),
        check_vma=False,
    )
```

```python
import collections
import functools
import math

import jax
import jax.numpy as jnp
import numpy as np
from jax import lax
from jax.experimental import pallas as pl
from jax.experimental.pallas import tpu as pltpu
from jax.sharding import PartitionSpec as P

MESH = pl.DeviceIdType.MESH
F32 = jnp.float32
BF16 = jnp.bfloat16

neighbour_steps = ((-1, -1), (-1, 0), (-1, 1), (0, -1), (0, 1), (1, -1), (1, 0), (1, 1))
BUCKETS = 8
CAP = 8
INNER = 96
HALO = BUCKETS * CAP
EDGES = INNER + HALO
ATOMS = 8
C = 128
RADIAL = 512

framed_rows = [(degree, order) for order in (0, 1, -1, 2, -2) for degree in range(abs(order), 7)]
low_rows = [f for f, (degree, order) in enumerate(framed_rows) if degree <= 4]
high_rows = [f for f, (degree, order) in enumerate(framed_rows) if degree > 4]
packed_rows = low_rows + high_rows
LOW = len(low_rows)
HIGH = len(high_rows)
FRAMED = LOW + HIGH
travel_rows = low_rows + [None] + high_rows
PAIRS = len(travel_rows) // 2
LOW_PAIRS = (LOW + 1) // 2
LOW_TRAVEL = LOW_PAIRS * 16
TRAVEL = PAIRS * 16
group_bounds = ((0, 7), (7, 13), (13, 19), (19, 24), (24, 29))


def harmonics(east, north, height):
    columns = np.zeros((height.shape[0], 49))
    real_part = np.ones(height.shape)
    imag_part = np.zeros(height.shape)
    for moment in range(7):
        if moment > 0:
            real_part, imag_part = (
                real_part * east - imag_part * north,
                real_part * north + imag_part * east,
            )
        older = np.zeros(height.shape)
        newer = (
            (-1.0) ** moment * float(np.prod(np.arange(1, 2 * moment, 2))) * np.ones(height.shape)
        )
        for degree in range(moment, 7):
            if degree > moment:
                older, newer = (
                    newer,
                    ((2 * degree - 1) * height * newer - (degree + moment - 1) * older)
                    / (degree - moment),
                )
            factor = math.sqrt(
                (2 * degree + 1)
                / (4.0 * math.pi)
                * math.factorial(degree - moment)
                / math.factorial(degree + moment)
            )
            centre = degree * degree + degree
            if moment == 0:
                columns[:, centre] = factor * newer
            else:
                columns[:, centre + moment] = math.sqrt(2.0) * factor * newer * real_part
                columns[:, centre - moment] = math.sqrt(2.0) * factor * newer * imag_part
    return columns


def legendre_pair(order, points):
    older = np.ones(points.shape)
    newer = points * 1.0
    for degree in range(2, order + 1):
        older, newer = (newer, ((2 * degree - 1) * points * newer - (degree - 1) * older) / degree)
    slope = order * (points * newer - older) / (points * points - 1.0)
    return (newer, slope)


def gauss_nodes(order):
    nodes = np.cos(math.pi * (np.arange(order) + 0.75) / (order + 0.5))
    for sweep in range(20):
        value, slope = legendre_pair(order, nodes)
        nodes = nodes - value / slope
    value, slope = legendre_pair(order, nodes)
    return (nodes, 2.0 / ((1.0 - nodes * nodes) * slope * slope))


def tilt_table():
    nodes, node_weights = gauss_nodes(7)
    turns = 16
    azimuth = 2.0 * math.pi * np.arange(turns) / turns
    height = np.repeat(nodes, turns)
    weights = np.repeat(node_weights, turns) * (2.0 * math.pi / turns)
    spread = np.tile(azimuth, nodes.shape[0])
    radius = np.sqrt(np.maximum(1.0 - height * height, 0.0))
    east = radius * np.cos(spread)
    north = radius * np.sin(spread)
    before = harmonics(east, north, height)
    after = harmonics(east, -height, north)
    full = after.T @ (before * weights[:, None])
    table = np.zeros((49, 49))
    for degree in range(7):
        first_row = degree * degree
        last_row = first_row + 2 * degree + 1
        table[first_row:last_row, first_row:last_row] = full[first_row:last_row, first_row:last_row]
    return table


def split_bf16(table):
    high = table.astype(jnp.bfloat16)
    low = (table - high.astype(np.float64)).astype(jnp.bfloat16)
    return high, low


@functools.lru_cache(maxsize=None)
def rotation_tables():
    tilt = tilt_table()
    degrees = np.array([l for l in range(7) for m in range(-l, l + 1)])
    orders = np.array([m for l in range(7) for m in range(-l, l + 1)])
    partner = degrees * degrees + degrees - orders
    signs = -np.sign(orders).astype(np.float64)
    matrix = np.zeros((16, 49, 49))
    for i in range(49):
        moment = abs(orders[i])
        matrix[moment] += np.outer(tilt[i], tilt[i])
        if moment > 0:
            matrix[6 + moment] += signs[i] * np.outer(tilt[i], tilt[partner[i]])
    swapped = matrix[:, :, partner] * (-signs)[None, None, :]
    first = np.zeros((16, FRAMED * 256))
    for place, f in enumerate(packed_rows):
        degree, order = framed_rows[f]
        row = degree * degree + degree + order
        start = 0 if degree <= 4 else 24
        for j in range(degree * degree, (degree + 1) * (degree + 1)):
            for atom in range(4):
                lane = place * 256 + atom * 32 + j - start
                first[:, lane] = matrix[:, row, j]
                first[:, lane + 128] = swapped[:, row, j]
    high, low = split_bf16(first)
    first = np.concatenate([high, low, high], axis=0)
    second = np.zeros((128, 512))
    for column, (lowest, highest, start) in enumerate(((0, 25, 0), (25, 49, 24))):
        for j in range(lowest, highest):
            moment = abs(orders[j])
            for atom in range(4):
                lane = column * 256 + atom * 32 + j - start
                for part in (64, 96):
                    second[part + moment, lane] = 1.0
                    if moment > 0:
                        second[part + 6 + moment, lane + 128] = 1.0
    return first, second.astype(jnp.bfloat16)


LOW_PART = slice(0, 25 * ATOMS)
HIGH_PART = slice(24 * ATOMS, 49 * ATOMS)


def place_tables():
    gather = np.zeros((25 * ATOMS, 256))
    for place in range(25):
        for atom in range(ATOMS):
            gather[place * ATOMS + atom, atom * 32 + place] = 1.0
    return gather.astype(jnp.bfloat16), gather.T.astype(jnp.bfloat16)


def cosine_terms():
    points = 0.125 + 0.125 * np.cos(math.pi * (np.arange(200) + 0.5) / 200)
    fit = np.polynomial.chebyshev.Chebyshev.fit(
        points, np.cos(2.0 * math.pi * np.sqrt(points)), 8, domain=[0.0, 0.25]
    )
    return [float(term) for term in fit.convert(kind=np.polynomial.Polynomial).coef]


def column_of(columns, which):
    return columns[:, which : which + 1]


def dot(left, right):
    return jnp.dot(left, right, preferred_element_type=F32)


def dot_rows(left, right):
    return lax.dot_general(left, right, (((0,), (0,)), ((), ())), preferred_element_type=F32)


def dot_columns(left, right):
    return lax.dot_general(left, right, (((1,), (1,)), ((), ())), preferred_element_type=F32)


def angle_terms(alpha, beta):
    lane = lax.broadcasted_iota(jnp.int32, (1, 128), 1)
    term = lane & 15
    moment = jnp.where(term < 7, term, term - 6).astype(F32)
    shift = jnp.where(term < 7, 0.0, -0.25).astype(F32)
    code = jnp.where(lane < 64, beta, alpha)
    turns = code * (moment * (1.0 / 4096.0)) + shift
    turns = turns - jnp.floor(turns + 0.5)
    square = turns * turns
    terms = cosine_terms()
    value = terms[-1]
    for coefficient in terms[-2::-1]:
        value = value * square + coefficient
    high = value.astype(BF16).astype(F32)
    return jnp.where((lane & 63) < 32, high, value - high).astype(BF16)


def atom_masks(atoms):
    lane = lax.broadcasted_iota(jnp.int32, (1, 128), 1) >> 5
    lane = lane.astype(F32)
    return [jnp.where(atoms == lane + 4.0 * half, 1.0, 0.0).astype(BF16) for half in range(2)]


def coefficient_blocks(refs, spread):
    return [
        dot(spread, jnp.concatenate([ref[part, :] for ref in refs], axis=1)).astype(BF16)
        for part in (LOW_PART, HIGH_PART)
    ]


def place_rows(gather, columns):
    high = columns.astype(BF16)
    low = (columns - high.astype(F32)).astype(BF16)
    return dot_columns(gather, high) + dot_columns(gather, low)


def join_sets(low, high):
    return jnp.concatenate(
        [low[0:192], low[192:200] + high[0:ATOMS], high[ATOMS:200]], axis=0
    ).astype(BF16)


GROUP = (
    "source_low",
    "source_high",
    "framed_zero",
    "framed_one",
    "framed_two",
    "hidden",
    "upstream",
    "back_low",
    "back_high",
)
Group = collections.namedtuple("Group", ("edges",) + GROUP)


def group_scratch(edges):
    return [
        ((LOW * edges, 256), BF16),
        ((HIGH * edges, 256), BF16),
        ((edges, 7 * C), BF16),
        ((2 * edges, 12 * C), BF16),
        ((2 * edges, 10 * C), BF16),
        ((FRAMED, edges, C), F32),
        ((FRAMED, edges, C), F32),
        ((LOW * edges, C), BF16),
        ((HIGH * edges, C), BF16),
    ]


def of_place(place, edges, low, high):
    if place < LOW:
        return low, slice(place * edges, (place + 1) * edges)
    return high, slice((place - LOW) * edges, (place - LOW + 1) * edges)


def put_grouped(group, f, block, sign):
    if f < 7:
        group.framed_zero[:, f * C : (f + 1) * C] = block
        return
    grouped, size, at = (group.framed_one, 6, f - 7) if f < 19 else (group.framed_two, 5, f - 19)
    minus, at = at // size, at % size
    own = slice(minus * group.edges, (minus + 1) * group.edges)
    other = slice((1 - minus) * group.edges, (2 - minus) * group.edges)
    grouped[own, at * C : (at + 1) * C] = block
    grouped[other, (size + at) * C : (size + at + 1) * C] = (
        block if (sign > 0) == (minus == 1) else -block
    )


def chunks(rows):
    return [(at, min(at + 2, rows)) for at in range(0, rows, 2)]


def convolve(group, w_zero, w_one, w_two, loads):
    loads[0].wait()
    gate = None
    for begin, end in chunks(7):
        value = dot(group.framed_zero[...], w_zero[:, begin * C : end * C])
        if gate is None:
            gate = 1.0 / (1.0 + jnp.exp(-value[:, 0:C]))
        for f in range(begin, end):
            group.hidden[f] = value[:, (f - begin) * C : (f - begin + 1) * C] * gate
    for number, (grouped, weights, size, plus, minus) in enumerate(
        ((group.framed_one, w_one, 6, 7, 13), (group.framed_two, w_two, 5, 19, 24))
    ):
        loads[1 + number].wait()
        for begin, end in chunks(size):
            value = dot(grouped[...], weights[:, begin * C : end * C])
            for f in range(begin, end):
                columns = slice((f - begin) * C, (f - begin + 1) * C)
                group.hidden[plus + f] = value[0 : group.edges, columns] * gate
                group.hidden[minus + f] = value[group.edges :, columns] * gate
    return gate


def back_through_gate(group, gate):
    total = group.upstream[0] * group.hidden[0]
    for f in range(1, FRAMED):
        total = total + group.upstream[f] * group.hidden[f]
    through = total * (0.25 * (1.0 - gate))
    scaled_gate = 0.25 * gate
    for f in range(FRAMED):
        block = group.upstream[f] * scaled_gate
        if f == 0:
            block = block + through
        put_grouped(group, f, block.astype(BF16), 1)


def convolve_back(group, radial, w_zero, w_one, w_two):
    def put_back(f, block):
        rows, at = of_place(packed_rows.index(f), group.edges, group.back_low, group.back_high)
        rows[at, :] = (block * radial).astype(BF16)

    for begin, end in chunks(7):
        value = dot(group.framed_zero[...], w_zero[:, begin * C : end * C])
        for f in range(begin, end):
            put_back(f, value[:, (f - begin) * C : (f - begin + 1) * C])
    for grouped, weights, size, plus, minus in (
        (group.framed_one, w_one, 6, 7, 13),
        (group.framed_two, w_two, 5, 19, 24),
    ):
        for begin, end in chunks(size):
            value = dot(grouped[...], weights[:, begin * C : end * C])
            for f in range(begin, end):
                columns = slice((f - begin) * C, (f - begin + 1) * C)
                put_back(plus + f, value[0 : group.edges, columns])
                put_back(minus + f, value[group.edges :, columns])


def gradient_columns(group):
    return (
        dot_rows(group.back_low[...], group.source_low[...]),
        dot_rows(group.back_high[...], group.source_high[...]),
    )


def radial_rows(codes, weight_high, weight_low):
    centre = lax.broadcasted_iota(jnp.int32, (1, RADIAL), 1).astype(F32) * 2.0
    distance = (codes - centre) * (22.0 / 1024.0)
    basis = jnp.exp(-0.5 * (distance * distance))
    basis_high = basis.astype(BF16)
    basis_low = (basis - basis_high.astype(F32)).astype(BF16)
    return dot(basis_high, weight_high) + (
        dot(basis_high, weight_low) + dot(basis_low, weight_high)
    )


def wide_masks(atoms):
    masks = [mask.astype(F32) for mask in atom_masks(atoms)]
    return [
        [
            jnp.concatenate([mask[b * CAP : (b + 1) * CAP]] * 2, axis=0).astype(BF16)
            for b in range(BUCKETS)
        ]
        for mask in masks
    ]


def put_pair(pair, rows, masks, low, high):
    for bucket in range(BUCKETS):
        slots = slice(bucket * CAP, (bucket + 1) * CAP)
        joined = jnp.concatenate([rows[0][slots], rows[1][slots]], axis=0).astype(BF16)
        for half in range(2):
            columns = slice(128 * half, 128 * half + 128)
            masked = joined * masks[half][bucket]
            if pair < LOW_PAIRS:
                low[bucket, 16 * pair : 16 * pair + 16, columns] = masked
            else:
                at = 16 * (pair - LOW_PAIRS)
                high[bucket, at : at + 16, columns] = masked


def kernel(domains_x, domains_y, names, *refs):
    refs = collections.namedtuple("Refs", names)(*refs)
    halo = Group(HALO, *(getattr(refs, "halo_" + name) for name in GROUP))
    inner = Group(INNER, *(getattr(refs, "inner_" + name) for name in GROUP))
    place_x = lax.axis_index("gx")
    place_y = lax.axis_index("gy")
    image = lax.axis_index("img")

    def inside(step_x, step_y):
        x = place_x + step_x
        y = place_y + step_y
        return (x >= 0) & (x < domains_x) & (y >= 0) & (y < domains_y)

    def device_at(step_x, step_y):
        return (place_x + step_x, place_y + step_y, image)

    barrier = pltpu.get_barrier_semaphore()
    for step_x, step_y in reversed(neighbour_steps):

        @pl.when(inside(step_x, step_y))
        def _(step_x=step_x, step_y=step_y):
            pl.semaphore_signal(
                barrier, inc=1, device_id=device_at(step_x, step_y), device_id_type=MESH
            )

    loads = {}
    for number, name in enumerate(LOADED):
        loads[name] = pltpu.make_async_copy(
            getattr(refs, name + "_hbm"), getattr(refs, name), refs.load_sems.at[number]
        )
        loads[name].start()

    class Once:
        def __init__(self, name):
            self.name = name

        def wait(self):
            if self.name in loads:
                loads.pop(self.name).wait()

    for bucket, (step_x, step_y) in enumerate(neighbour_steps):

        @pl.when(jnp.logical_not(inside(-step_x, -step_y)))
        def _(bucket=bucket):
            refs.codes_in[bucket] = jnp.full((CAP, 128), -1.0, F32)
            refs.hidden_in[bucket] = jnp.zeros((TRAVEL, C), BF16)

        @pl.when(jnp.logical_not(inside(step_x, step_y)))
        def _(bucket=bucket):
            refs.cotangent_in[bucket] = jnp.zeros((ATOMS * 49, C), BF16)

    def exchange(move, bucket, way):
        source, target, send, recv = move
        step_x, step_y = neighbour_steps[bucket]
        return pltpu.make_async_remote_copy(
            src_ref=source if source is refs.cotangent_hbm else source.at[bucket],
            dst_ref=target.at[bucket],
            send_sem=send.at[bucket],
            recv_sem=recv.at[bucket],
            device_id=device_at(way * step_x, way * step_y),
            device_id_type=MESH,
        )

    def each(move, way, buckets, act):
        for bucket in buckets:
            step_x, step_y = neighbour_steps[bucket]

            @pl.when(inside(way * step_x, way * step_y))
            def _(bucket=bucket):
                act(exchange(move, bucket, way))

    def start(move, way, buckets=BUCKET_ORDER):
        each(move, way, buckets, lambda copy: copy.start())

    def await_sent(move, way, buckets=BUCKET_ORDER):
        each(move, way, buckets, lambda copy: copy.wait_send())

    def await_arrivals(move, way, buckets=BUCKET_ORDER):
        each(move, -way, buckets, lambda copy: copy.wait_recv())

    codes_move = (refs.codes_out, refs.codes_in, refs.codes_send, refs.codes_recv)
    cotangent_move = (
        refs.cotangent_hbm,
        refs.cotangent_in,
        refs.cotangent_send,
        refs.cotangent_recv,
    )
    hidden_move = (refs.hidden_out, refs.hidden_in, refs.hidden_send, refs.hidden_recv)

    beside_x = jnp.where(place_x > 0, 2, 1) + jnp.where(place_x < domains_x - 1, 1, 0)
    beside_y = jnp.where(place_y > 0, 2, 1) + jnp.where(place_y < domains_y - 1, 1, 0)

    refs.codes_table[...] = jnp.zeros((128, 128), F32)
    for name in ("inner_edges", "halo_edges", "halo_counts"):
        Once(name).wait()
    counts = refs.halo_counts[...].astype(F32)
    for which in range(5):
        refs.codes_table[which * BUCKETS : (which + 1) * BUCKETS, 0:CAP] = refs.halo_edges[
            which
        ].astype(F32)
        refs.codes_table[40 + which : 41 + which, 0:INNER] = refs.inner_edges[which].astype(F32)
    turned_codes = refs.codes_table[...].T
    inner_codes = [column_of(turned_codes[0:INNER], 40 + which) for which in range(5)]
    lane = lax.broadcasted_iota(jnp.int32, (CAP, 128), 1)
    slot = lax.broadcasted_iota(jnp.int32, (CAP, 1), 0).astype(F32)
    slot_codes = [
        [column_of(turned_codes[0:CAP], which * BUCKETS + bucket) for bucket in range(BUCKETS)]
        for which in range(5)
    ]
    halo_targets = []
    for bucket in range(BUCKETS):
        target = jnp.where(slot < column_of(counts, bucket), slot_codes[1][bucket], -1.0)
        refs.codes_out[bucket] = jnp.where(
            lane == 0, target, jnp.where(lane == 1, slot_codes[2][bucket], slot_codes[3][bucket])
        )
        halo_targets.append(target)
    halo_codes = [jnp.concatenate(columns, axis=0) for columns in slot_codes]
    pl.semaphore_wait(barrier, beside_x * beside_y - 1)
    start(cotangent_move, -1, BUCKET_ORDER[0:4])
    start(codes_move, 1)
    start(cotangent_move, -1, BUCKET_ORDER[4:8])

    def spin_factors(terms):
        both = dot(terms, refs.second[...])
        return [
            (both[:, 256 * k : 256 * k + 128], both[:, 256 * k + 128 : 256 * k + 256])
            for k in range(2)
        ]

    def rotation_row(terms, factors, place):
        cosine, sine = factors[0 if place < LOW else 1]
        both = dot(terms, refs.first[:, place * 256 : place * 256 + 256])
        return cosine * both[:, 0:128] + sine * both[:, 128:256]

    def frame(group, codes, radial, put_row, put_rows):
        terms = angle_terms(codes[2], codes[3])
        factors = spin_factors(terms)
        terms = terms[:, 0:48]
        masks = atom_masks(codes[0])
        for pair in range(PAIRS):
            pair_rows = []
            for f in travel_rows[2 * pair : 2 * pair + 2]:
                if f is None:
                    pair_rows.append(jnp.zeros((group.edges, 128), F32))
                    continue
                place = packed_rows.index(f)
                wide = rotation_row(terms, factors, place)
                pair_rows.append(wide)
                row = wide.astype(BF16)
                put_row(place, row)
                masked = jnp.concatenate([row * masks[0], row * masks[1]], axis=1)
                rows, at = of_place(place, group.edges, group.source_low, group.source_high)
                rows[at, :] = masked
                turned = dot(masked, feature_low if place < LOW else feature_high)
                put_grouped(group, f, (turned * radial).astype(BF16), -1)
            put_rows(pair, pair_rows)

    for name in ("first", "second", "features", "spread", "radial"):
        Once(name).wait()
    feature_low, feature_high = coefficient_blocks([refs.features], refs.spread[...])
    weight = refs.radial[...]
    weight_high = weight.astype(BF16)
    weight_low = (weight - weight_high.astype(F32)).astype(BF16)
    halo_radial = radial_rows(halo_codes[4], weight_high, weight_low)
    target_masks = wide_masks(jnp.concatenate(halo_targets, axis=0))
    frame(
        halo,
        halo_codes,
        halo_radial,
        lambda place, row: None,
        lambda pair, rows: put_pair(pair, rows, target_masks, refs.target_low, refs.target_high),
    )
    weights = (refs.w_zero, refs.w_one, refs.w_two)
    weight_loads = [Once(name) for name in ("w_zero", "w_one", "w_two")]
    halo_gate = convolve(halo, *weights, weight_loads)
    for pair in range(PAIRS):
        f, g = travel_rows[2 * pair : 2 * pair + 2]
        for bucket in range(BUCKETS):
            slots = slice(bucket * CAP, (bucket + 1) * CAP)
            upper = halo.hidden[f, slots, :]
            lower = jnp.zeros((CAP, C), F32) if g is None else halo.hidden[g, slots, :]
            refs.hidden_out[bucket, 16 * pair : 16 * pair + 16, :] = jnp.concatenate(
                [upper, lower], axis=0
            ).astype(BF16)

    back_weights = (refs.back_zero, refs.back_one, refs.back_two)
    for matrix, turned, size in zip(weights, back_weights, (7 * C, 6 * C, 5 * C)):
        for begin in range(0, matrix.shape[0], size):
            turned[begin : begin + size, :] = matrix[begin : begin + size, :].T

    inner_radial = radial_rows(inner_codes[4], weight_high, weight_low)
    inner_masks = atom_masks(inner_codes[1])

    def put_inner(place, row):
        rows, at = of_place(place, INNER, refs.inner_target_low, refs.inner_target_high)
        rows[at, :] = jnp.concatenate([row * inner_masks[0], row * inner_masks[1]], axis=1)

    frame(inner, inner_codes, inner_radial, put_inner, lambda pair, rows: None)
    inner_gate = convolve(inner, *weights, weight_loads)
    Once("cotangent").wait()
    cot_low, cot_high = coefficient_blocks([refs.cotangent], refs.spread[...])
    for place, f in enumerate(packed_rows):
        rows, at = of_place(place, INNER, refs.inner_target_low, refs.inner_target_high)
        inner.upstream[f] = dot(rows[at, :], cot_low if place < LOW else cot_high)
        rows, at = of_place(place, INNER, refs.inner_hidden_low, refs.inner_hidden_high)
        rows[at, :] = inner.hidden[f].astype(BF16)
    back_through_gate(inner, inner_gate)
    convolve_back(inner, inner_radial, *back_weights)
    gradient_low, gradient_high = gradient_columns(inner)
    low = dot_rows(refs.inner_hidden_low[...], refs.inner_target_low[...])
    high = dot_rows(refs.inner_hidden_high[...], refs.inner_target_high[...])

    for bucket in BUCKET_ORDER:
        await_sent(cotangent_move, -1, (BUCKETS - 1 - bucket,))
        start(hidden_move, 1, (bucket,))

    for natural, target in (
        (refs.natural_low, refs.target_low),
        (refs.natural_high, refs.target_high),
    ):
        for bucket in range(BUCKETS):
            natural[bucket] = dot(target[bucket], refs.spread[...]).astype(BF16)

    Once("gather").wait()

    await_arrivals(codes_move, 1)
    arrived = refs.codes_in[...].reshape(HALO, 128)
    in_terms = angle_terms(column_of(arrived, 1), column_of(arrived, 2))
    in_factors = spin_factors(in_terms)
    in_terms = in_terms[:, 0:48]
    in_masks = wide_masks(column_of(arrived, 0))
    for pair in range(PAIRS):
        rows = [
            jnp.zeros((HALO, 128), F32)
            if f is None
            else rotation_row(in_terms, in_factors, packed_rows.index(f))
            for f in travel_rows[2 * pair : 2 * pair + 2]
        ]
        put_pair(pair, rows, in_masks, refs.incoming_low, refs.incoming_high)

    for bucket in range(BUCKETS):
        refs.turned_low[bucket] = dot_columns(refs.gather[...], refs.incoming_low[bucket]).astype(
            BF16
        )
        refs.turned_high[bucket] = dot_columns(
            refs.gather[...], refs.incoming_high[bucket]
        ).astype(BF16)
    low = place_rows(refs.gather[...], low)
    high = place_rows(refs.gather[...], high)

    for couple in range(0, BUCKETS, 2):
        buckets = BUCKET_ORDER[couple : couple + 2]
        await_arrivals(cotangent_move, -1, buckets)
        for bucket in buckets:
            slots = slice(bucket * CAP, (bucket + 1) * CAP)
            turned = (
                dot(refs.natural_low[bucket], refs.cotangent_in[bucket, LOW_PART, :]),
                dot(refs.natural_high[bucket], refs.cotangent_in[bucket, HIGH_PART, :]),
            )
            for pair in range(PAIRS):
                of_set = turned[0 if pair < LOW_PAIRS else 1]
                at = 16 * (pair if pair < LOW_PAIRS else pair - LOW_PAIRS)
                for half, f in enumerate(travel_rows[2 * pair : 2 * pair + 2]):
                    if f is not None:
                        halo.upstream[f, slots, :] = of_set[
                            at + CAP * half : at + CAP * (half + 1)
                        ]
    back_through_gate(halo, halo_gate)
    convolve_back(halo, halo_radial, *back_weights)
    halo_low, halo_high = gradient_columns(halo)
    refs.gradient[...] = join_sets(
        place_rows(refs.gather[...], gradient_low + halo_low),
        place_rows(refs.gather[...], gradient_high + halo_high),
    )
    gradient_store = pltpu.make_async_copy(
        refs.gradient, refs.result_hbm.at[1], refs.store_sems.at[1]
    )
    gradient_store.start()

    for begin, end in ((0, 4), (4, BUCKETS)):
        await_arrivals(hidden_move, 1, BUCKET_ORDER[begin:end])
        for bucket in BUCKET_ORDER[begin:end]:
            low = low + dot(refs.turned_low[bucket], refs.hidden_in[bucket, 0:LOW_TRAVEL, :])
            high = high + dot(
                refs.turned_high[bucket], refs.hidden_in[bucket, LOW_TRAVEL:TRAVEL, :]
            )
    refs.aggregate[...] = join_sets(0.25 * low, 0.25 * high)
    aggregate_store = pltpu.make_async_copy(
        refs.aggregate, refs.result_hbm.at[0], refs.store_sems.at[0]
    )
    aggregate_store.start()
    await_sent(codes_move, 1)
    await_sent(hidden_move, 1)
    gradient_store.wait()
    aggregate_store.wait()


LOADED = (
    "inner_edges",
    "halo_edges",
    "halo_counts",
    "first",
    "second",
    "features",
    "spread",
    "radial",
    "w_zero",
    "w_one",
    "w_two",
    "cotangent",
    "gather",
)
BUCKET_ORDER = (0, 2, 5, 7, 1, 6, 3, 4)


def on_device(
    domains_x,
    domains_y,
    features,
    cotangent,
    w_zero,
    w_one,
    w_two,
    radial_weight,
    inner_edges,
    halo_edges,
    halo_counts,
):
    first, second = rotation_tables()
    gather, spread = place_tables()
    arrays = dict(
        inner_edges=inner_edges.transpose(1, 0, 2),
        halo_edges=halo_edges.transpose(0, 2, 1, 3).reshape(5, BUCKETS, CAP),
        halo_counts=halo_counts,
        first=jnp.asarray(first),
        second=jnp.asarray(second),
        features=features.transpose(1, 0, 2).reshape(49 * ATOMS, C),
        spread=jnp.asarray(spread),
        radial=radial_weight,
        w_zero=w_zero,
        w_one=w_one.reshape(12 * C, 6 * C),
        w_two=w_two.reshape(10 * C, 5 * C),
        cotangent=cotangent.transpose(1, 0, 2).reshape(49 * ATOMS, C),
        gather=jnp.asarray(gather),
    )
    scratch = {name: (arrays[name].shape, arrays[name].dtype) for name in LOADED}
    high_travel = TRAVEL - LOW_TRAVEL
    scratch.update(
        back_zero=scratch["w_zero"],
        back_one=scratch["w_one"],
        back_two=scratch["w_two"],
        codes_table=((128, 128), F32),
        codes_out=((BUCKETS, CAP, 128), F32),
        codes_in=((BUCKETS, CAP, 128), F32),
        inner_target_low=((LOW * INNER, 256), BF16),
        inner_target_high=((HIGH * INNER, 256), BF16),
        inner_hidden_low=((LOW * INNER, C), BF16),
        inner_hidden_high=((HIGH * INNER, C), BF16),
        target_low=((BUCKETS, LOW_TRAVEL, 256), BF16),
        target_high=((BUCKETS, high_travel, 256), BF16),
        natural_low=((BUCKETS, LOW_TRAVEL, 25 * ATOMS), BF16),
        natural_high=((BUCKETS, high_travel, 25 * ATOMS), BF16),
        incoming_low=((BUCKETS, LOW_TRAVEL, 256), BF16),
        incoming_high=((BUCKETS, high_travel, 256), BF16),
        turned_low=((BUCKETS, 25 * ATOMS, LOW_TRAVEL), BF16),
        turned_high=((BUCKETS, 25 * ATOMS, high_travel), BF16),
        hidden_out=((BUCKETS, TRAVEL, C), BF16),
        hidden_in=((BUCKETS, TRAVEL, C), BF16),
        cotangent_in=((BUCKETS, 49 * ATOMS, C), BF16),
        aggregate=((49 * ATOMS, C), BF16),
        gradient=((49 * ATOMS, C), BF16),
    )
    for prefix, edges in (("halo_", HALO), ("inner_", INNER)):
        for name, shape in zip(GROUP, group_scratch(edges)):
            scratch[prefix + name] = shape
    semaphores = dict(load_sems=len(LOADED), store_sems=2)
    for move in ("codes", "cotangent", "hidden"):
        semaphores[move + "_send"] = BUCKETS
        semaphores[move + "_recv"] = BUCKETS
    names = [name + "_hbm" for name in LOADED] + ["result_hbm"] + list(scratch) + list(semaphores)
    result = pl.pallas_call(
        functools.partial(kernel, domains_x, domains_y, tuple(names)),
        out_shape=jax.ShapeDtypeStruct((2, 49 * ATOMS, C), BF16),
        in_specs=[pl.BlockSpec(memory_space=pltpu.HBM)] * len(LOADED),
        out_specs=pl.BlockSpec(memory_space=pltpu.HBM),
        scratch_shapes=[pltpu.VMEM(shape, dtype) for shape, dtype in scratch.values()]
        + [pltpu.SemaphoreType.DMA((count,)) for count in semaphores.values()],
        compiler_params=pltpu.CompilerParams(
            collective_id=0, has_side_effects=True, vmem_limit_bytes=60 * 1024 * 1024
        ),
        cost_estimate=pl.CostEstimate(
            flops=6 * 10**9, bytes_accessed=8 * 10**6, transcendentals=10**5
        ),
        name="message_layer",
    )(*[arrays[name] for name in LOADED])
    return tuple(rows.reshape(49, ATOMS, C).transpose(1, 0, 2) for rows in (result[0], result[1]))


def solution(mesh):
    return jax.shard_map(
        functools.partial(on_device, mesh.shape["gx"], mesh.shape["gy"]),
        mesh=mesh,
        in_specs=(
            P(("img", "gx", "gy"), None, None),
            P(("img", "gx", "gy"), None, None),
            P(),
            P(),
            P(),
            P(),
            P(("img", "gx", "gy"), None, None),
            P(("img", "gx", "gy"), None, None, None),
            P(("img", "gx", "gy"), None),
        ),
        out_specs=(P(("img", "gx", "gy"), None, None), P(("img", "gx", "gy"), None, None)),
        check_vma=False,
    )
```

```python
import collections
import functools
import math

import jax
import jax.numpy as jnp
import numpy as np
from jax import lax
from jax.experimental import pallas as pl
from jax.experimental.pallas import tpu as pltpu
from jax.sharding import PartitionSpec as P

MESH = pl.DeviceIdType.MESH
F32 = jnp.float32
BF16 = jnp.bfloat16

neighbour_steps = ((-1, -1), (-1, 0), (-1, 1), (0, -1), (0, 1), (1, -1), (1, 0), (1, 1))
BUCKETS = 8
CAP = 8
INNER = 96
HALO = BUCKETS * CAP
EDGES = INNER + HALO
ATOMS = 8
C = 128
RADIAL = 512

framed_rows = [(degree, order) for order in (0, 1, -1, 2, -2) for degree in range(abs(order), 7)]
low_rows = [f for f, (degree, order) in enumerate(framed_rows) if degree <= 4]
high_rows = [f for f, (degree, order) in enumerate(framed_rows) if degree > 4]
packed_rows = low_rows + high_rows
LOW = len(low_rows)
HIGH = len(high_rows)
FRAMED = LOW + HIGH
travel_rows = low_rows + [None] + high_rows
PAIRS = len(travel_rows) // 2
LOW_PAIRS = (LOW + 1) // 2
LOW_TRAVEL = LOW_PAIRS * 16
TRAVEL = PAIRS * 16
group_bounds = ((0, 7), (7, 13), (13, 19), (19, 24), (24, 29))


def harmonics(east, north, height):
    columns = np.zeros((height.shape[0], 49))
    real_part = np.ones(height.shape)
    imag_part = np.zeros(height.shape)
    for moment in range(7):
        if moment > 0:
            real_part, imag_part = (
                real_part * east - imag_part * north,
                real_part * north + imag_part * east,
            )
        older = np.zeros(height.shape)
        newer = (
            (-1.0) ** moment * float(np.prod(np.arange(1, 2 * moment, 2))) * np.ones(height.shape)
        )
        for degree in range(moment, 7):
            if degree > moment:
                older, newer = (
                    newer,
                    ((2 * degree - 1) * height * newer - (degree + moment - 1) * older)
                    / (degree - moment),
                )
            factor = math.sqrt(
                (2 * degree + 1)
                / (4.0 * math.pi)
                * math.factorial(degree - moment)
                / math.factorial(degree + moment)
            )
            centre = degree * degree + degree
            if moment == 0:
                columns[:, centre] = factor * newer
            else:
                columns[:, centre + moment] = math.sqrt(2.0) * factor * newer * real_part
                columns[:, centre - moment] = math.sqrt(2.0) * factor * newer * imag_part
    return columns


def legendre_pair(order, points):
    older = np.ones(points.shape)
    newer = points * 1.0
    for degree in range(2, order + 1):
        older, newer = (newer, ((2 * degree - 1) * points * newer - (degree - 1) * older) / degree)
    slope = order * (points * newer - older) / (points * points - 1.0)
    return (newer, slope)


def gauss_nodes(order):
    nodes = np.cos(math.pi * (np.arange(order) + 0.75) / (order + 0.5))
    for sweep in range(20):
        value, slope = legendre_pair(order, nodes)
        nodes = nodes - value / slope
    value, slope = legendre_pair(order, nodes)
    return (nodes, 2.0 / ((1.0 - nodes * nodes) * slope * slope))


def tilt_table():
    nodes, node_weights = gauss_nodes(7)
    turns = 16
    azimuth = 2.0 * math.pi * np.arange(turns) / turns
    height = np.repeat(nodes, turns)
    weights = np.repeat(node_weights, turns) * (2.0 * math.pi / turns)
    spread = np.tile(azimuth, nodes.shape[0])
    radius = np.sqrt(np.maximum(1.0 - height * height, 0.0))
    east = radius * np.cos(spread)
    north = radius * np.sin(spread)
    before = harmonics(east, north, height)
    after = harmonics(east, -height, north)
    full = after.T @ (before * weights[:, None])
    table = np.zeros((49, 49))
    for degree in range(7):
        first_row = degree * degree
        last_row = first_row + 2 * degree + 1
        table[first_row:last_row, first_row:last_row] = full[first_row:last_row, first_row:last_row]
    return table


def split_bf16(table):
    high = table.astype(jnp.bfloat16)
    low = (table - high.astype(np.float64)).astype(jnp.bfloat16)
    return high, low


@functools.lru_cache(maxsize=None)
def rotation_tables():
    tilt = tilt_table()
    degrees = np.array([l for l in range(7) for m in range(-l, l + 1)])
    orders = np.array([m for l in range(7) for m in range(-l, l + 1)])
    partner = degrees * degrees + degrees - orders
    signs = -np.sign(orders).astype(np.float64)
    matrix = np.zeros((16, 49, 49))
    for i in range(49):
        moment = abs(orders[i])
        matrix[moment] += np.outer(tilt[i], tilt[i])
        if moment > 0:
            matrix[6 + moment] += signs[i] * np.outer(tilt[i], tilt[partner[i]])
    swapped = matrix[:, :, partner] * (-signs)[None, None, :]
    first = np.zeros((16, FRAMED * 256))
    for place, f in enumerate(packed_rows):
        degree, order = framed_rows[f]
        row = degree * degree + degree + order
        start = 0 if degree <= 4 else 24
        for j in range(degree * degree, (degree + 1) * (degree + 1)):
            for atom in range(4):
                lane = place * 256 + atom * 32 + j - start
                first[:, lane] = matrix[:, row, j]
                first[:, lane + 128] = swapped[:, row, j]
    high, low = split_bf16(first)
    first = np.concatenate([high, low, high], axis=0)
    second = np.zeros((128, 512))
    for column, (lowest, highest, start) in enumerate(((0, 25, 0), (25, 49, 24))):
        for j in range(lowest, highest):
            moment = abs(orders[j])
            for atom in range(4):
                lane = column * 256 + atom * 32 + j - start
                for part in (64, 96):
                    second[part + moment, lane] = 1.0
                    if moment > 0:
                        second[part + 6 + moment, lane + 128] = 1.0
    return first, second.astype(jnp.bfloat16)


LOW_PART = slice(0, 25 * ATOMS)
HIGH_PART = slice(24 * ATOMS, 49 * ATOMS)


def place_tables():
    gather = np.zeros((25 * ATOMS, 256))
    for place in range(25):
        for atom in range(ATOMS):
            gather[place * ATOMS + atom, atom * 32 + place] = 1.0
    return gather.astype(jnp.bfloat16), gather.T.astype(jnp.bfloat16)


def cosine_terms():
    points = 0.125 + 0.125 * np.cos(math.pi * (np.arange(200) + 0.5) / 200)
    fit = np.polynomial.chebyshev.Chebyshev.fit(
        points, np.cos(2.0 * math.pi * np.sqrt(points)), 8, domain=[0.0, 0.25]
    )
    return [float(term) for term in fit.convert(kind=np.polynomial.Polynomial).coef]


def column_of(columns, which):
    return columns[:, which : which + 1]


def dot(left, right):
    return jnp.dot(left, right, preferred_element_type=F32)


def dot_rows(left, right):
    return lax.dot_general(left, right, (((0,), (0,)), ((), ())), preferred_element_type=F32)


def dot_columns(left, right):
    return lax.dot_general(left, right, (((1,), (1,)), ((), ())), preferred_element_type=F32)


def angle_terms(alpha, beta):
    lane = lax.broadcasted_iota(jnp.int32, (1, 128), 1)
    term = lane & 15
    moment = jnp.where(term < 7, term, term - 6).astype(F32)
    shift = jnp.where(term < 7, 0.0, -0.25).astype(F32)
    code = jnp.where(lane < 64, beta, alpha)
    turns = code * (moment * (1.0 / 4096.0)) + shift
    turns = turns - jnp.floor(turns + 0.5)
    square = turns * turns
    terms = cosine_terms()
    value = terms[-1]
    for coefficient in terms[-2::-1]:
        value = value * square + coefficient
    high = value.astype(BF16).astype(F32)
    return jnp.where((lane & 63) < 32, high, value - high).astype(BF16)


def atom_masks(atoms):
    lane = lax.broadcasted_iota(jnp.int32, (1, 128), 1) >> 5
    lane = lane.astype(F32)
    return [jnp.where(atoms == lane + 4.0 * half, 1.0, 0.0).astype(BF16) for half in range(2)]


def coefficient_blocks(refs, spread):
    return [
        dot(spread, jnp.concatenate([ref[part, :] for ref in refs], axis=1)).astype(BF16)
        for part in (LOW_PART, HIGH_PART)
    ]


def place_rows(gather, columns):
    high = columns.astype(BF16)
    low = (columns - high.astype(F32)).astype(BF16)
    return dot_columns(gather, high) + dot_columns(gather, low)


def join_sets(low, high):
    return jnp.concatenate(
        [low[0:192], low[192:200] + high[0:ATOMS], high[ATOMS:200]], axis=0
    ).astype(BF16)


GROUP = (
    "source_low",
    "source_high",
    "framed_zero",
    "framed_one",
    "framed_two",
    "hidden",
    "upstream",
    "back_low",
    "back_high",
)
Group = collections.namedtuple("Group", ("edges",) + GROUP)


def group_scratch(edges):
    return [
        ((LOW * edges, 256), BF16),
        ((HIGH * edges, 256), BF16),
        ((edges, 7 * C), BF16),
        ((2 * edges, 12 * C), BF16),
        ((2 * edges, 10 * C), BF16),
        ((FRAMED, edges, C), F32),
        ((FRAMED, edges, C), F32),
        ((LOW * edges, C), BF16),
        ((HIGH * edges, C), BF16),
    ]


def of_place(place, edges, low, high):
    if place < LOW:
        return low, slice(place * edges, (place + 1) * edges)
    return high, slice((place - LOW) * edges, (place - LOW + 1) * edges)


def put_grouped(group, f, block, sign):
    if f < 7:
        group.framed_zero[:, f * C : (f + 1) * C] = block
        return
    grouped, size, at = (group.framed_one, 6, f - 7) if f < 19 else (group.framed_two, 5, f - 19)
    minus, at = at // size, at % size
    own = slice(minus * group.edges, (minus + 1) * group.edges)
    other = slice((1 - minus) * group.edges, (2 - minus) * group.edges)
    grouped[own, at * C : (at + 1) * C] = block
    grouped[other, (size + at) * C : (size + at + 1) * C] = (
        block if (sign > 0) == (minus == 1) else -block
    )


def chunks(rows):
    return [(at, min(at + 2, rows)) for at in range(0, rows, 2)]


def convolve(group, w_zero, w_one, w_two, loads):
    loads[0].wait()
    gate = None
    for begin, end in chunks(7):
        value = dot(group.framed_zero[...], w_zero[:, begin * C : end * C])
        if gate is None:
            gate = 1.0 / (1.0 + jnp.exp(-value[:, 0:C]))
        for f in range(begin, end):
            group.hidden[f] = value[:, (f - begin) * C : (f - begin + 1) * C] * gate
    for number, (grouped, weights, size, plus, minus) in enumerate(
        ((group.framed_one, w_one, 6, 7, 13), (group.framed_two, w_two, 5, 19, 24))
    ):
        loads[1 + number].wait()
        for begin, end in chunks(size):
            value = dot(grouped[...], weights[:, begin * C : end * C])
            for f in range(begin, end):
                columns = slice((f - begin) * C, (f - begin + 1) * C)
                group.hidden[plus + f] = value[0 : group.edges, columns] * gate
                group.hidden[minus + f] = value[group.edges :, columns] * gate
    return gate


def back_through_gate(group, gate):
    total = group.upstream[0] * group.hidden[0]
    for f in range(1, FRAMED):
        total = total + group.upstream[f] * group.hidden[f]
    through = total * (0.25 * (1.0 - gate))
    scaled_gate = 0.25 * gate
    for f in range(FRAMED):
        block = group.upstream[f] * scaled_gate
        if f == 0:
            block = block + through
        put_grouped(group, f, block.astype(BF16), 1)


def convolve_back(group, radial, w_zero, w_one, w_two):
    def put_back(f, block):
        rows, at = of_place(packed_rows.index(f), group.edges, group.back_low, group.back_high)
        rows[at, :] = (block * radial).astype(BF16)

    for begin, end in chunks(7):
        value = dot(group.framed_zero[...], w_zero[:, begin * C : end * C])
        for f in range(begin, end):
            put_back(f, value[:, (f - begin) * C : (f - begin + 1) * C])
    for grouped, weights, size, plus, minus in (
        (group.framed_one, w_one, 6, 7, 13),
        (group.framed_two, w_two, 5, 19, 24),
    ):
        for begin, end in chunks(size):
            value = dot(grouped[...], weights[:, begin * C : end * C])
            for f in range(begin, end):
                columns = slice((f - begin) * C, (f - begin + 1) * C)
                put_back(plus + f, value[0 : group.edges, columns])
                put_back(minus + f, value[group.edges :, columns])


def gradient_columns(group):
    return (
        dot_rows(group.back_low[...], group.source_low[...]),
        dot_rows(group.back_high[...], group.source_high[...]),
    )


def radial_rows(codes, weight_high, weight_low):
    centre = lax.broadcasted_iota(jnp.int32, (1, RADIAL), 1).astype(F32) * 2.0
    distance = (codes - centre) * (22.0 / 1024.0)
    basis = jnp.exp(-0.5 * (distance * distance))
    basis_high = basis.astype(BF16)
    basis_low = (basis - basis_high.astype(F32)).astype(BF16)
    return dot(basis_high, weight_high) + (
        dot(basis_high, weight_low) + dot(basis_low, weight_high)
    )


def wide_masks(atoms):
    masks = [mask.astype(F32) for mask in atom_masks(atoms)]
    return [
        [
            jnp.concatenate([mask[b * CAP : (b + 1) * CAP]] * 2, axis=0).astype(BF16)
            for b in range(BUCKETS)
        ]
        for mask in masks
    ]


def put_pair(pair, rows, masks, low, high):
    for bucket in range(BUCKETS):
        slots = slice(bucket * CAP, (bucket + 1) * CAP)
        joined = jnp.concatenate([rows[0][slots], rows[1][slots]], axis=0).astype(BF16)
        for half in range(2):
            columns = slice(128 * half, 128 * half + 128)
            masked = joined * masks[half][bucket]
            if pair < LOW_PAIRS:
                low[bucket, 16 * pair : 16 * pair + 16, columns] = masked
            else:
                at = 16 * (pair - LOW_PAIRS)
                high[bucket, at : at + 16, columns] = masked


def kernel(domains_x, domains_y, names, *refs):
    refs = collections.namedtuple("Refs", names)(*refs)
    halo = Group(HALO, *(getattr(refs, "halo_" + name) for name in GROUP))
    inner = Group(INNER, *(getattr(refs, "inner_" + name) for name in GROUP))
    place_x = lax.axis_index("gx")
    place_y = lax.axis_index("gy")
    image = lax.axis_index("img")

    def inside(step_x, step_y):
        x = place_x + step_x
        y = place_y + step_y
        return (x >= 0) & (x < domains_x) & (y >= 0) & (y < domains_y)

    def device_at(step_x, step_y):
        return (place_x + step_x, place_y + step_y, image)

    barrier = pltpu.get_barrier_semaphore()
    for step_x, step_y in reversed(neighbour_steps):

        @pl.when(inside(step_x, step_y))
        def _(step_x=step_x, step_y=step_y):
            pl.semaphore_signal(
                barrier, inc=1, device_id=device_at(step_x, step_y), device_id_type=MESH
            )

    loads = {}
    for number, name in enumerate(LOADED):
        loads[name] = pltpu.make_async_copy(
            getattr(refs, name + "_hbm"), getattr(refs, name), refs.load_sems.at[number]
        )
        loads[name].start()

    class Once:
        def __init__(self, name):
            self.name = name

        def wait(self):
            if self.name in loads:
                loads.pop(self.name).wait()

    for bucket, (step_x, step_y) in enumerate(neighbour_steps):

        @pl.when(jnp.logical_not(inside(-step_x, -step_y)))
        def _(bucket=bucket):
            refs.codes_in[bucket] = jnp.full((CAP, 128), -1.0, F32)
            refs.hidden_in[bucket] = jnp.zeros((TRAVEL, C), BF16)

        @pl.when(jnp.logical_not(inside(step_x, step_y)))
        def _(bucket=bucket):
            refs.cotangent_in[bucket] = jnp.zeros((ATOMS * 49, C), BF16)

    def exchange(move, bucket, way):
        source, target, send, recv = move
        step_x, step_y = neighbour_steps[bucket]
        return pltpu.make_async_remote_copy(
            src_ref=source if source is refs.cotangent_hbm else source.at[bucket],
            dst_ref=target.at[bucket],
            send_sem=send.at[bucket],
            recv_sem=recv.at[bucket],
            device_id=device_at(way * step_x, way * step_y),
            device_id_type=MESH,
        )

    def each(move, way, buckets, act):
        for bucket in buckets:
            step_x, step_y = neighbour_steps[bucket]

            @pl.when(inside(way * step_x, way * step_y))
            def _(bucket=bucket):
                act(exchange(move, bucket, way))

    def start(move, way, buckets=BUCKET_ORDER):
        each(move, way, buckets, lambda copy: copy.start())

    def await_sent(move, way, buckets=BUCKET_ORDER):
        each(move, way, buckets, lambda copy: copy.wait_send())

    def await_arrivals(move, way, buckets=BUCKET_ORDER):
        each(move, -way, buckets, lambda copy: copy.wait_recv())

    codes_move = (refs.codes_out, refs.codes_in, refs.codes_send, refs.codes_recv)
    cotangent_move = (
        refs.cotangent_hbm,
        refs.cotangent_in,
        refs.cotangent_send,
        refs.cotangent_recv,
    )
    hidden_move = (refs.hidden_out, refs.hidden_in, refs.hidden_send, refs.hidden_recv)

    beside_x = jnp.where(place_x > 0, 2, 1) + jnp.where(place_x < domains_x - 1, 1, 0)
    beside_y = jnp.where(place_y > 0, 2, 1) + jnp.where(place_y < domains_y - 1, 1, 0)

    refs.codes_table[...] = jnp.zeros((128, 128), F32)
    for name in ("inner_edges", "halo_edges", "halo_counts"):
        Once(name).wait()
    counts = refs.halo_counts[...].astype(F32)
    for which in range(5):
        refs.codes_table[which * BUCKETS : (which + 1) * BUCKETS, 0:CAP] = refs.halo_edges[
            which
        ].astype(F32)
        refs.codes_table[40 + which : 41 + which, 0:INNER] = refs.inner_edges[which].astype(F32)
    turned_codes = refs.codes_table[...].T
    inner_codes = [column_of(turned_codes[0:INNER], 40 + which) for which in range(5)]
    lane = lax.broadcasted_iota(jnp.int32, (CAP, 128), 1)
    slot = lax.broadcasted_iota(jnp.int32, (CAP, 1), 0).astype(F32)
    slot_codes = [
        [column_of(turned_codes[0:CAP], which * BUCKETS + bucket) for bucket in range(BUCKETS)]
        for which in range(5)
    ]
    halo_targets = []
    for bucket in range(BUCKETS):
        target = jnp.where(slot < column_of(counts, bucket), slot_codes[1][bucket], -1.0)
        refs.codes_out[bucket] = jnp.where(
            lane == 0, target, jnp.where(lane == 1, slot_codes[2][bucket], slot_codes[3][bucket])
        )
        halo_targets.append(target)
    halo_codes = [jnp.concatenate(columns, axis=0) for columns in slot_codes]
    pl.semaphore_wait(barrier, beside_x * beside_y - 1)
    start(cotangent_move, -1, BUCKET_ORDER[0:4])
    start(codes_move, 1)
    start(cotangent_move, -1, BUCKET_ORDER[4:8])

    def spin_factors(terms):
        both = dot(terms, refs.second[...])
        return [
            (both[:, 256 * k : 256 * k + 128], both[:, 256 * k + 128 : 256 * k + 256])
            for k in range(2)
        ]

    def rotation_row(terms, factors, place):
        cosine, sine = factors[0 if place < LOW else 1]
        both = dot(terms, refs.first[:, place * 256 : place * 256 + 256])
        return cosine * both[:, 0:128] + sine * both[:, 128:256]

    def frame(group, codes, radial, put_row, put_rows):
        terms = angle_terms(codes[2], codes[3])
        factors = spin_factors(terms)
        terms = terms[:, 0:48]
        masks = atom_masks(codes[0])
        for pair in range(PAIRS):
            pair_rows = []
            for f in travel_rows[2 * pair : 2 * pair + 2]:
                if f is None:
                    pair_rows.append(jnp.zeros((group.edges, 128), F32))
                    continue
                place = packed_rows.index(f)
                wide = rotation_row(terms, factors, place)
                pair_rows.append(wide)
                row = wide.astype(BF16)
                put_row(place, row)
                masked = jnp.concatenate([row * masks[0], row * masks[1]], axis=1)
                rows, at = of_place(place, group.edges, group.source_low, group.source_high)
                rows[at, :] = masked
                turned = dot(masked, feature_low if place < LOW else feature_high)
                put_grouped(group, f, (turned * radial).astype(BF16), -1)
            put_rows(pair, pair_rows)

    for name in ("first", "second", "features", "spread", "radial"):
        Once(name).wait()
    feature_low, feature_high = coefficient_blocks([refs.features], refs.spread[...])
    weight = refs.radial[...]
    weight_high = weight.astype(BF16)
    weight_low = (weight - weight_high.astype(F32)).astype(BF16)
    halo_radial = radial_rows(halo_codes[4], weight_high, weight_low)
    target_masks = wide_masks(jnp.concatenate(halo_targets, axis=0))
    frame(
        halo,
        halo_codes,
        halo_radial,
        lambda place, row: None,
        lambda pair, rows: put_pair(pair, rows, target_masks, refs.target_low, refs.target_high),
    )
    weights = (refs.w_zero, refs.w_one, refs.w_two)
    weight_loads = [Once(name) for name in ("w_zero", "w_one", "w_two")]
    halo_gate = convolve(halo, *weights, weight_loads)
    for pair in range(PAIRS):
        f, g = travel_rows[2 * pair : 2 * pair + 2]
        for bucket in range(BUCKETS):
            slots = slice(bucket * CAP, (bucket + 1) * CAP)
            upper = halo.hidden[f, slots, :]
            lower = jnp.zeros((CAP, C), F32) if g is None else halo.hidden[g, slots, :]
            refs.hidden_out[bucket, 16 * pair : 16 * pair + 16, :] = jnp.concatenate(
                [upper, lower], axis=0
            ).astype(BF16)

    back_weights = (refs.back_zero, refs.back_one, refs.back_two)
    for matrix, turned, size in zip(weights, back_weights, (7 * C, 6 * C, 5 * C)):
        for begin in range(0, matrix.shape[0], size):
            turned[begin : begin + size, :] = matrix[begin : begin + size, :].T

    inner_radial = radial_rows(inner_codes[4], weight_high, weight_low)
    inner_masks = atom_masks(inner_codes[1])

    def put_inner(place, row):
        rows, at = of_place(place, INNER, refs.inner_target_low, refs.inner_target_high)
        rows[at, :] = jnp.concatenate([row * inner_masks[0], row * inner_masks[1]], axis=1)

    frame(inner, inner_codes, inner_radial, put_inner, lambda pair, rows: None)
    inner_gate = convolve(inner, *weights, weight_loads)
    Once("cotangent").wait()
    cot_low, cot_high = coefficient_blocks([refs.cotangent], refs.spread[...])
    for place, f in enumerate(packed_rows):
        rows, at = of_place(place, INNER, refs.inner_target_low, refs.inner_target_high)
        inner.upstream[f] = dot(rows[at, :], cot_low if place < LOW else cot_high)
        rows, at = of_place(place, INNER, refs.inner_hidden_low, refs.inner_hidden_high)
        rows[at, :] = inner.hidden[f].astype(BF16)
    back_through_gate(inner, inner_gate)
    convolve_back(inner, inner_radial, *back_weights)
    gradient_low, gradient_high = gradient_columns(inner)
    for bucket in BUCKET_ORDER:
        await_sent(cotangent_move, -1, (BUCKETS - 1 - bucket,))
        start(hidden_move, 1, (bucket,))
    low = dot_rows(refs.inner_hidden_low[...], refs.inner_target_low[...])
    high = dot_rows(refs.inner_hidden_high[...], refs.inner_target_high[...])


    for natural, target in (
        (refs.natural_low, refs.target_low),
        (refs.natural_high, refs.target_high),
    ):
        for bucket in range(BUCKETS):
            natural[bucket] = dot(target[bucket], refs.spread[...]).astype(BF16)

    Once("gather").wait()

    await_arrivals(codes_move, 1)
    arrived = refs.codes_in[...].reshape(HALO, 128)
    in_terms = angle_terms(column_of(arrived, 1), column_of(arrived, 2))
    in_factors = spin_factors(in_terms)
    in_terms = in_terms[:, 0:48]
    in_masks = wide_masks(column_of(arrived, 0))
    for pair in range(PAIRS):
        rows = [
            jnp.zeros((HALO, 128), F32)
            if f is None
            else rotation_row(in_terms, in_factors, packed_rows.index(f))
            for f in travel_rows[2 * pair : 2 * pair + 2]
        ]
        put_pair(pair, rows, in_masks, refs.incoming_low, refs.incoming_high)

    for bucket in range(BUCKETS):
        refs.turned_low[bucket] = dot_columns(refs.gather[...], refs.incoming_low[bucket]).astype(
            BF16
        )
        refs.turned_high[bucket] = dot_columns(
            refs.gather[...], refs.incoming_high[bucket]
        ).astype(BF16)
    low = place_rows(refs.gather[...], low)
    high = place_rows(refs.gather[...], high)

    for couple in range(0, BUCKETS, 2):
        buckets = BUCKET_ORDER[couple : couple + 2]
        await_arrivals(cotangent_move, -1, buckets)
        for bucket in buckets:
            slots = slice(bucket * CAP, (bucket + 1) * CAP)
            turned = (
                dot(refs.natural_low[bucket], refs.cotangent_in[bucket, LOW_PART, :]),
                dot(refs.natural_high[bucket], refs.cotangent_in[bucket, HIGH_PART, :]),
            )
            for pair in range(PAIRS):
                of_set = turned[0 if pair < LOW_PAIRS else 1]
                at = 16 * (pair if pair < LOW_PAIRS else pair - LOW_PAIRS)
                for half, f in enumerate(travel_rows[2 * pair : 2 * pair + 2]):
                    if f is not None:
                        halo.upstream[f, slots, :] = of_set[
                            at + CAP * half : at + CAP * (half + 1)
                        ]
    back_through_gate(halo, halo_gate)
    convolve_back(halo, halo_radial, *back_weights)
    halo_low, halo_high = gradient_columns(halo)
    refs.gradient[...] = join_sets(
        place_rows(refs.gather[...], gradient_low + halo_low),
        place_rows(refs.gather[...], gradient_high + halo_high),
    )
    gradient_store = pltpu.make_async_copy(
        refs.gradient, refs.result_hbm.at[1], refs.store_sems.at[1]
    )
    gradient_store.start()

    for begin, end in ((0, 4), (4, BUCKETS)):
        await_arrivals(hidden_move, 1, BUCKET_ORDER[begin:end])
        for bucket in BUCKET_ORDER[begin:end]:
            low = low + dot(refs.turned_low[bucket], refs.hidden_in[bucket, 0:LOW_TRAVEL, :])
            high = high + dot(
                refs.turned_high[bucket], refs.hidden_in[bucket, LOW_TRAVEL:TRAVEL, :]
            )
    refs.aggregate[...] = join_sets(0.25 * low, 0.25 * high)
    aggregate_store = pltpu.make_async_copy(
        refs.aggregate, refs.result_hbm.at[0], refs.store_sems.at[0]
    )
    aggregate_store.start()
    await_sent(codes_move, 1)
    await_sent(hidden_move, 1)
    gradient_store.wait()
    aggregate_store.wait()


LOADED = (
    "inner_edges",
    "halo_edges",
    "halo_counts",
    "first",
    "second",
    "features",
    "spread",
    "radial",
    "w_zero",
    "w_one",
    "w_two",
    "cotangent",
    "gather",
)
BUCKET_ORDER = (0, 2, 5, 7, 1, 6, 3, 4)


def on_device(
    domains_x,
    domains_y,
    features,
    cotangent,
    w_zero,
    w_one,
    w_two,
    radial_weight,
    inner_edges,
    halo_edges,
    halo_counts,
):
    first, second = rotation_tables()
    gather, spread = place_tables()
    arrays = dict(
        inner_edges=inner_edges.transpose(1, 0, 2),
        halo_edges=halo_edges.transpose(0, 2, 1, 3).reshape(5, BUCKETS, CAP),
        halo_counts=halo_counts,
        first=jnp.asarray(first),
        second=jnp.asarray(second),
        features=features.transpose(1, 0, 2).reshape(49 * ATOMS, C),
        spread=jnp.asarray(spread),
        radial=radial_weight,
        w_zero=w_zero,
        w_one=w_one.reshape(12 * C, 6 * C),
        w_two=w_two.reshape(10 * C, 5 * C),
        cotangent=cotangent.transpose(1, 0, 2).reshape(49 * ATOMS, C),
        gather=jnp.asarray(gather),
    )
    scratch = {name: (arrays[name].shape, arrays[name].dtype) for name in LOADED}
    high_travel = TRAVEL - LOW_TRAVEL
    scratch.update(
        back_zero=scratch["w_zero"],
        back_one=scratch["w_one"],
        back_two=scratch["w_two"],
        codes_table=((128, 128), F32),
        codes_out=((BUCKETS, CAP, 128), F32),
        codes_in=((BUCKETS, CAP, 128), F32),
        inner_target_low=((LOW * INNER, 256), BF16),
        inner_target_high=((HIGH * INNER, 256), BF16),
        inner_hidden_low=((LOW * INNER, C), BF16),
        inner_hidden_high=((HIGH * INNER, C), BF16),
        target_low=((BUCKETS, LOW_TRAVEL, 256), BF16),
        target_high=((BUCKETS, high_travel, 256), BF16),
        natural_low=((BUCKETS, LOW_TRAVEL, 25 * ATOMS), BF16),
        natural_high=((BUCKETS, high_travel, 25 * ATOMS), BF16),
        incoming_low=((BUCKETS, LOW_TRAVEL, 256), BF16),
        incoming_high=((BUCKETS, high_travel, 256), BF16),
        turned_low=((BUCKETS, 25 * ATOMS, LOW_TRAVEL), BF16),
        turned_high=((BUCKETS, 25 * ATOMS, high_travel), BF16),
        hidden_out=((BUCKETS, TRAVEL, C), BF16),
        hidden_in=((BUCKETS, TRAVEL, C), BF16),
        cotangent_in=((BUCKETS, 49 * ATOMS, C), BF16),
        aggregate=((49 * ATOMS, C), BF16),
        gradient=((49 * ATOMS, C), BF16),
    )
    for prefix, edges in (("halo_", HALO), ("inner_", INNER)):
        for name, shape in zip(GROUP, group_scratch(edges)):
            scratch[prefix + name] = shape
    semaphores = dict(load_sems=len(LOADED), store_sems=2)
    for move in ("codes", "cotangent", "hidden"):
        semaphores[move + "_send"] = BUCKETS
        semaphores[move + "_recv"] = BUCKETS
    names = [name + "_hbm" for name in LOADED] + ["result_hbm"] + list(scratch) + list(semaphores)
    result = pl.pallas_call(
        functools.partial(kernel, domains_x, domains_y, tuple(names)),
        out_shape=jax.ShapeDtypeStruct((2, 49 * ATOMS, C), BF16),
        in_specs=[pl.BlockSpec(memory_space=pltpu.HBM)] * len(LOADED),
        out_specs=pl.BlockSpec(memory_space=pltpu.HBM),
        scratch_shapes=[pltpu.VMEM(shape, dtype) for shape, dtype in scratch.values()]
        + [pltpu.SemaphoreType.DMA((count,)) for count in semaphores.values()],
        compiler_params=pltpu.CompilerParams(
            collective_id=0, has_side_effects=True, vmem_limit_bytes=60 * 1024 * 1024
        ),
        cost_estimate=pl.CostEstimate(
            flops=6 * 10**9, bytes_accessed=8 * 10**6, transcendentals=10**5
        ),
        name="message_layer",
    )(*[arrays[name] for name in LOADED])
    return tuple(rows.reshape(49, ATOMS, C).transpose(1, 0, 2) for rows in (result[0], result[1]))


def solution(mesh):
    return jax.shard_map(
        functools.partial(on_device, mesh.shape["gx"], mesh.shape["gy"]),
        mesh=mesh,
        in_specs=(
            P(("img", "gx", "gy"), None, None),
            P(("img", "gx", "gy"), None, None),
            P(),
            P(),
            P(),
            P(),
            P(("img", "gx", "gy"), None, None),
            P(("img", "gx", "gy"), None, None, None),
            P(("img", "gx", "gy"), None),
        ),
        out_specs=(P(("img", "gx", "gy"), None, None), P(("img", "gx", "gy"), None, None)),
        check_vma=False,
    )
```
